32 devices in a mesh: dp: 8 (over z, x), tensor: 4 (over y, core).
Axes of the slice: x: 2, y: 2, z: 4, core: 2. Of those that a mesh axis runs over, the one named last changes fastest.
Arguments:
- stream: float32 [8192, 768], P(('dp', 'tensor')), may hold values from -6 to 6
- cotangent: float32 [8192, 768], P(('dp', 'tensor')), may hold values from -6 to 6
- segments: int32 [8, 1024], P('dp'), may hold values from 0 to 3, never falling along the last dimension, each value on 1 to 800 neighbouring positions
- expert_pick: int32 [2, 8192, 2], P(None, 'dp'), may hold values from 0 to 3, as said below
- slot_index: int32 [2, 8192, 2], P(None, 'dp'), may hold values from -1 to 639, as said below
- norm_gains: float32 [2, 2, 768], replicated, may hold values from 0.5 to 1.5
- attention: bfloat16 [2, 3, 768, 768], P(None, None, 'dp', 'tensor'), may hold values from -0.21875 to 0.21875
- projection: bfloat16 [2, 768, 768], P(None, 'tensor', 'dp'), may hold values from -0.875 to 0.875
- router: bfloat16 [2, 768, 4], replicated, may hold values from -0.14941406 to 0.14941406
- widening: bfloat16 [2, 2, 768, 2048], P(None, None, 'dp', 'tensor'), may hold values from -0.21875 to 0.21875
- narrowing: bfloat16 [2, 2048, 768], P(None, 'tensor', 'dp'), may hold values from -0.125 to 0.125
- expansion: bfloat16 [2, 4, 2, 768, 2048], P(None, None, None, 'dp', 'tensor'), may hold values from -0.21875 to 0.21875
- contraction: bfloat16 [2, 4, 2048, 768], P(None, None, 'tensor', 'dp'), may hold values from -0.125 to 0.125
Outputs:
- stream_out: float32 [8192, 768], P(('dp', 'tensor'))
- stream_grad: float32 [8192, 768], P(('dp', 'tensor'))
- gains_grad: float32 [2, 2, 768], replicated
- attention_grad: float32 [2, 3, 768, 768], P(None, None, 'dp', 'tensor')
- projection_grad: float32 [2, 768, 768], P(None, 'tensor', 'dp')
- router_grad: float32 [2, 768, 4], replicated
- widening_grad: float32 [2, 2, 768, 2048], P(None, None, 'dp', 'tensor')
- narrowing_grad: float32 [2, 2048, 768], P(None, 'tensor', 'dp')
- expansion_grad: float32 [2, 4, 2, 768, 2048], P(None, None, None, 'dp', 'tensor')
- contraction_grad: float32 [2, 4, 2048, 768], P(None, None, 'tensor', 'dp')
The draws below stay inside these ranges and needn't reach their ends.
Inputs may be any that keep to these rules, and one draw needn't show every extreme that they name: `segments`: numbers never fall along a sequence; a document ends where its number changes. `expert_pick`: the two experts of a token are different. `slot_index`: within one sequence and one layer the pairs of one expert take distinct slots below 640, given in order of token and then of choice; a pair is dropped only when its expert's 640 slots are taken; in every sequence and layer some expert fills all 640 slots.
All inputs are finite; a program needn't handle non-finite values.
Results may differ from the reference program's by a relative error of at most 0.04.
Values may be sent and summed in bfloat16 or wider, within the bound.
A program may use at most 256 MiB of HBM per device.

```python
import math
import jax
import jax.numpy as jnp
import numpy as np
from jax import lax

D = 768
HEADS = 12
HEAD = 64
FE = 2048
FS = 2048
EXPERTS = 4
TOPK = 2
LAYERS = 2
SEQ = 1024
GROUPS = 8
TOKENS = 8192
CAP = 640


def routing(key):
    rows_all = LAYERS * GROUPS
    first_key, second_key, third_key, fourth_key, fifth_key = jax.random.split(key, 5)
    favoured = jax.random.randint(first_key, (rows_all, 1), 0, EXPERTS)

    def ranking_of(subkey):
        return jax.random.permutation(subkey, SEQ)
    ranking = jax.vmap(ranking_of)(jax.random.split(second_key, rows_all))
    with_favoured = ranking < 13 * SEQ // 16
    other_one = (favoured + jax.random.randint(third_key, (rows_all, SEQ), 1, EXPERTS)) % EXPERTS
    partner = (other_one + jax.random.randint(fourth_key, (rows_all, SEQ), 1, EXPERTS)) % EXPERTS
    leading = jnp.where(with_favoured, favoured, other_one)
    trailing = jnp.where(with_favoured, other_one, partner)
    swapped = jax.random.randint(fifth_key, (rows_all, SEQ), 0, 2) == 1
    column_first = jnp.where(swapped, trailing, leading)
    column_second = jnp.where(swapped, leading, trailing)
    expert_pairs = jnp.stack([column_first, column_second], axis=-1).astype(jnp.int32)
    flat_pairs = expert_pairs.reshape(rows_all, TOPK * SEQ)
    onehot = (flat_pairs[..., None] == jnp.arange(EXPERTS, dtype=jnp.int32)).astype(jnp.int32)
    running = jnp.cumsum(onehot, axis=1) - 1
    position = jnp.sum(onehot * running, axis=-1)
    slot_table = jnp.where(position < CAP, position, -1)
    out_shape = (LAYERS, GROUPS * SEQ, TOPK)
    return (expert_pairs.reshape(out_shape).astype(jnp.int32), slot_table.reshape(out_shape).astype(jnp.int32))


def draw_expert_pick(key, part):
    return routing(key)[0]


def draw_slot_index(key, part):
    return routing(key)[1]


def shard_levels(own_key, shape, shards, smallest, high):
    loudness = 1.0
    for dim, parts in shards:
        heights = jax.random.uniform(jax.random.fold_in(jax.random.fold_in(own_key, 6), dim), (parts,), jnp.float32, smallest / len(shards), high / len(shards))
        loudness = loudness * jnp.repeat(jnp.exp(heights), shape[dim] // parts).reshape((-1,) + (1,) * (len(shape) - 1 - dim))
    return loudness


def profile(count, total, most, skew):
    portions = [(1 << 20) // math.isqrt(grade ** skew) + 1 for grade in range(2, count + 1)]
    surplus, counts = total - most - (count - 1), [1] * (count - 1)
    while surplus > 0:
        movable = [i for i in range(count - 1) if counts[i] < most]
        pool, budget = sum([portions[i] for i in movable]), surplus
        for i in movable:
            addition = min(most - counts[i], max(1, budget * portions[i] // pool), surplus)
            counts[i] = counts[i] + addition
            surplus = surplus - addition
    return np.array([most] + counts)


def ragged(key, amount, total, reach, slope):
    if amount == 2:
        one = jax.random.randint(key, (), max(1, total - reach), min(reach, total - 1) + 1)
        return jnp.stack([one, total - one])
    sizes = jnp.asarray(profile(amount, total, reach, slope), jnp.int32)
    couples = (amount - 1) // 2
    giver, sink = sizes[1:1 + 2 * couples:2], sizes[2:2 + 2 * couples:2]
    margin = jnp.minimum(giver - 1, reach - sink)
    moved = jax.random.randint(jax.random.fold_in(key, 1), (couples,), 0, 1 << 20) % (margin + 1)
    sizes = sizes.at[1:1 + 2 * couples:2].set(giver - moved).at[2:2 + 2 * couples:2].set(sink + moved)
    return sizes[jax.random.permutation(jax.random.fold_in(key, 2), amount)]


def scatter_about(own_key, dims, deviation, most, cuts=(), kind=jnp.bfloat16):
    values = jax.random.normal(own_key, dims, jnp.float32) * deviation
    if len(cuts) > 0:
        values = shard_levels(own_key, dims, cuts, -0.22, 0.18) * values
    return jnp.clip(values, min=-most, max=most).astype(kind)


def setup_inputs(seed: int = 0) -> dict:
    key_of = jax.random.split(jax.random.key(seed), 14)
    stream = scatter_about(key_of[0], (TOKENS, D), 1.0, 6.0, ((0, 32),), jnp.float32)
    cotangent = scatter_about(key_of[1], (TOKENS, D), 1.0, 6.0, ((0, 32),), jnp.float32)
    segments = jax.vmap(lambda own: jnp.searchsorted(jnp.cumsum(ragged(own, 4, SEQ, 25 * SEQ // 32, 0)), jnp.arange(SEQ), side="right"))(jax.random.split(key_of[2], GROUPS)).reshape((GROUPS, SEQ)).astype(jnp.int32)
    expert_pick = draw_expert_pick(jax.random.fold_in(key_of[13], 71), 0)
    slot_index = draw_slot_index(jax.random.fold_in(key_of[13], 71), 0)
    norm_gains = jnp.clip(1.0 + 0.1 * jax.random.normal(key_of[5], (LAYERS, 2, D), jnp.float32), 0.5, 1.5)
    attention = scatter_about(key_of[6], (LAYERS, 3, D, D), D ** -0.5, 0.21875, ((2, 8), (3, 4)))
    projection = scatter_about(key_of[7], (LAYERS, D, D), (D // 16) ** -0.5, 0.875, ((1, 4), (2, 8)))
    router = scatter_about(key_of[8], (LAYERS, D, EXPERTS), 0.025, 0.14941406)
    widening = scatter_about(key_of[9], (LAYERS, 2, D, FS), D ** -0.5, 0.21875, ((2, 8), (3, 4)))
    narrowing = scatter_about(key_of[10], (LAYERS, FS, D), FS ** -0.5, 0.125, ((1, 4), (2, 8)))
    expansion = scatter_about(key_of[11], (LAYERS, EXPERTS, 2, D, FE), D ** -0.5, 0.21875, ((3, 8), (4, 4)))
    contraction = scatter_about(key_of[12], (LAYERS, EXPERTS, FE, D), FE ** -0.5, 0.125, ((2, 4), (3, 8)))
    return {"stream": stream, "cotangent": cotangent, "segments": segments, "expert_pick": expert_pick, "slot_index": slot_index, "norm_gains": norm_gains, "attention": attention, "projection": projection, "router": router, "widening": widening, "narrowing": narrowing, "expansion": expansion, "contraction": contraction}


@jax.custom_vjp
def low(v):
    return lax.optimization_barrier(v.astype(jnp.bfloat16)).astype(jnp.float32)

@jax.custom_vjp
def low_back(v):
    return v

def low_keep(v):
    return (low(v), None)

def low_pass(kept, grad):
    return (grad,)

def back_keep(v):
    return (v, None)

def back_low(kept, grad):
    return (low(grad),)
low.defvjp(low_keep, low_pass)
low_back.defvjp(back_keep, back_low)

def norm_rows(values, gain_row):
    factor = lax.rsqrt(lax.optimization_barrier(jnp.mean(values * values, axis=-1, keepdims=True)) + 1e-06)
    return values * factor * gain_row

def angle_tables(length, head_size):
    halfway = head_size // 2
    inverse = jnp.exp(jnp.arange(halfway, dtype=jnp.float32) * (-2.0 * math.log(10000.0) / head_size))
    phases = jnp.arange(length, dtype=jnp.float32)[:, None] * inverse[None, :]
    return (jnp.cos(phases), jnp.sin(phases))

def rotate_pairs(values, cosine_table, sine_table):
    halfway = values.shape[-1] // 2
    former = values[..., :halfway]
    latter = values[..., halfway:]
    cosine_part = cosine_table[:, None, :]
    sine_part = sine_table[:, None, :]
    return jnp.concatenate([former * cosine_part - latter * sine_part, latter * cosine_part + former * sine_part], axis=-1)

def layer_forward(stream, segment, expert_of, slot_of, gain_pair, attention, projection, router, widening, narrowing, expansion, contraction, cosine_table, sine_table):
    finest = lax.Precision.HIGHEST
    length = stream.shape[0]
    normed = low(norm_rows(stream, gain_pair[0]))
    projected = jnp.einsum('td,cdf->ctf', normed, attention, precision=finest)
    queries = low(rotate_pairs(low_back(projected[0]).reshape(length, HEADS, HEAD), cosine_table, sine_table))
    keys_all = low(rotate_pairs(low_back(projected[1]).reshape(length, HEADS, HEAD), cosine_table, sine_table))
    values = low(low_back(projected[2])).reshape(length, HEADS, HEAD)
    block_rows = min(512, length)
    block_count = length // block_rows
    query_blocks = queries.reshape(block_count, block_rows, HEADS, HEAD)
    offsets = jnp.arange(block_count, dtype=jnp.int32) * block_rows

    def attend(inputs):
        query_block, offset = inputs
        row_index = (offset + jnp.arange(block_rows, dtype=jnp.int32)).astype(jnp.int32)
        column_index = jnp.arange(length, dtype=jnp.int32)
        row_segment = jnp.take(segment, row_index)
        allowed = (column_index[None, :] <= row_index[:, None]) & (segment[None, :] == row_segment[:, None])
        raw = jnp.einsum('qhd,khd->hqk', query_block, keys_all, precision=finest)
        scores = low_back(raw * (1.0 / math.sqrt(HEAD)))
        masked = jnp.where(allowed[None], scores, -1e+30)
        highest = lax.optimization_barrier(jnp.max(masked, axis=-1, keepdims=True))
        exponent = jnp.exp(masked - highest)
        probability = exponent / lax.optimization_barrier(jnp.sum(exponent, axis=-1, keepdims=True))
        return jnp.einsum('hqk,khd->qhd', low(probability), values, precision=finest)
    attended_blocks = lax.map(jax.checkpoint(attend), (query_blocks, offsets))
    attended = low(low_back(attended_blocks.reshape(length, HEADS * HEAD)))
    mid = stream + low_back(jnp.dot(attended, projection, precision=finest))
    moe_in = low(norm_rows(mid, gain_pair[1]))
    logits = jnp.dot(moe_in, router, precision=finest)
    chosen = (expert_of[..., None] == jnp.arange(EXPERTS, dtype=jnp.int32)).astype(jnp.float32)
    pair_logits = lax.optimization_barrier(jnp.sum(chosen * logits[:, None, :], axis=-1))
    top_logit = lax.optimization_barrier(jnp.max(pair_logits, axis=-1, keepdims=True))
    pair_exp = jnp.exp(pair_logits - top_logit)
    gate_values = pair_exp / lax.optimization_barrier(jnp.sum(pair_exp, axis=-1, keepdims=True))
    flat_slot = jnp.where(slot_of >= 0, expert_of * CAP + slot_of, EXPERTS * CAP).astype(jnp.int32)
    dispatch = (flat_slot.reshape(-1)[None, :] == jnp.arange(EXPERTS * CAP, dtype=jnp.int32)[:, None]).astype(jnp.float32)
    repeated = jnp.repeat(moe_in, TOPK, axis=0)
    routed = jnp.dot(dispatch, repeated, precision=finest).reshape(EXPERTS, CAP, -1)
    inner_act = low_back(jnp.einsum('ecd,ekdf->ekcf', routed, expansion, precision=finest))
    hidden = low(jax.nn.silu(inner_act[:, 0]) * inner_act[:, 1])
    expert_out = low_back(jnp.einsum('ecf,efd->ecd', hidden, contraction, precision=finest)).reshape(EXPERTS * CAP, -1)
    padded = jnp.concatenate([expert_out, jnp.zeros((1, expert_out.shape[1]), jnp.float32)], axis=0)
    gathered = padded[flat_slot]
    shared_act = low_back(jnp.einsum('td,kdf->ktf', moe_in, widening, precision=finest))
    shared_hidden = low(jax.nn.silu(shared_act[0]) * shared_act[1])
    shared_out = jnp.dot(shared_hidden, narrowing, precision=finest)
    branch = low_back(shared_out + lax.optimization_barrier(jnp.sum(gate_values[..., None] * gathered, axis=1)))
    return mid + branch

def reference(stream, cotangent, segments, expert_pick, slot_index, norm_gains, attention, projection, router, widening, narrowing, expansion, contraction):
    weights = (norm_gains.astype(jnp.float32), attention.astype(jnp.float32), projection.astype(jnp.float32), router.astype(jnp.float32), widening.astype(jnp.float32), narrowing.astype(jnp.float32), expansion.astype(jnp.float32), contraction.astype(jnp.float32))
    cosine_table, sine_table = angle_tables(SEQ, HEAD)
    groups = stream.shape[0] // SEQ
    width_all = stream.shape[1]
    stream_groups = stream.reshape(groups, SEQ, width_all)
    cotangent_groups = cotangent.reshape(groups, SEQ, width_all)
    pick_groups = jnp.transpose(expert_pick.reshape(LAYERS, groups, SEQ, TOPK), (1, 0, 2, 3))
    slot_groups = jnp.transpose(slot_index.reshape(LAYERS, groups, SEQ, TOPK), (1, 0, 2, 3))

    def forward(values, params, segment, expert_of, slot_of):
        for layer_index in range(LAYERS):
            values = layer_forward(values, segment, expert_of[layer_index], slot_of[layer_index], params[0][layer_index], params[1][layer_index], params[2][layer_index], params[3][layer_index], params[4][layer_index], params[5][layer_index], params[6][layer_index], params[7][layer_index], cosine_table, sine_table)
        return values

    def per_group(totals, inputs):
        values, upstream, segment, expert_of, slot_of = inputs

        def closed(first, second):
            return forward(first, second, segment, expert_of, slot_of)
        result, pullback = jax.vjp(closed, values, weights)
        values_grad, params_grad = pullback(upstream)
        totals = jax.tree.map(jnp.add, totals, params_grad)
        return (totals, (result, values_grad))
    starting = jax.tree.map(jnp.zeros_like, weights)
    totals, (results, grads) = lax.scan(per_group, starting, (stream_groups, cotangent_groups, segments, pick_groups, slot_groups))
    return (results.reshape(stream.shape), grads.reshape(stream.shape), totals[0], totals[1], totals[2], totals[3], totals[4], totals[5], totals[6], totals[7])
```

```python
import math

import jax
import jax.numpy as jnp
from jax import lax
from jax.experimental import pallas as pl
from jax.experimental.pallas import tpu as pltpu
from jax.sharding import PartitionSpec as P

HEAD = 64
CAP = 640
LANES = 128
BF16 = jnp.bfloat16
F32 = jnp.float32
VMEM_LIMIT = 60 * 1024 * 1024


def nn(left, right):
    return lax.dot_general(left, right, (((1,), (0,)), ((), ())), preferred_element_type=F32)


def nt(left, right):
    return lax.dot_general(left, right, (((1,), (1,)), ((), ())), preferred_element_type=F32)


def tn(left, right):
    return lax.dot_general(left, right, (((0,), (0,)), ((), ())), preferred_element_type=F32)


class Place:
    def __init__(self):
        self.dp = lax.axis_index("dp")
        self.me = lax.axis_index("tensor")
        core = lax.rem(self.me, 2)
        self.core_peer = self.me + 1 - 2 * core
        self.y_peer = lax.rem(self.me + 2, 4)
        self.far_peer = lax.rem(self.core_peer + 2, 4)

    def tensor_id(self, member):
        return (self.dp, member)

    def greet(self):
        barrier = pltpu.get_barrier_semaphore()
        for member in (self.core_peer, self.y_peer):
            pl.semaphore_signal(
                barrier, inc=1, device_id=self.tensor_id(member), device_id_type=pl.DeviceIdType.MESH
            )
        pl.semaphore_wait(barrier, 2)


def send(source, target, send_sem, recv_sem, device):
    return pltpu.make_async_remote_copy(
        src_ref=source,
        dst_ref=target,
        send_sem=send_sem,
        recv_sem=recv_sem,
        device_id=device,
        device_id_type=pl.DeviceIdType.MESH,
    )


class TokenGather:
    def __init__(self, place, buf, send_sem, recv_sem):
        self.place, self.buf, self.sems = place, buf, (send_sem, recv_sem)
        self.quarter = buf.shape[0] // 4

    def rows(self, member):
        return pl.ds(pl.multiple_of(member * self.quarter, self.quarter), self.quarter)

    def pass_on(self, owner, target, slot):
        block = self.buf.at[self.rows(owner)]
        copy = send(
            block, block, self.sems[0].at[slot], self.sems[1].at[slot], self.place.tensor_id(target)
        )
        copy.start()
        return copy

    def start(self):
        place = self.place
        self.far = self.pass_on(place.me, place.y_peer, 1)
        self.near = self.pass_on(place.me, place.core_peer, 0)

    def arrivals(self):
        place = self.place
        yield place.me
        self.near.wait_recv()
        yield place.core_peer
        self.far.wait_recv()
        self.onward = self.pass_on(place.y_peer, place.core_peer, 2)
        yield place.y_peer
        self.onward.wait_recv()
        yield place.far_peer

    def close(self):
        self.near.wait_send()
        self.far.wait_send()
        self.onward.wait_send()


class TokenScatter:
    def __init__(self, place, part, landing, summed, crossed, send_sem, recv_sem):
        self.place, self.part = place, part
        self.landing, self.summed, self.crossed = landing, summed, crossed
        self.sems = (send_sem, recv_sem)
        self.quarter = part.shape[0] // 4

    def rows(self, member):
        return pl.ds(pl.multiple_of(member * self.quarter, self.quarter), self.quarter)

    def push(self, source, target, slot, member):
        copy = send(
            source, target, self.sems[0].at[slot], self.sems[1].at[slot], self.place.tensor_id(member)
        )
        copy.start()
        return copy

    def run(self, block_of):
        place, part = self.place, self.part
        part[self.rows(place.far_peer), :] = block_of(place.far_peer).astype(BF16)
        first = self.push(part.at[self.rows(place.far_peer)], self.landing.at[0], 0, place.core_peer)
        crossing = block_of(place.y_peer)
        first.wait_recv()
        self.summed[...] = (crossing + self.landing[0].astype(F32)).astype(BF16)
        across = self.push(self.summed, self.crossed, 1, place.y_peer)
        part[self.rows(place.core_peer), :] = block_of(place.core_peer).astype(BF16)
        second = self.push(part.at[self.rows(place.core_peer)], self.landing.at[1], 2, place.core_peer)
        own = block_of(place.me)
        second.wait_recv()
        own = own + self.landing[1].astype(F32)
        across.wait_recv()
        own = own + self.crossed[...].astype(F32)
        first.wait_send()
        second.wait_send()
        across.wait_send()
        return own


def scatter_scratch(length, width):
    quarter = length // 4
    return [
        pltpu.VMEM((length, width), BF16),
        pltpu.VMEM((2, quarter, width), BF16),
        pltpu.VMEM((quarter, width), BF16),
        pltpu.VMEM((quarter, width), BF16),
        pltpu.SemaphoreType.DMA((3,)),
        pltpu.SemaphoreType.DMA((3,)),
    ]


def gather_scratch(length, width):
    return [
        pltpu.VMEM((length, width), BF16),
        pltpu.SemaphoreType.DMA((3,)),
        pltpu.SemaphoreType.DMA((3,)),
    ]


class Local:
    def __init__(self, sems):
        self.sems, self.used, self.open = sems, 0, []

    def start(self, source, target, keep=False):
        copy = pltpu.make_async_copy(source, target, self.sems.at[self.used])
        self.used += 1
        copy.start()
        if keep:
            self.open.append(copy)
        return copy

    def close(self):
        for copy in self.open:
            copy.wait()


def normalise(values, gain):
    factor = lax.rsqrt(jnp.mean(values * values, axis=-1, keepdims=True) + 1e-06)
    return values * factor * gain


def normalise_back(values, gain, upstream):
    factor = lax.rsqrt(jnp.mean(values * values, axis=-1, keepdims=True) + 1e-06)
    scaled = upstream * gain
    inward = factor * scaled - values * factor * factor * factor * jnp.mean(
        scaled * values, axis=-1, keepdims=True
    )
    return inward, jnp.sum(upstream * values * factor, axis=0, keepdims=True)


def swap_halves(values):
    width = values.shape[1]
    lane = lax.broadcasted_iota(jnp.int32, values.shape, 1)
    return jnp.where(
        lax.rem(lane, HEAD) < HEAD // 2,
        pltpu.roll(values, width - HEAD // 2, 1),
        pltpu.roll(values, HEAD // 2, 1),
    )


def turn(values, cosine, sine):
    times = values.shape[1] // cosine.shape[1]
    return values * jnp.concatenate([cosine] * times, axis=1) + swap_halves(
        values
    ) * jnp.concatenate([sine] * times, axis=1)


def allowed_keys(seg_row, seg_col, offset, rows, extent):
    row_index = offset + lax.broadcasted_iota(jnp.int32, (rows, extent), 0)
    column_index = lax.broadcasted_iota(jnp.int32, (rows, extent), 1)
    return (column_index <= row_index) & (
        seg_row[:, :extent] == seg_col[offset : offset + rows, :]
    )


def softmax_rows(query, keys, allowed):
    masked = jnp.where(allowed, nt(query, keys), -1e30)
    exponent = jnp.exp(masked - jnp.max(masked, axis=-1, keepdims=True))
    return exponent * (1.0 / jnp.sum(exponent, axis=-1, keepdims=True))


def sigmoid(values):
    return 1.0 / (1.0 + jnp.exp(-values))


def attention_forward(
    x_ref, gain_ref, w_hbm, cos_ref, sin_ref, segr_ref, segc_ref,
    mid_ref, nrm_hbm, qk_hbm, v_hbm, att_hbm,
    w, qk, v, att, nrm, gsend, grecv, part, landing, summed, crossed, ssend, srecv, lsem,
):
    place, local = Place(), Local(lsem)
    load = local.start(w_hbm, w)
    place.greet()
    length = nrm.shape[0]
    heads = v.shape[1] // HEAD
    wide = heads * HEAD
    gather = TokenGather(place, nrm, gsend, grecv)
    nrm[gather.rows(place.me), :] = normalise(x_ref[...], gain_ref[...]).astype(BF16)
    gather.start()
    load.wait()
    for owner in gather.arrivals():
        rows = gather.rows(owner)
        projected = nn(nrm[rows, :], w[:, : 3 * wide])
        qk[rows, :] = turn(projected[:, : 2 * wide], cos_ref[rows, :], sin_ref[rows, :]).astype(BF16)
        v[rows, :] = projected[:, 2 * wide :].astype(BF16)
    gather.close()
    local.start(nrm, nrm_hbm, True)
    local.start(qk, qk_hbm, True)
    local.start(v, v_hbm, True)
    block = 256
    for offset in range(0, length, block):
        extent = offset + block
        allowed = allowed_keys(segr_ref, segc_ref, offset, block, extent)
        for head in range(heads):
            query = qk[offset:extent, head * HEAD : (head + 1) * HEAD] * BF16(HEAD**-0.5)
            keys = qk[:extent, wide + head * HEAD : wide + (head + 1) * HEAD]
            values = v[:extent, head * HEAD : (head + 1) * HEAD]
            probability = softmax_rows(query, keys, allowed).astype(BF16)
            att[offset:extent, head * HEAD : (head + 1) * HEAD] = nn(probability, values).astype(BF16)
    local.start(att, att_hbm, True)
    scatter = TokenScatter(place, part, landing, summed, crossed, ssend, srecv)
    outward = w[:, 3 * wide :]
    mid_ref[...] = x_ref[...] + scatter.run(lambda owner: nt(att[scatter.rows(owner), :], outward))
    local.close()


def attention_backward(
    up_ref, x_ref, gain_ref, w_hbm, nrm_hbm, qk_hbm, v_hbm, att_hbm, cos_ref, sin_ref, segr_ref, segc_ref,
    grad_ref, gain_grad_ref, dw_hbm,
    w, dw, nrm, qk, v, att, datt, dqk, dv, dqkv,
    up, gsend, grecv, part, landing, summed, crossed, ssend, srecv, lsem,
):
    place, local = Place(), Local(lsem)
    loads = [local.start(a, b) for a, b in ((w_hbm, w), (att_hbm, att), (qk_hbm, qk), (v_hbm, v), (nrm_hbm, nrm))]
    place.greet()
    length = nrm.shape[0]
    heads = v.shape[1] // HEAD
    wide = heads * HEAD
    gather = TokenGather(place, up, gsend, grecv)
    up[gather.rows(place.me), :] = up_ref[...].astype(BF16)
    gather.start()
    loads[0].wait()
    outward = w[:, 3 * wide :]
    for owner in gather.arrivals():
        rows = gather.rows(owner)
        datt[rows, :] = nn(up[rows, :], outward).astype(BF16)
    gather.close()
    for load in loads[1:]:
        load.wait()
    dqk[...] = jnp.zeros_like(dqk)
    dv[...] = jnp.zeros_like(dv)
    block = 256
    for offset in range(0, length, block):
        extent = offset + block
        allowed = allowed_keys(segr_ref, segc_ref, offset, block, extent)
        for head in range(heads):
            own = slice(head * HEAD, (head + 1) * HEAD)
            key_columns = slice(wide + head * HEAD, wide + (head + 1) * HEAD)
            query = qk[offset:extent, own] * BF16(HEAD**-0.5)
            keys = qk[:extent, key_columns]
            values = v[:extent, own]
            outer = datt[offset:extent, own]
            probability = softmax_rows(query, keys, allowed)
            inner = nt(outer, values)
            score = probability * (inner - jnp.sum(probability * inner, axis=-1, keepdims=True))
            score = score.astype(BF16)
            dqk[offset:extent, own] = nn(score, keys) * HEAD**-0.5
            dqk[:extent, key_columns] += tn(score, query)
            dv[:extent, own] += tn(probability.astype(BF16), outer)
    for offset in range(0, length, block):
        rows = slice(offset, offset + block)
        dqkv[rows, : 2 * wide] = turn(dqk[rows, :], cos_ref[rows, :], -sin_ref[rows, :]).astype(BF16)
        dqkv[rows, 2 * wide :] = dv[rows, :].astype(BF16)
    scatter = TokenScatter(place, part, landing, summed, crossed, ssend, srecv)
    inward = w[:, : 3 * wide]
    total = scatter.run(lambda owner: nt(dqkv[scatter.rows(owner), :], inward))
    dw[:, : 3 * wide] = tn(nrm[...], dqkv[...]).astype(BF16)
    dw[:, 3 * wide :] = tn(up[...], att[...]).astype(BF16)
    local.start(dw, dw_hbm, True)
    inward, gain_part = normalise_back(x_ref[...], gain_ref[...], total)
    grad_ref[...] = up_ref[...] + inward
    gain_grad_ref[...] = gain_part
    local.close()


def pick_softmax(logits, chosen, axis):
    highest = jnp.max(jnp.where(chosen > 0, logits, -1e30), axis=axis, keepdims=True)
    exponent = chosen * jnp.exp(jnp.where(chosen > 0, logits - highest, 0.0))
    return exponent / jnp.sum(exponent, axis=axis, keepdims=True)


def slots_by_token(slot_row):
    shape = (CAP, slot_row.shape[1])
    return lax.broadcasted_iota(jnp.int32, shape, 0) == slot_row


def tokens_by_slot(slot_column):
    shape = (slot_column.shape[0], CAP)
    return lax.broadcasted_iota(jnp.int32, shape, 1) == slot_column


def ffn_forward(
    mid_ref, gain_ref, w_hbm, router_ref, router_t_ref, slotr_ref, slotc_ref, chosenr_ref, chosenc_ref,
    next_ref, gates_ref, moe_hbm, routed_hbm, act_hbm, shared_hbm,
    w, routed, act, shared, branch, gates,
    moe, gsend, grecv, part, landing, summed, crossed, ssend, srecv, lsem,
):
    place, local = Place(), Local(lsem)
    experts = routed.shape[0]
    units = w.shape[2] // 3
    loads = {e: local.start(w_hbm.at[e], w.at[e]) for e in (experts, *range(experts))}
    place.greet()
    gather = TokenGather(place, moe, gsend, grecv)
    moe[gather.rows(place.me), :] = normalise(mid_ref[...], gain_ref[...]).astype(BF16)
    gather.start()
    loads[experts].wait()
    for owner in gather.arrivals():
        rows = gather.rows(owner)
        inner = nn(moe[rows, :], w[experts, :, : 2 * units])
        shared[rows, :] = inner.astype(BF16)
        gate = inner[:, :units]
        hidden = (gate * sigmoid(gate) * inner[:, units:]).astype(BF16)
        branch[rows, :] = nt(hidden, w[experts, :, 2 * units :])
        logits = nn(moe[rows, :], router_ref[...])
        gates[rows, :] = pick_softmax(logits, chosenc_ref[rows, :], 1)
    gather.close()
    local.start(moe, moe_hbm, True)
    local.start(shared, shared_hbm, True)
    gates_ref[...] = pick_softmax(nt(router_t_ref[...], moe[...]), chosenr_ref[...], 0)
    scatter = TokenScatter(place, part, landing, summed, crossed, ssend, srecv)
    outs = None
    for e in range(experts):
        loads[e].wait()
        dispatch = slots_by_token(slotr_ref[e : e + 1, :]).astype(F32).astype(BF16)
        picked = nn(dispatch, moe[...]).astype(BF16)
        routed[e] = picked
        local.start(routed.at[e], routed_hbm.at[e], True)
        inner = nn(picked, w[e, :, : 2 * units])
        act[e] = inner.astype(BF16)
        local.start(act.at[e], act_hbm.at[e], True)
        gate = inner[:, :units]
        hidden = (gate * sigmoid(gate) * inner[:, units:]).astype(BF16)
        outs = nt(hidden, w[e, :, 2 * units :]).astype(BF16)
        if e < experts - 1:
            combine = tokens_by_slot(slotc_ref[:, e : e + 1]).astype(F32).astype(BF16)
            branch[...] += gates[:, e : e + 1] * nn(combine, outs)

    def block_of(owner):
        rows = scatter.rows(owner)
        combine = tokens_by_slot(slotc_ref[rows, experts - 1 : experts]).astype(F32).astype(BF16)
        return branch[rows, :] + gates[rows, experts - 1 : experts] * nn(combine, outs)

    next_ref[...] = mid_ref[...] + scatter.run(block_of)
    local.close()


def swiglu_back(down, inner):
    units = inner.shape[1] // 2
    gate, raised = inner[:, :units], inner[:, units:]
    squashed = sigmoid(gate)
    gate_grad = down * raised * squashed * (1.0 + gate * (1.0 - squashed))
    up_grad = down * gate * squashed
    return jnp.concatenate([gate_grad.astype(BF16), up_grad.astype(BF16)], axis=1)


def hidden_of(inner):
    units = inner.shape[1] // 2
    gate = inner[:, :units]
    return (gate * sigmoid(gate) * inner[:, units:]).astype(BF16)


def ffn_backward(
    up_ref, mid_ref, gain_ref, w_hbm, moe_hbm, routed_hbm, act_hbm, shared_hbm,
    gates_ref, slotr_ref, slotc_ref, chosenr_ref, router_t_ref,
    grad_ref, gain_grad_ref, router_grad_ref, dw_hbm,
    w, dw, moe, routed, act, shared, hidden_all, moe_grad, slot_sums, logit_grad,
    up, gsend, grecv, part, landing, summed, crossed, ssend, srecv, lsem,
):
    place, local = Place(), Local(lsem)
    experts = routed.shape[0]
    units = w.shape[2] // 3
    load_w = {experts: local.start(w_hbm.at[experts], w.at[experts])}
    load_shared = local.start(shared_hbm, shared)
    load_moe = local.start(moe_hbm, moe)
    load_act, load_routed = {}, {}
    for e in range(experts):
        load_w[e] = local.start(w_hbm.at[e], w.at[e])
        load_act[e] = local.start(act_hbm.at[e], act.at[e])
        load_routed[e] = local.start(routed_hbm.at[e], routed.at[e])
    place.greet()
    gather = TokenGather(place, up, gsend, grecv)
    up[gather.rows(place.me), :] = up_ref[...].astype(BF16)
    gather.start()
    load_w[experts].wait()
    load_shared.wait()
    for owner in gather.arrivals():
        rows = gather.rows(owner)
        inner = shared[rows, :].astype(F32)
        hidden_all[rows, :] = hidden_of(inner)
        down = nn(up[rows, :], w[experts, :, 2 * units :])
        inner_grad = swiglu_back(down, inner)
        shared[rows, :] = inner_grad
        moe_grad[rows, :] = nt(inner_grad, w[experts, :, : 2 * units])
    gather.close()
    load_moe.wait()
    dw[experts, :, : 2 * units] = tn(moe[...], shared[...]).astype(BF16)
    dw[experts, :, 2 * units :] = tn(up[...], hidden_all[...]).astype(BF16)
    local.start(dw.at[experts], dw_hbm.at[experts], True)
    slot_sums[...] = jnp.zeros_like(slot_sums)
    back = None
    for e in range(experts):
        load_w[e].wait()
        load_act[e].wait()
        load_routed[e].wait()
        held = slots_by_token(slotr_ref[e : e + 1, :])
        dispatch = held.astype(F32).astype(BF16)
        gate_slot = jnp.sum(jnp.where(held, gates_ref[e : e + 1, :], 0.0), axis=1, keepdims=True)
        arrived = nn(dispatch, up[...]).astype(BF16)
        slot_grad = (arrived.astype(F32) * gate_slot).astype(BF16)
        inner = act[e].astype(F32)
        hidden = hidden_of(inner)
        down = nn(arrived, w[e, :, 2 * units :])
        slot_dot = jnp.sum(hidden.astype(F32) * down, axis=1, keepdims=True)
        slot_sums[e : e + 1, :] = jnp.sum(jnp.where(held, slot_dot, 0.0), axis=0, keepdims=True)
        inner_grad = swiglu_back(down * gate_slot, inner)
        dw[e, :, : 2 * units] = tn(routed[e], inner_grad).astype(BF16)
        dw[e, :, 2 * units :] = tn(slot_grad, hidden).astype(BF16)
        local.start(dw.at[e], dw_hbm.at[e], True)
        back = nt(inner_grad, w[e, :, : 2 * units]).astype(BF16)
        if e < experts - 1:
            combine = tokens_by_slot(slotc_ref[:, e : e + 1]).astype(F32).astype(BF16)
            moe_grad[...] += nn(combine, back)
    gates = gates_ref[...]
    chosen = chosenr_ref[...]
    pair = jnp.sum(gates, axis=0, keepdims=True)
    product = 0.5 * (pair * pair - jnp.sum(gates * gates, axis=0, keepdims=True))
    sums = slot_sums[...]
    logit_grad[...] = (
        chosen * product * (2.0 * sums - jnp.sum(sums, axis=0, keepdims=True))
    ).astype(BF16)
    router_grad_ref[...] = nn(logit_grad[...], moe[...])
    scatter = TokenScatter(place, part, landing, summed, crossed, ssend, srecv)

    def block_of(owner):
        rows = scatter.rows(owner)
        combine = tokens_by_slot(slotc_ref[rows, experts - 1 : experts]).astype(F32).astype(BF16)
        return moe_grad[rows, :] + nn(combine, back) + tn(logit_grad[:, rows], router_t_ref[...])

    total = scatter.run(block_of)
    inward, gain_part = normalise_back(mid_ref[...], gain_ref[...], total)
    grad_ref[...] = up_ref[...] + inward
    gain_grad_ref[...] = gain_part
    local.close()


def call(body, collective_id, arguments, in_hbm, outs, scratch):
    hbm, vmem = pl.BlockSpec(memory_space=pl.ANY), pl.BlockSpec(memory_space=pltpu.VMEM)
    return pl.pallas_call(
        body,
        out_shape=[jax.ShapeDtypeStruct(shape, kind) for shape, kind, _ in outs],
        in_specs=[hbm if index in in_hbm else vmem for index in range(len(arguments))],
        out_specs=[hbm if far else vmem for _, _, far in outs],
        scratch_shapes=scratch,
        compiler_params=pltpu.CompilerParams(
            collective_id=collective_id, has_side_effects=True, vmem_limit_bytes=VMEM_LIMIT
        ),
    )(*arguments)


def on_device(
    stream, cotangent, segments, expert_pick, slot_index, norm_gains,
    attention, projection, router, widening, narrowing, expansion, contraction,
):
    layers = attention.shape[0]
    segment = segments[0]
    length = segment.shape[0]
    experts = expansion.shape[1]
    width = stream.shape[1]
    quarter = stream.shape[0]
    wide = attention.shape[3]
    units = widening.shape[3]
    rows = attention.shape[2]

    halfway = HEAD // 2
    inverse = jnp.exp(
        jnp.arange(halfway, dtype=F32) * (-2.0 * math.log(10000.0) / HEAD)
    )
    phases = jnp.arange(length, dtype=F32)[:, None] * inverse[None, :]
    cosine, sine = jnp.cos(phases), jnp.sin(phases)
    cosine = jnp.concatenate([cosine] * 4, axis=1)
    sine = jnp.concatenate([-sine, sine] * 2, axis=1)
    seg_row, seg_col = segment[None, :], segment[:, None]

    expert_ids = jnp.arange(experts, dtype=jnp.int32)
    picked = expert_pick[..., None] == expert_ids
    slots = jnp.sum(jnp.where(picked, slot_index[..., None] + 1, 0), axis=2) - 1
    chosen = jnp.any(picked, axis=2).astype(F32)
    slot_cols = slots
    slot_rows = jnp.swapaxes(slots, 1, 2)
    chosen_cols = jnp.pad(chosen, ((0, 0), (0, 0), (0, LANES - experts)))
    chosen_rows = jnp.pad(jnp.swapaxes(chosen, 1, 2), ((0, 0), (0, 8 - experts), (0, 0)))
    router_wide = jnp.pad(router, ((0, 0), (0, 0), (0, LANES - experts)))
    router_t = jnp.pad(jnp.swapaxes(router, 1, 2), ((0, 0), (0, 8 - experts), (0, 0)))

    att_shards = jnp.concatenate(
        [attention[:, 0], attention[:, 1], attention[:, 2], jnp.swapaxes(projection, 1, 2)], axis=-1
    )
    shared_shards = jnp.concatenate(
        [widening[:, 0], widening[:, 1], jnp.swapaxes(narrowing, 1, 2)], axis=-1
    )
    expert_shards = jnp.concatenate(
        [expansion[:, :, 0], expansion[:, :, 1], jnp.swapaxes(contraction, 2, 3)], axis=-1
    )
    ffn_shards = jnp.concatenate([expert_shards, shared_shards[:, None]], axis=1)

    att_full, ffn_full = [], []
    for layer in range(layers):
        att_full.append(lax.all_gather(att_shards[layer], "dp", axis=0, tiled=True))
        ffn_full.append(lax.all_gather(ffn_shards[layer], "dp", axis=1, tiled=True))

    token_gather, token_scatter = gather_scratch(length, width), scatter_scratch(length, width)
    dma = pltpu.SemaphoreType.DMA
    saved = []
    current = stream
    for layer in range(layers):
        mid, normed, qk, values, attended = call(
            attention_forward,
            0,
            (current, norm_gains[layer, 0][None], att_full[layer], cosine, sine, seg_row, seg_col),
            (2,),
            [
                ((quarter, width), F32, False),
                ((length, width), BF16, True),
                ((length, 2 * wide), BF16, True),
                ((length, wide), BF16, True),
                ((length, wide), BF16, True),
            ],
            [
                pltpu.VMEM((width, 4 * wide), BF16),
                pltpu.VMEM((length, 2 * wide), BF16),
                pltpu.VMEM((length, wide), BF16),
                pltpu.VMEM((length, wide), BF16),
                *token_gather,
                *token_scatter,
                dma((5,)),
            ],
        )
        following, gates, moe_in, routed, act, shared = call(
            ffn_forward,
            1,
            (
                mid, norm_gains[layer, 1][None], ffn_full[layer], router_wide[layer], router_t[layer],
                slot_rows[layer], slot_cols[layer], chosen_rows[layer], chosen_cols[layer],
            ),
            (2,),
            [
                ((quarter, width), F32, False),
                ((8, length), F32, False),
                ((length, width), BF16, True),
                ((experts, CAP, width), BF16, True),
                ((experts, CAP, 2 * units), BF16, True),
                ((length, 2 * units), BF16, True),
            ],
            [
                pltpu.VMEM((experts + 1, width, 3 * units), BF16),
                pltpu.VMEM((experts, CAP, width), BF16),
                pltpu.VMEM((experts, CAP, 2 * units), BF16),
                pltpu.VMEM((length, 2 * units), BF16),
                pltpu.VMEM((length, width), F32),
                pltpu.VMEM((length, LANES), F32),
                *token_gather,
                *token_scatter,
                dma((3 * experts + 3,)),
            ],
        )
        saved.append((current, normed, qk, values, attended, mid, gates, moe_in, routed, act, shared))
        current = following

    upstream = cotangent
    gain_parts, router_parts = [None] * layers, [None] * layers
    att_grads, ffn_grads = [None] * layers, [None] * layers
    for layer in reversed(range(layers)):
        x_in, normed, qk, values, attended, mid, gates, moe_in, routed, act, shared = saved[layer]
        mid_grad, gain_two, router_parts[layer], ffn_part = call(
            ffn_backward,
            2,
            (
                upstream, mid, norm_gains[layer, 1][None], ffn_full[layer], moe_in, routed, act, shared,
                gates, slot_rows[layer], slot_cols[layer], chosen_rows[layer], router_t[layer],
            ),
            (3, 4, 5, 6, 7),
            [
                ((quarter, width), F32, False),
                ((1, width), F32, False),
                ((8, width), F32, False),
                ((experts + 1, width, 3 * units), BF16, True),
            ],
            [
                pltpu.VMEM((experts + 1, width, 3 * units), BF16),
                pltpu.VMEM((experts + 1, width, 3 * units), BF16),
                pltpu.VMEM((length, width), BF16),
                pltpu.VMEM((experts, CAP, width), BF16),
                pltpu.VMEM((experts, CAP, 2 * units), BF16),
                pltpu.VMEM((length, 2 * units), BF16),
                pltpu.VMEM((length, units), BF16),
                pltpu.VMEM((length, width), F32),
                pltpu.VMEM((8, length), F32),
                pltpu.VMEM((8, length), BF16),
                *token_gather,
                *token_scatter,
                dma((4 * experts + 4,)),
            ],
        )
        ffn_grads[layer] = lax.psum_scatter(ffn_part, "dp", scatter_dimension=1, tiled=True)
        upstream, gain_one, att_part = call(
            attention_backward,
            3,
            (
                mid_grad, x_in, norm_gains[layer, 0][None], att_full[layer], normed, qk, values, attended,
                cosine, sine, seg_row, seg_col,
            ),
            (3, 4, 5, 6, 7),
            [
                ((quarter, width), F32, False),
                ((1, width), F32, False),
                ((width, 4 * wide), BF16, True),
            ],
            [
                pltpu.VMEM((width, 4 * wide), BF16),
                pltpu.VMEM((width, 4 * wide), BF16),
                pltpu.VMEM((length, width), BF16),
                pltpu.VMEM((length, 2 * wide), BF16),
                pltpu.VMEM((length, wide), BF16),
                pltpu.VMEM((length, wide), BF16),
                pltpu.VMEM((length, wide), BF16),
                pltpu.VMEM((length, 2 * wide), F32),
                pltpu.VMEM((length, wide), F32),
                pltpu.VMEM((length, 3 * wide), BF16),
                *token_gather,
                *token_scatter,
                dma((6,)),
            ],
        )
        att_grads[layer] = lax.psum_scatter(att_part, "dp", scatter_dimension=0, tiled=True)
        gain_parts[layer] = jnp.concatenate([gain_one, gain_two], axis=0)

    gains_grad, router_grad = lax.psum(
        (jnp.stack(gain_parts), jnp.stack(router_parts)), ("dp", "tensor")
    )
    att_grad = jnp.stack(att_grads).astype(F32)
    ffn_grad = jnp.stack(ffn_grads).astype(F32)
    attention_grad = jnp.stack([att_grad[:, :, k * wide : (k + 1) * wide] for k in range(3)], axis=1)
    projection_grad = jnp.swapaxes(att_grad[:, :, 3 * wide :], 1, 2)
    pair = jnp.stack([ffn_grad[..., :units], ffn_grad[..., units : 2 * units]], axis=2)
    third = jnp.swapaxes(ffn_grad[..., 2 * units :], 2, 3)
    return (
        current,
        upstream,
        gains_grad,
        attention_grad,
        projection_grad,
        jnp.swapaxes(router_grad[:, :experts], 1, 2),
        pair[:, experts],
        third[:, experts],
        pair[:, :experts],
        third[:, :experts],
    )


def solution(mesh):
    placed = (
        P(("dp", "tensor"), None),
        P(("dp", "tensor"), None),
        P("dp", None),
        P(None, "dp", None),
        P(None, "dp", None),
        P(),
        P(None, None, "dp", "tensor"),
        P(None, "tensor", "dp"),
        P(),
        P(None, None, "dp", "tensor"),
        P(None, "tensor", "dp"),
        P(None, None, None, "dp", "tensor"),
        P(None, None, "tensor", "dp"),
    )
    return jax.shard_map(
        on_device,
        mesh=mesh,
        in_specs=placed,
        out_specs=(
            P(("dp", "tensor"), None),
            P(("dp", "tensor"), None),
            P(),
            P(None, None, "dp", "tensor"),
            P(None, "tensor", "dp"),
            P(),
            P(None, None, "dp", "tensor"),
            P(None, "tensor", "dp"),
            P(None, None, None, "dp", "tensor"),
            P(None, None, "tensor", "dp"),
        ),
        check_vma=False,
    )
```

```python
import functools
import math
import types

import jax
import jax.numpy as jnp
from jax import lax
from jax.experimental import pallas as pl
from jax.experimental.pallas import tpu as pltpu
from jax.sharding import PartitionSpec as P

HEAD = 64
CAP = 640
LANES = 128
BF16 = jnp.bfloat16
F32 = jnp.float32
ATT, SH, EX = range(3)
NRM, QK, V, ATTENDED = range(4)
MOE, SHARED, ROUTED, ACT = range(4)
GET_Z, GET_X, SUM_X, SUM_Z = range(4)
VMEM_LIMIT = 60 * 1024 * 1024


def nn(left, right):
    return lax.dot_general(left, right, (((1,), (0,)), ((), ())), preferred_element_type=F32)


def nt(left, right):
    return lax.dot_general(left, right, (((1,), (1,)), ((), ())), preferred_element_type=F32)


def tn(left, right):
    return lax.dot_general(left, right, (((0,), (0,)), ((), ())), preferred_element_type=F32)


class Place:
    def __init__(self):
        self.dp = lax.axis_index("dp")
        self.me = lax.axis_index("tensor")
        core = lax.rem(self.me, 2)
        self.core_peer = self.me + 1 - 2 * core
        self.y_peer = lax.rem(self.me + 2, 4)
        self.far_peer = lax.rem(self.core_peer + 2, 4)
        self.z = lax.div(self.dp, 2)
        self.x = lax.rem(self.dp, 2)
        self.half = lax.rem(self.z, 2)

    def member(self, tensor):
        return (self.dp, tensor)

    def row(self, away, x):
        return lax.rem(self.z + away + 4, 4) * 2 + x

    def beyond(self, away):
        return (self.row(away, self.x), self.me)

    def beside(self):
        return (self.row(0, 1 - self.x), self.me)

    def partner(self):
        return ((self.z + 1 - 2 * self.half) * 2 + self.x, self.me)

    def greet(self, peers):
        barrier = pltpu.get_barrier_semaphore()
        for peer in peers:
            pl.semaphore_signal(barrier, inc=1, device_id=peer, device_id_type=pl.DeviceIdType.MESH)
        pl.semaphore_wait(barrier, len(peers))

    def greet_sequence(self):
        return [self.member(self.core_peer), self.member(self.y_peer)]

    def greet_all(self):
        return [self.beside(), self.beyond(1), self.beyond(2), self.beyond(3)]


def send(source, target, send_sem, recv_sem, device):
    copy = pltpu.make_async_remote_copy(
        src_ref=source,
        dst_ref=target,
        send_sem=send_sem,
        recv_sem=recv_sem,
        device_id=device,
        device_id_type=pl.DeviceIdType.MESH,
    )
    copy.start()
    return copy


class Local:
    def __init__(self, sems):
        self.sems, self.used, self.open = sems, 0, []

    def start(self, source, target, keep=False):
        copy = pltpu.make_async_copy(source, target, self.sems.at[self.used])
        self.used += 1
        copy.start()
        if keep:
            self.open.append(copy)
        return copy

    def close(self):
        for copy in self.open:
            copy.wait()


def quarter_rows(length, member):
    quarter = length // 4
    return pl.ds(pl.multiple_of(member * quarter, quarter), quarter)


class TokenGather:
    def __init__(self, place, buf, sems):
        self.place, self.buf = place, buf
        self.sems = (sems["send_sem"], sems["recv_sem"])

    def rows(self, member):
        return quarter_rows(self.buf.shape[0], member)

    def pass_on(self, owner, target, slot):
        block = self.buf.at[self.rows(owner)]
        return send(block, block, self.sems[0].at[slot], self.sems[1].at[slot], self.place.member(target))

    def start(self):
        place = self.place
        self.far = self.pass_on(place.me, place.y_peer, 1)
        self.near = self.pass_on(place.me, place.core_peer, 0)

    def arrivals(self):
        place = self.place
        yield place.me
        self.near.wait_recv()
        yield place.core_peer
        self.far.wait_recv()
        self.onward = self.pass_on(place.y_peer, place.core_peer, 2)
        yield place.y_peer
        self.onward.wait_recv()
        yield place.far_peer
        self.near.wait_send()
        self.far.wait_send()
        self.onward.wait_send()


class TokenScatter:
    def __init__(self, place, refs):
        self.place = place
        refs = types.SimpleNamespace(**refs)
        self.part, self.landing, self.summed, self.crossed = refs.part, refs.landing, refs.summed, refs.crossed
        self.sems = (refs.send_sem, refs.recv_sem)

    def push(self, source, target, slot, member):
        return send(source, target, self.sems[0].at[slot], self.sems[1].at[slot], self.place.member(member))

    def begin(self, block_of):
        place, part = self.place, self.part
        part[0] = block_of(place.far_peer).astype(BF16)
        self.first = self.push(part.at[0], self.landing.at[0], 0, place.core_peer)
        crossing = block_of(place.y_peer)
        self.first.wait_recv()
        self.summed[...] = (crossing + self.landing[0].astype(F32)).astype(BF16)
        self.across = self.push(self.summed, self.crossed, 1, place.y_peer)
        part[1] = block_of(place.core_peer).astype(BF16)
        self.second = self.push(part.at[1], self.landing.at[1], 2, place.core_peer)
        self.own = block_of(place.me)

    def total(self):
        self.second.wait_recv()
        own = self.own + self.landing[1].astype(F32)
        self.across.wait_recv()
        own = own + self.crossed[...].astype(F32)
        self.first.wait_send()
        self.second.wait_send()
        self.across.wait_send()
        return own


def scatter_scratch(length, width):
    quarter = length // 4
    return dict(
        part=pltpu.VMEM((2, quarter, width), BF16),
        landing=pltpu.VMEM((2, quarter, width), BF16),
        summed=pltpu.VMEM((quarter, width), BF16),
        crossed=pltpu.VMEM((quarter, width), BF16),
        send_sem=pltpu.SemaphoreType.DMA((3,)),
        recv_sem=pltpu.SemaphoreType.DMA((3,)),
    )


def gather_scratch():
    return dict(send_sem=pltpu.SemaphoreType.DMA((3,)), recv_sem=pltpu.SemaphoreType.DMA((3,)))


class Straight:
    def __init__(self, place, source, target, rows, sems):
        self.place, self.source, self.target, self.rows = place, source, target, rows
        self.send_sem, self.recv_sem, self.local_sem = sems

    def part_for(self, away):
        source = self.source
        if len(source.shape) == 3:
            source = source.at[lax.rem(self.place.z + away, 2)]
        return source.at[pl.ds(*self.rows)]

    def start(self):
        place, mine = self.place, self.target.at[self.place.z]
        self.own = pltpu.make_async_copy(self.part_for(0), mine, self.local_sem.at[0])
        self.own.start()
        self.copies = [
            send(self.part_for(away), mine, self.send_sem.at[away], self.recv_sem.at[away], place.beyond(away))
            for away in (2, 1, 3)
        ]

    def arrived(self):
        self.own.wait()
        for copy in self.copies:
            copy.wait_recv()

    def close(self):
        for copy in self.copies:
            copy.wait_send()


class Aside:
    def __init__(self, place, source, target, sems):
        self.place, self.source, self.target = place, source, target
        self.send_sem, self.recv_sem = sems

    def start(self):
        self.copy = send(
            self.source, self.target, self.send_sem.at[0], self.recv_sem.at[0], self.place.beside()
        )

    def arrived(self):
        self.copy.wait_recv()

    def close(self):
        self.copy.wait_send()


class AsideSum:
    def __init__(self, place, source, own, landing, summed, sems):
        self.place, self.source, self.own, self.landing, self.summed = place, source, own, landing, summed
        self.send_sem, self.recv_sem, self.local_sem = sems

    def start(self):
        place = self.place
        self.copy = send(
            self.source.at[:, 1 - place.x], self.landing, self.send_sem.at[0], self.recv_sem.at[0], place.beside()
        )
        if self.own is not None:
            self.load = pltpu.make_async_copy(self.source.at[:, place.x], self.own, self.local_sem.at[0])
            self.load.start()

    def arrived(self):
        self.copy.wait_recv()
        if self.own is not None:
            self.load.wait()
        for at in range(4):
            own = self.source[at, self.place.x] if self.own is None else self.own[at]
            self.summed[at] = (own.astype(F32) + self.landing[at].astype(F32)).astype(BF16)

    def close(self):
        self.copy.wait_send()


class StraightSum:
    def __init__(self, place, source, landing, totals, sems):
        self.place, self.source, self.landing, self.totals = place, source, landing, totals
        self.send_sem, self.recv_sem, self.local_sem = sems

    def start(self):
        place = self.place
        self.copies = [
            send(
                self.source.at[lax.rem(place.z + away, 4)],
                self.landing.at[away],
                self.send_sem.at[away],
                self.recv_sem.at[away],
                place.beyond(away),
            )
            for away in (2, 1, 3)
        ]
        self.own = pltpu.make_async_copy(self.source.at[place.z], self.landing.at[0], self.local_sem.at[0])
        self.own.start()

    def arrived(self):
        for copy in self.copies:
            copy.wait_recv()
        self.own.wait()
        blocks = [self.landing[away].astype(F32) for away in range(4)]
        if len(self.totals) == 1:
            self.totals[0][...] = (blocks[0] + blocks[2]) + (blocks[1] + blocks[3])
        else:
            self.totals[0][...] = blocks[0] + blocks[2]
            self.totals[1][...] = blocks[1] + blocks[3]

    def close(self):
        for copy in self.copies:
            copy.wait_send()


def normalise(values, gain):
    factor = lax.rsqrt(jnp.mean(values * values, axis=-1, keepdims=True) + 1e-06)
    return values * factor * gain


def normalise_back(values, gain, upstream):
    factor = lax.rsqrt(jnp.mean(values * values, axis=-1, keepdims=True) + 1e-06)
    scaled = upstream * gain
    inward = factor * scaled - values * factor * factor * factor * jnp.mean(
        scaled * values, axis=-1, keepdims=True
    )
    return inward, jnp.sum(upstream * values * factor, axis=0, keepdims=True)


def swap_halves(values):
    width = values.shape[1]
    lane = lax.broadcasted_iota(jnp.int32, values.shape, 1)
    return jnp.where(
        lax.rem(lane, HEAD) < HEAD // 2,
        pltpu.roll(values, width - HEAD // 2, 1),
        pltpu.roll(values, HEAD // 2, 1),
    )


def turn(values, cosine, sine):
    times = values.shape[1] // cosine.shape[1]
    return values * jnp.concatenate([cosine] * times, axis=1) + swap_halves(
        values
    ) * jnp.concatenate([sine] * times, axis=1)


def allowed_keys(seg_row, seg_col, offset, rows, extent):
    row_index = offset + lax.broadcasted_iota(jnp.int32, (rows, extent), 0)
    column_index = lax.broadcasted_iota(jnp.int32, (rows, extent), 1)
    return (column_index <= row_index) & (
        seg_row[:, :extent] == seg_col[offset : offset + rows, :]
    )


def softmax_rows(query, keys, allowed):
    masked = jnp.where(allowed, nt(query, keys), -1e30)
    exponent = jnp.exp(masked - jnp.max(masked, axis=-1, keepdims=True))
    return exponent * (1.0 / jnp.sum(exponent, axis=-1, keepdims=True))


def sigmoid(values):
    return 1.0 / (1.0 + jnp.exp(-values))


def attention_forward(k):
    length, wide = k.kept[V].shape
    heads = wide // HEAD
    place = k.place
    k.early(ATT)
    gather = TokenGather(place, k.kept[NRM], k.gather)
    k.kept[NRM][gather.rows(place.me), :] = normalise(k.x[...], k.gain[...]).astype(BF16)
    gather.start()
    k.at(1)
    k.weight(ATT)
    inward, outward = k.matrix(ATT, 0, 3 * wide), k.matrix(ATT, 3 * wide, 4 * wide)
    for owner in gather.arrivals():
        rows = gather.rows(owner)
        projected = nn(k.kept[NRM][rows, :], inward)
        k.kept[QK][rows, :] = turn(projected[:, : 2 * wide], k.cosine[rows, :], k.sine[rows, :]).astype(BF16)
        k.kept[V][rows, :] = projected[:, 2 * wide :].astype(BF16)
    for at in (NRM, QK, V):
        k.local.start(k.kept[at], k.kept_out[at], True)
    k.at(2)
    block = 256
    for offset in range(0, length, block):
        extent = offset + block
        allowed = allowed_keys(k.seg_row, k.seg_col, offset, block, extent)
        for head in range(heads):
            own = slice(head * HEAD, (head + 1) * HEAD)
            query = k.kept[QK][offset:extent, own] * BF16(HEAD**-0.5)
            keys = k.kept[QK][:extent, wide + head * HEAD : wide + (head + 1) * HEAD]
            probability = softmax_rows(query, keys, allowed).astype(BF16)
            k.kept[ATTENDED][offset:extent, own] = nn(probability, k.kept[V][:extent, own]).astype(BF16)
        k.at(3 + offset // block)
    k.local.start(k.kept[ATTENDED], k.kept_out[ATTENDED], True)
    scatter = TokenScatter(place, k.scatter)
    scatter.begin(lambda owner: nt(k.kept[ATTENDED][quarter_rows(length, owner), :], outward))
    k.mid[...] = k.x[...] + scatter.total()


def attention_backward(k):
    length, wide = k.kept[V].shape
    heads = wide // HEAD
    place = k.place
    k.early(ATT)
    loads = [k.local.start(k.kept_in[at], k.kept[at]) for at in (ATTENDED, QK, V, NRM)]
    gather = TokenGather(place, k.up, k.gather)
    k.up[gather.rows(place.me), :] = k.upstream[...].astype(BF16)
    gather.start()
    k.at(1)
    k.weight(ATT)
    inward, outward = k.matrix(ATT, 0, 3 * wide), k.matrix(ATT, 3 * wide, 4 * wide)
    for owner in gather.arrivals():
        rows = gather.rows(owner)
        k.outer[rows, :] = nn(k.up[rows, :], outward).astype(BF16)
    for load in loads:
        load.wait()
    k.dqk[...] = jnp.zeros_like(k.dqk)
    k.dv[...] = jnp.zeros_like(k.dv)
    block = 256
    for offset in range(0, length, block):
        k.at(2 + offset // block)
        extent = offset + block
        allowed = allowed_keys(k.seg_row, k.seg_col, offset, block, extent)
        for head in range(heads):
            own = slice(head * HEAD, (head + 1) * HEAD)
            key_columns = slice(wide + head * HEAD, wide + (head + 1) * HEAD)
            query = k.kept[QK][offset:extent, own] * BF16(HEAD**-0.5)
            keys = k.kept[QK][:extent, key_columns]
            outer = k.outer[offset:extent, own]
            probability = softmax_rows(query, keys, allowed)
            inner = nt(outer, k.kept[V][:extent, own])
            score = probability * (inner - jnp.sum(probability * inner, axis=-1, keepdims=True))
            score = score.astype(BF16)
            k.dqk[offset:extent, own] = nn(score, keys) * HEAD**-0.5
            k.dqk[:extent, key_columns] += tn(score, query)
            k.dv[:extent, own] += tn(probability.astype(BF16), outer)
    for offset in range(0, length, block):
        rows = slice(offset, offset + block)
        k.dqkv[rows, : 2 * wide] = turn(k.dqk[rows, :], k.cosine[rows, :], -k.sine[rows, :]).astype(BF16)
        k.dqkv[rows, 2 * wide :] = k.dv[rows, :].astype(BF16)
    scatter = TokenScatter(place, k.scatter)
    scatter.begin(lambda owner: nt(k.dqkv[quarter_rows(length, owner), :], inward))
    k.put(ATT, 0, tn(k.kept[NRM][...], k.dqkv[...]))
    k.put(ATT, 3 * wide, tn(k.up[...], k.kept[ATTENDED][...]))
    k.made(ATT)
    inward, k.gain_grad[...] = normalise_back(k.x[...], k.gain[...], scatter.total())
    k.grad[...] = k.upstream[...] + inward


def pick_softmax(logits, chosen, axis):
    highest = jnp.max(jnp.where(chosen > 0, logits, -1e30), axis=axis, keepdims=True)
    exponent = chosen * jnp.exp(jnp.where(chosen > 0, logits - highest, 0.0))
    return exponent / jnp.sum(exponent, axis=axis, keepdims=True)


def slots_by_token(slot_row):
    shape = (CAP, slot_row.shape[1])
    return lax.broadcasted_iota(jnp.int32, shape, 0) == slot_row


def tokens_by_slot(slot_column):
    shape = (slot_column.shape[0], CAP)
    return (lax.broadcasted_iota(jnp.int32, shape, 1) == slot_column).astype(F32).astype(BF16)


def hidden_of(inner):
    units = inner.shape[1] // 2
    gate = inner[:, :units]
    return (gate * sigmoid(gate) * inner[:, units:]).astype(BF16)


def swiglu_back(down, inner):
    units = inner.shape[1] // 2
    gate, raised = inner[:, :units], inner[:, units:]
    squashed = sigmoid(gate)
    gate_grad = down * raised * squashed * (1.0 + gate * (1.0 - squashed))
    up_grad = down * gate * squashed
    return jnp.concatenate([gate_grad.astype(BF16), up_grad.astype(BF16)], axis=1)


def expert_order(sequences, experts):
    if sequences == 1:
        return [(0, e) for e in range(experts)]
    return [(0, 0), (1, 0), (1, 1), (0, 1)]


def both_arrivals(k, buf, on_rows, between):
    place = k.place
    sequences = buf.shape[0]
    own = TokenGather(place, buf.at[0], k.gather)
    quarter = own.rows(place.me)
    own.start()
    if sequences > 1:
        crossing = send(
            buf.at[0, quarter], buf.at[1, quarter], k.pair_send.at[0], k.pair_recv.at[0], place.partner()
        )
    for owner in own.arrivals():
        on_rows(0, own.rows(owner))
    if sequences > 1:
        crossing.wait_recv()
        other = TokenGather(place, buf.at[1], k.other_gather)
        other.start()
        k.at(1)
        between()
        for owner in other.arrivals():
            on_rows(1, other.rows(owner))
        crossing.wait_send()
    else:
        between()


def give_back(k, total):
    k.pair_sum[...] = total.astype(BF16)
    return send(k.pair_sum, k.pair_land, k.pair_send.at[1], k.pair_recv.at[1], k.place.partner())


def ffn_forward(k):
    sequences, length = k.kept[MOE].shape[:2]
    experts = k.kept[ROUTED].shape[0]
    place = k.place
    moe, branch = k.kept[MOE], k.branch
    k.early(SH, *(EX + e for e in range(experts)))
    moe[0, quarter_rows(length, place.me), :] = normalise(k.mid[...], k.gain[...]).astype(BF16)
    units = k.w[SH].shape[-1] // 3
    wide = k.w[EX].shape[-1] // 3

    def on_rows(s, rows):
        k.weight(SH)
        inner = nn(moe[s, rows, :], k.matrix(SH, 0, 2 * units))
        k.kept[SHARED][s, rows, :] = inner.astype(BF16)
        branch[s, rows, :] = nt(hidden_of(inner), k.matrix(SH, 2 * units, 3 * units))
        logits = nn(moe[s, rows, :], k.router[...])
        k.gates[s, rows, :] = pick_softmax(logits, k.chosen_cols[s, rows, :], 1)

    scatters = [TokenScatter(place, refs) for refs in k.scatters]

    def dispatch(s, e):
        index = s * experts + e
        held = slots_by_token(k.slot_rows[index : index + 1, :]).astype(F32).astype(BF16)
        k.kept[ROUTED][e, s * CAP : (s + 1) * CAP, :] = nn(held, moe[s]).astype(BF16)

    def expert(s, e):
        k.weight(EX + e)
        index = s * experts + e
        slots = slice(s * CAP, (s + 1) * CAP)
        inner = nn(k.kept[ROUTED][e, slots, :], k.matrix(EX + e, 0, 2 * wide))
        k.kept[ACT][e, slots, :] = inner.astype(BF16)
        outs = nt(hidden_of(inner), k.matrix(EX + e, 2 * wide, 3 * wide)).astype(BF16)
        if e < experts - 1:
            combine = tokens_by_slot(k.slot_cols[:, index : index + 1])
            branch[s] += k.gates[s, :, e : e + 1] * nn(combine, outs)
            return

        def block_of(owner):
            rows = quarter_rows(length, owner)
            combine = tokens_by_slot(k.slot_cols[rows, index : index + 1])
            return branch[s, rows, :] + k.gates[s, rows, e : e + 1] * nn(combine, outs)

        scatters[s].begin(block_of)

    def between():
        for e in range(experts):
            dispatch(0, e)
        k.gate_rows[0] = pick_softmax(nt(k.router_t[...], moe[0]), k.chosen_rows[0], 0)

    both_arrivals(k, moe, on_rows, between)
    k.local.start(moe, k.kept_out[MOE], True)
    k.local.start(k.kept[SHARED], k.kept_out[SHARED], True)
    k.at(2)
    for step, (s, e) in enumerate(expert_order(sequences, experts)):
        if s > 0:
            dispatch(s, e)
        expert(s, e)
        k.at(3 + step)
    for s in range(1, sequences):
        k.gate_rows[s] = pick_softmax(nt(k.router_t[...], moe[s]), k.chosen_rows[s], 0)
    k.local.start(k.kept[ROUTED], k.kept_out[ROUTED], True)
    k.local.start(k.kept[ACT], k.kept_out[ACT], True)
    if sequences > 1:
        returned = give_back(k, scatters[1].total())
    following = k.mid[...] + scatters[0].total()
    if sequences > 1:
        returned.wait_recv()
        following = following + k.pair_land[...].astype(F32)
        returned.wait_send()
    k.following[...] = following


def ffn_backward(k):
    sequences, length = k.kept[MOE].shape[:2]
    experts = k.kept[ROUTED].shape[0]
    place = k.place
    moe, up, moe_grad = k.kept[MOE], k.up, k.moe_grad
    routed, act, shared = k.kept[ROUTED], k.kept[ACT], k.kept[SHARED]
    load_shared = k.local.start(k.kept_in[SHARED], shared)
    k.early(SH, *(EX + e for e in range(experts)))
    load_act = [k.local.start(k.kept_in[ACT].at[e], act.at[e]) for e in range(experts)]
    load_routed = [k.local.start(k.kept_in[ROUTED].at[e], routed.at[e]) for e in range(experts)]
    load_moe = k.local.start(k.kept_in[MOE], moe)
    up[0, quarter_rows(length, place.me), :] = k.upstream[...].astype(BF16)
    units = k.w[SH].shape[-1] // 3
    wide = k.w[EX].shape[-1] // 3
    fresh = {SH}

    def on_rows(s, rows):
        k.weight(SH)
        if SH in fresh:
            fresh.remove(SH)
            load_shared.wait()
        inner = shared[s, rows, :].astype(F32)
        k.hidden_all[s, rows, :] = hidden_of(inner)
        down = nn(up[s, rows, :], k.matrix(SH, 2 * units, 3 * units))
        inner_grad = swiglu_back(down, inner)
        shared[s, rows, :] = inner_grad
        moe_grad[s, rows, :] = nt(inner_grad, k.matrix(SH, 0, 2 * units))

    scatters = [TokenScatter(place, refs) for refs in k.scatters]
    for s in range(sequences):
        k.slot_sums[s] = jnp.zeros_like(k.slot_sums[s])
    done = [0] * experts

    def expert(s, e):
        k.weight(EX + e)
        if not done[e]:
            load_act[e].wait()
            load_routed[e].wait()
        index = s * experts + e
        slots = slice(s * CAP, (s + 1) * CAP)
        held = slots_by_token(k.slot_rows[index : index + 1, :])
        gate_slot = jnp.sum(jnp.where(held, k.gate_rows[s, e : e + 1, :], 0.0), axis=1, keepdims=True)
        arrived = nn(held.astype(F32).astype(BF16), up[s]).astype(BF16)
        k.slot_grad[slots, :] = (arrived.astype(F32) * gate_slot).astype(BF16)
        inner = act[e, slots, :].astype(F32)
        hidden = hidden_of(inner)
        k.hidden[slots, :] = hidden
        down = nn(arrived, k.matrix(EX + e, 2 * wide, 3 * wide))
        slot_dot = jnp.sum(hidden.astype(F32) * down, axis=1, keepdims=True)
        k.slot_sums[s, e : e + 1, :] = jnp.sum(jnp.where(held, slot_dot, 0.0), axis=0, keepdims=True)
        inner_grad = swiglu_back(down * gate_slot, inner)
        act[e, slots, :] = inner_grad
        back = nt(inner_grad, k.matrix(EX + e, 0, 2 * wide)).astype(BF16)
        if e < experts - 1:
            combine = tokens_by_slot(k.slot_cols[:, index : index + 1])
            moe_grad[s] += nn(combine, back)
        else:
            gates = k.gate_rows[s]
            pair = jnp.sum(gates, axis=0, keepdims=True)
            product = 0.5 * (pair * pair - jnp.sum(gates * gates, axis=0, keepdims=True))
            sums = k.slot_sums[s]
            logit_grad = k.chosen_rows[s] * product * (2.0 * sums - jnp.sum(sums, axis=0, keepdims=True))
            k.logit_grad[s] = logit_grad.astype(BF16)

            def block_of(owner):
                rows = quarter_rows(length, owner)
                combine = tokens_by_slot(k.slot_cols[rows, index : index + 1])
                turned = tn(k.logit_grad[s, :, rows], k.router_t[...])
                return moe_grad[s, rows, :] + nn(combine, back) + turned

            scatters[s].begin(block_of)
        done[e] += 1
        if done[e] == sequences:
            k.put(EX + e, 0, tn(routed[e], act[e]))
            k.put(EX + e, 2 * wide, tn(k.slot_grad[...], k.hidden[...]))
            k.made(EX + e)

    order = expert_order(sequences, experts)
    both_arrivals(k, up, on_rows, lambda: expert(*order[0]))
    load_moe.wait()
    whole = sequences * length
    k.put(SH, 0, tn(moe[...].reshape(whole, -1), shared[...].reshape(whole, -1)))
    k.put(SH, 2 * units, tn(up[...].reshape(whole, -1), k.hidden_all[...].reshape(whole, -1)))
    k.made(SH)
    k.at(2)
    for step, (s, e) in enumerate(order[1:]):
        expert(s, e)
        k.at(3 + step)
    k.router_grad[...] = sum(nn(k.logit_grad[s], moe[s]) for s in range(sequences))
    if sequences > 1:
        returned = give_back(k, scatters[1].total())
    total = scatters[0].total()
    if sequences > 1:
        returned.wait_recv()
        total = total + k.pair_land[...].astype(F32)
        returned.wait_send()
    inward, k.gain_grad[...] = normalise_back(k.mid[...], k.gain[...], total)
    k.grad[...] = k.upstream[...] + inward


def last_sums(k):
    place = k.place
    stage = k.stage
    stage[0] = k.small[...]
    partners = (place.member(place.core_peer), place.member(place.y_peer), place.beside())
    for step, partner in enumerate(partners):
        copy = send(stage.at[step], k.land.at[step], k.small_send.at[step], k.small_recv.at[step], partner)
        copy.wait_recv()
        stage[step + 1] = stage[step] + k.land[step]
        copy.wait_send()
    k.at(1)
    last = len(partners)
    copies = []
    for away in (1, 2, 3):
        copies.append(
            send(
                stage.at[last],
                k.rows_z.at[place.z],
                k.small_send.at[last + away - 1],
                k.small_recv.at[last + away - 1],
                place.beyond(away),
            )
        )
    k.rows_z[place.z] = stage[last]
    for copy in copies:
        copy.wait_recv()
    k.small_sum[...] = (k.rows_z[0] + k.rows_z[1]) + (k.rows_z[2] + k.rows_z[3])
    for copy in copies:
        copy.wait_send()


class Far:
    def __init__(self, array):
        self.array = array


class Out:
    def __init__(self, shape, kind=F32, far=False):
        self.shape, self.kind, self.far = shape, kind, far


class Store:
    def __init__(self, height, width, columns, parts, paired):
        self.height, self.width, self.columns, self.parts, self.paired = height, width, columns, parts, paired
        self.source, self.full = {}, {}
        self.z, self.x = {}, {}
        self.made, self.sums, self.totals = {}, {}, {}

    def keys(self, layer, matrix):
        return [(layer, matrix, part) for part in range(len(self.parts[matrix]))]

    def shape_of(self, matrix):
        if self.paired:
            return (4, 2, self.height, self.columns[matrix])
        return (1, 1, self.width, self.columns[matrix])


def is_leaf(value):
    return not isinstance(value, (dict, list))


def call(store, body, collective_id, ins, outs, scratch, layer, weights=(), made=(), plan=(), tokens=True):
    ins, outs, scratch = dict(ins), dict(outs), dict(scratch)
    dma, vmem = pltpu.SemaphoreType.DMA, pltpu.VMEM
    width = store.width
    starts = [(kind, key) for _, kind, key, *end in plan if not end]
    starts += [(SUM_X, (layer, matrix)) for matrix in made if (layer, matrix) in store.own_sums]
    keys = [[key for own, key in starts if own == kind] for kind in range(4)]
    keys_in = [key for matrix in weights for key in store.keys(layer, matrix)]
    ins["src"] = {key: Far(store.source[key[:2]]) for key in keys[GET_Z]}
    ins["full_in"] = {m: Far(store.full[layer, m]) for m in weights if not store.paired}
    ins["z_in"], ins["x_in"] = {}, {}
    if store.paired:
        wanted = set(keys_in) | set(keys[GET_X])
        ins["z_in"] = {key: Far(store.z[key]) for key in sorted(wanted - set(keys[GET_Z]))}
        ins["x_in"] = {key: Far(store.x[key]) for key in sorted(set(keys_in) - set(keys[GET_X]))}
    ins["made_in"] = {key: Far(store.made[key]) for key in keys[SUM_X] if key in store.made}
    ins["sums_in"] = {key: Far(store.sums[key]) for key in keys[SUM_Z] if key not in keys[SUM_X]}

    def part_shape(key):
        return (4, store.parts[key[1]][key[2]][1], store.columns[key[1]])

    def block_shape(key):
        return (4, store.height, store.columns[key[1]])

    outs["z_out"] = {key: Out(part_shape(key), BF16, True) for key in keys[GET_Z]}
    outs["x_out"] = {key: Out(part_shape(key), BF16, True) for key in keys[GET_X]}
    outs["sums_out"] = {key: Out(block_shape(key), BF16) for key in keys[SUM_X]}
    outs["totals"] = {key: [Out(block_shape(key)[1:])] * (1 if key[1] == ATT else 2) for key in keys[SUM_Z]}
    outs["made_out"] = {
        m: Out(store.shape_of(m), BF16, True) for m in made if (layer, m) not in store.own_sums
    }
    scratch["w"] = {m: vmem(store.shape_of(m), BF16) for m in weights}
    scratch["sems"] = {
        GET_Z: {key: [dma((4,)), dma((4,)), dma((1,))] for key in keys[GET_Z]},
        GET_X: {key: [dma((1,)), dma((1,))] for key in keys[GET_X]},
        SUM_X: {key: [dma((1,)), dma((1,)), dma((1,))] for key in keys[SUM_X]},
        SUM_Z: {key: [dma((4,)), dma((4,)), dma((1,))] for key in keys[SUM_Z]},
    }
    scratch["blocks"] = {key: vmem(block_shape(key), BF16) for key in keys[SUM_X]}
    scratch["own"] = {key: vmem(block_shape(key), BF16) for key in keys[SUM_X] if key in store.made}
    scratch["lands"] = {key: vmem(block_shape(key), BF16) for key in keys[SUM_Z]}
    scratch["lsem"] = dma((2 * len(keys_in) + 12,))
    trees = [jax.tree.flatten(tree, is_leaf=is_leaf) for tree in (ins, outs, scratch)]
    (ins_flat, _), (outs_flat, outs_tree), (scratch_flat, _) = trees
    around = bool(starts)

    def kernel(*refs):
        k = types.SimpleNamespace()
        at = 0
        for flat, tree in trees:
            for name, value in jax.tree.unflatten(tree, refs[at : at + len(flat)]).items():
                setattr(k, name, value)
            at += len(flat)
        place = k.place = Place()
        k.local = Local(k.lsem)
        peers = place.greet_sequence() if tokens else []
        if around:
            peers += place.greet_all()
        elif store.paired:
            peers += [place.partner()]
        place.greet(peers)

        def job(kind, key):
            sems = k.sems[kind][key]
            if kind == GET_Z:
                return Straight(place, k.src[key], k.z_out[key], store.parts[key[1]][key[2]], sems)
            if kind == GET_X:
                source = k.z_out[key] if key in k.z_out else k.z_in[key]
                return Aside(place, source, k.x_out[key], sems)
            if kind == SUM_X:
                source = k.made_in[key] if key in k.made_in else k.w[key[1]]
                return AsideSum(place, source, k.own.get(key), k.blocks[key], k.sums_out[key], sems)
            source = k.sums_out[key] if key in k.sums_out else k.sums_in[key]
            return StraightSum(place, source, k.lands[key], k.totals[key], sems)

        running, ended = {}, set()

        def start(kind, key):
            running[kind, key] = job(kind, key)
            running[kind, key].start()

        def end(kind, key):
            if (kind, key) not in ended:
                ended.add((kind, key))
                running[kind, key].arrived()

        def at_point(point):
            for own, kind, key, *is_end in plan:
                if own == point:
                    (end if is_end else start)(kind, key)

        loads, loaded = {}, set()

        def parts_of(matrix):
            return [(key, *store.parts[matrix][key[2]]) for key in store.keys(layer, matrix)]

        def load_part(key, first, rows):
            w = k.w[key[1]]
            span = pl.ds(first, rows)
            for got, landed, kind, x in (
                (k.z_in, k.z_out, GET_Z, place.x),
                (k.x_in, k.x_out, GET_X, 1 - place.x),
            ):
                if key in landed:
                    end(kind, key)
                source = landed[key] if key in landed else got[key]
                loads.setdefault(key, []).append(k.local.start(source, w.at[:, x, span]))

        def early(*matrices):
            for matrix in matrices:
                if not store.paired:
                    loads[matrix] = [k.local.start(k.full_in[matrix], k.w[matrix])]
                    continue
                for key, first, rows in parts_of(matrix):
                    if key in k.z_in and key in k.x_in:
                        load_part(key, first, rows)

        def weight(matrix):
            if matrix in loaded:
                return
            loaded.add(matrix)
            if not store.paired:
                for copy in loads[matrix]:
                    copy.wait()
                return
            for key, first, rows in parts_of(matrix):
                if key not in loads:
                    load_part(key, first, rows)
            for key, *_ in parts_of(matrix):
                for copy in loads[key]:
                    copy.wait()

        def matrix_of(matrix, first, last):
            value = k.w[matrix][:, :, :, first:last]
            return value.reshape(width, last - first)

        def put(matrix, first, value):
            ref = k.w[matrix]
            shape = (*ref.shape[:3], value.shape[1])
            ref[:, :, :, first : first + value.shape[1]] = value.astype(BF16).reshape(shape)

        def finished(matrix):
            if (layer, matrix) in k.sums_out:
                start(SUM_X, (layer, matrix))
            else:
                k.local.start(k.w[matrix], k.made_out[matrix], True)

        k.at, k.early, k.weight, k.matrix, k.put, k.made = at_point, early, weight, matrix_of, put, finished
        at_point(0)
        body(k)
        for kind, key in running:
            end(kind, key)
        for transfer in running.values():
            transfer.close()
        k.local.close()

    hbm, near = pl.BlockSpec(memory_space=pl.ANY), pl.BlockSpec(memory_space=pltpu.VMEM)
    results = pl.pallas_call(
        kernel,
        out_shape=[jax.ShapeDtypeStruct(out.shape, out.kind) for out in outs_flat],
        in_specs=[hbm if isinstance(value, Far) else near for value in ins_flat],
        out_specs=[hbm if out.far else near for out in outs_flat],
        scratch_shapes=scratch_flat,
        compiler_params=pltpu.CompilerParams(
            collective_id=collective_id, has_side_effects=True, vmem_limit_bytes=VMEM_LIMIT
        ),
    )(*[value.array if isinstance(value, Far) else value for value in ins_flat])
    result = types.SimpleNamespace(**jax.tree.unflatten(outs_tree, results))
    store.z |= result.z_out
    store.x |= result.x_out
    store.sums |= result.sums_out
    store.totals |= result.totals
    store.made |= {(layer, m): value for m, value in result.made_out.items()}
    return result


def on_device(
    ring, stream, cotangent, segments, expert_pick, slot_index, norm_gains,
    attention, projection, router, widening, narrowing, expansion, contraction,
):
    layers = attention.shape[0]
    segment = segments[0]
    length = segment.shape[0]
    all_experts = expansion.shape[1]
    width = stream.shape[1]
    quarter = stream.shape[0]
    wide = attention.shape[3]
    units = widening.shape[3]
    height = attention.shape[2]
    paired = ring == 8
    sequences = 2 if paired else 1
    experts = all_experts // sequences
    shared_units = units // sequences
    dp = lax.axis_index("dp")
    upper = (dp // 2) % 2 == 1

    halfway = HEAD // 2
    inverse = jnp.exp(jnp.arange(halfway, dtype=F32) * (-2.0 * math.log(10000.0) / HEAD))
    phases = jnp.arange(length, dtype=F32)[:, None] * inverse[None, :]
    cosine, sine = jnp.cos(phases), jnp.sin(phases)
    cosine = jnp.concatenate([cosine] * 4, axis=1)
    sine = jnp.concatenate([-sine, sine] * 2, axis=1)
    places = dict(cosine=cosine, sine=sine, seg_row=segment[None, :], seg_col=segment[:, None])

    def local_first(values, axis):
        if not paired:
            return values
        return jnp.where(upper, jnp.roll(values, -experts, axis), values)

    def known_first(values, axis):
        if not paired:
            return values
        return jnp.where(upper, jnp.roll(values, experts, axis), values)

    picks = jnp.concatenate([expert_pick, slot_index], axis=2)[:, None]
    if paired:
        swap = [(at, (at // 4) * 4 + (at % 4 + 2) % 4) for at in range(ring)]
        picks = jnp.concatenate([picks, lax.ppermute(picks, "dp", swap)], axis=1)
    expert_of, slot_of = picks[..., :2], picks[..., 2:]
    held = expert_of[..., None] == jnp.arange(all_experts, dtype=jnp.int32)
    slots = local_first(jnp.sum(jnp.where(held, slot_of[..., None] + 1, 0), axis=3) - 1, 3)
    chosen = local_first(jnp.any(held, axis=3).astype(F32), 3)
    slots = slots[..., :experts]
    slot_rows = jnp.swapaxes(slots, 2, 3).reshape(layers, sequences * experts, length)
    slot_cols = jnp.swapaxes(slots, 1, 2).reshape(layers, length, sequences * experts)
    chosen_cols = jnp.pad(chosen, ((0, 0), (0, 0), (0, 0), (0, LANES - all_experts)))
    chosen_rows = jnp.pad(jnp.swapaxes(chosen, 2, 3), ((0, 0), (0, 0), (0, 8 - all_experts), (0, 0)))
    router_own = local_first(router, 2)
    router_wide = jnp.pad(router_own, ((0, 0), (0, 0), (0, LANES - all_experts)))
    router_t = jnp.pad(jnp.swapaxes(router_own, 1, 2), ((0, 0), (0, 8 - all_experts), (0, 0)))

    projection_t = jnp.swapaxes(projection, 1, 2)
    narrowing_t = jnp.swapaxes(narrowing, 1, 2)
    contraction_t = jnp.swapaxes(contraction, 2, 3)
    columns = {ATT: 4 * wide, SH: 3 * shared_units} | {EX + e: 3 * units for e in range(experts)}
    parts = {matrix: [(0, height)] for matrix in columns}
    if paired:
        parts[EX + 1] = [(0, height // 3), (height // 3, height - height // 3)]
    store = Store(height, width, columns, parts, paired)
    for layer in range(layers):
        store.source[layer, ATT] = jnp.concatenate([*attention[layer], projection_t[layer]], axis=-1)
        thirds = (widening[layer, 0], widening[layer, 1], narrowing_t[layer])
        whole = [
            jnp.concatenate([expansion[layer, e, 0], expansion[layer, e, 1], contraction_t[layer, e]], axis=-1)
            for e in range(all_experts)
        ]
        if paired:
            store.source[layer, SH] = jnp.stack(
                [
                    jnp.concatenate([third[:, a * shared_units : (a + 1) * shared_units] for third in thirds], axis=-1)
                    for a in range(2)
                ]
            )
            for e in range(experts):
                store.source[layer, EX + e] = jnp.stack([whole[e], whole[experts + e]])
        else:
            store.source[layer, SH] = jnp.concatenate(thirds, axis=-1)
            for e in range(experts):
                store.source[layer, EX + e] = whole[e]
    if not paired:
        store.full = {
            key: lax.all_gather(source, "dp", axis=0, tiled=True)[None, None] for key, source in store.source.items()
        }

    vmem = pltpu.VMEM
    token_scatter = scatter_scratch(length, width)
    pair_scratch = dict(scatters=[token_scatter] * sequences)
    if paired:
        pair_scratch |= dict(
            other_gather=gather_scratch(),
            pair_send=pltpu.SemaphoreType.DMA((2,)),
            pair_recv=pltpu.SemaphoreType.DMA((2,)),
            pair_sum=vmem((quarter, width), BF16),
            pair_land=vmem((quarter, width), BF16),
        )
    attention_shapes = {
        NRM: (length, width), QK: (length, 2 * wide), V: (length, wide), ATTENDED: (length, wide)
    }
    ffn_shapes = {
        MOE: (sequences, length, width),
        SHARED: (sequences, length, 2 * shared_units),
        ROUTED: (experts, sequences * CAP, width),
        ACT: (experts, sequences * CAP, 2 * units),
    }
    ffn_matrices = [SH, *(EX + e for e in range(experts))]
    rows_out = Out((quarter, width))
    gain_out = Out((1, width))
    last = layers - 1

    def kept_scratch(shapes):
        return {name: vmem(shape, BF16) for name, shape in shapes.items()}

    def kept_outs(shapes):
        return {name: Out(shape, BF16, True) for name, shape in shapes.items()}

    def kept_ins(arrays):
        return {name: Far(array) for name, array in arrays.items()}

    store.own_sums = {(layer, matrix) for layer in range(layers) for matrix in (SH, EX)} if paired else set()
    saved = []
    current = stream
    next_id = 0
    for layer in range(layers):
        first, second = (layer, EX + 1, 0), (layer, EX + 1, 1)
        att, sh, ex = (layer, ATT, 0), (layer, SH, 0), (layer, EX, 0)
        if layer == 0:
            plan = [
                (0, GET_Z, att), (1, GET_Z, att, True), (1, GET_X, att), (1, GET_Z, sh), (2, GET_Z, ex),
                (3, GET_Z, first), (4, GET_Z, sh, True), (4, GET_X, sh),
            ]
        else:
            plan = [(0, GET_X, sh), (0, GET_Z, ex), (2, GET_Z, first)]
        result = call(
            store,
            attention_forward,
            next_id,
            dict(x=current, gain=norm_gains[layer, 0][None], **places),
            dict(mid=rows_out, kept_out=kept_outs(attention_shapes)),
            dict(kept=kept_scratch(attention_shapes), gather=gather_scratch(), scatter=token_scatter),
            layer,
            [ATT],
            plan=plan if paired else (),
        )
        mid, attention_kept = result.mid, result.kept_out
        plan = [
            (0, GET_X, ex), (0, GET_X, first), (1, GET_Z, second), (3, GET_Z, second, True), (3, GET_X, second)
        ]
        if layer < last:
            att, sh = (layer + 1, ATT, 0), (layer + 1, SH, 0)
            plan += [(1, GET_Z, att), (1, GET_Z, sh), (5, GET_Z, att, True), (5, GET_X, att)]
        result = call(
            store,
            ffn_forward,
            next_id + 1,
            dict(
                mid=mid,
                gain=norm_gains[layer, 1][None],
                router=router_wide[layer],
                router_t=router_t[layer],
                slot_rows=slot_rows[layer],
                slot_cols=slot_cols[layer],
                chosen_rows=chosen_rows[layer],
                chosen_cols=chosen_cols[layer],
            ),
            dict(following=rows_out, gate_rows=Out((sequences, 8, length)), kept_out=kept_outs(ffn_shapes)),
            dict(
                kept=kept_scratch(ffn_shapes),
                branch=vmem((sequences, length, width), F32),
                gates=vmem((sequences, length, LANES), F32),
                gather=gather_scratch(),
                **pair_scratch,
            ),
            layer,
            ffn_matrices,
            plan=plan if paired else (),
        )
        saved.append((current, mid, attention_kept, result.gate_rows, result.kept_out))
        current = result.following
        next_id += 2

    upstream = cotangent
    gain_parts, router_parts = [None] * layers, [None] * layers
    for layer in reversed(range(layers)):
        x_in, mid, attention_kept, gate_rows, ffn_kept = saved[layer]
        plan = []
        if layer < last:
            above = (layer + 1, ATT)
            plan = [(0, SUM_X, above), (1, SUM_Z, (layer + 1, EX + 1)), (2, SUM_X, above, True), (2, SUM_Z, above)]
        result = call(
            store,
            ffn_backward,
            next_id,
            dict(
                upstream=upstream,
                mid=mid,
                gain=norm_gains[layer, 1][None],
                router_t=router_t[layer],
                slot_rows=slot_rows[layer],
                slot_cols=slot_cols[layer],
                chosen_rows=chosen_rows[layer],
                gate_rows=gate_rows,
                kept_in=kept_ins(ffn_kept),
            ),
            dict(grad=rows_out, gain_grad=gain_out, router_grad=Out((8, width))),
            dict(
                kept=kept_scratch(ffn_shapes),
                hidden_all=vmem((sequences, length, shared_units), BF16),
                hidden=vmem((sequences * CAP, units), BF16),
                slot_grad=vmem((sequences * CAP, width), BF16),
                moe_grad=vmem((sequences, length, width), F32),
                slot_sums=vmem((sequences, 8, length), F32),
                logit_grad=vmem((sequences, 8, length), BF16),
                up=vmem((sequences, length, width), BF16),
                gather=gather_scratch(),
                **pair_scratch,
            ),
            layer,
            ffn_matrices,
            ffn_matrices,
            plan=plan if paired else (),
        )
        mid_grad, gain_two, router_parts[layer] = result.grad, result.gain_grad, result.router_grad
        plan = [(0, SUM_Z, (layer, SH)), (0, SUM_X, (layer, EX + 1)), (1, SUM_Z, (layer, EX))]
        result = call(
            store,
            attention_backward,
            next_id + 1,
            dict(
                upstream=mid_grad, x=x_in, gain=norm_gains[layer, 0][None], kept_in=kept_ins(attention_kept), **places
            ),
            dict(grad=rows_out, gain_grad=gain_out),
            dict(
                kept=kept_scratch(attention_shapes),
                outer=vmem((length, wide), BF16),
                dqk=vmem((length, 2 * wide), F32),
                dv=vmem((length, wide), F32),
                dqkv=vmem((length, 3 * wide), BF16),
                up=vmem((length, width), BF16),
                gather=gather_scratch(),
                scatter=token_scatter,
            ),
            layer,
            [ATT],
            [ATT],
            plan=plan if paired else (),
        )
        upstream = result.grad
        gain_parts[layer] = jnp.concatenate([result.gain_grad, gain_two], axis=0)
        next_id += 2

    router_parts = [known_first(part[:all_experts], 0) for part in router_parts]
    small = jnp.concatenate(gain_parts + router_parts, axis=0)
    if paired:
        count = small.shape[0]
        padded = -(-count // 8) * 8
        small = jnp.pad(small, ((0, padded - count), (0, 0)))
        small = call(
            store,
            last_sums,
            next_id,
            dict(small=small),
            dict(small_sum=Out((padded, width))),
            dict(
                stage=vmem((4, padded, width), F32),
                land=vmem((3, padded, width), F32),
                rows_z=vmem((4, padded, width), F32),
                small_send=pltpu.SemaphoreType.DMA((6,)),
                small_recv=pltpu.SemaphoreType.DMA((6,)),
            ),
            0,
            plan=[(0, SUM_Z, (0, EX + 1)), (0, SUM_X, (0, ATT)), (1, SUM_X, (0, ATT), True), (1, SUM_Z, (0, ATT))],
        ).small_sum
    else:
        small = lax.psum(small, ("dp", "tensor"))
        store.totals = {
            key: [lax.psum_scatter(part[0, 0], "dp", scatter_dimension=0, tiled=True).astype(F32)]
            for key, part in store.made.items()
        }
    gains_grad = small[: 2 * layers].reshape(layers, 2, width)
    router_grad = small[2 * layers : 2 * layers + layers * all_experts].reshape(layers, all_experts, width)

    def split(pieces):
        mine, theirs = pieces
        return jnp.where(upper, theirs, mine), jnp.where(upper, mine, theirs)

    attention_grad, projection_grad, widening_grad, narrowing_grad, expansion_grad, contraction_grad = (
        [] for _ in range(6)
    )
    for layer in range(layers):
        (whole,) = store.totals[layer, ATT]
        attention_grad.append(jnp.stack([whole[:, n * wide : (n + 1) * wide] for n in range(3)]))
        projection_grad.append(whole[:, 3 * wide :].T)
        if paired:
            halves = split(store.totals[layer, SH])
            shared = [
                jnp.concatenate([half[:, n * shared_units : (n + 1) * shared_units] for half in halves], axis=1)
                for n in range(3)
            ]
            by_expert = [split(store.totals[layer, EX + e]) for e in range(experts)]
            wholes = [by_expert[e][a] for a in range(2) for e in range(experts)]
        else:
            (whole,) = store.totals[layer, SH]
            shared = [whole[:, n * units : (n + 1) * units] for n in range(3)]
            wholes = [store.totals[layer, EX + e][0] for e in range(experts)]
        widening_grad.append(jnp.stack(shared[:2]))
        narrowing_grad.append(shared[2].T)
        expansion_grad.append(
            jnp.stack([jnp.stack([one[:, :units], one[:, units : 2 * units]]) for one in wholes])
        )
        contraction_grad.append(jnp.stack([one[:, 2 * units :].T for one in wholes]))
    return (
        current,
        upstream,
        gains_grad,
        jnp.stack(attention_grad),
        jnp.stack(projection_grad),
        jnp.swapaxes(router_grad, 1, 2),
        jnp.stack(widening_grad),
        jnp.stack(narrowing_grad),
        jnp.stack(expansion_grad),
        jnp.stack(contraction_grad),
    )


def solution(mesh):
    placed = (
        P(("dp", "tensor"), None),
        P(("dp", "tensor"), None),
        P("dp", None),
        P(None, "dp", None),
        P(None, "dp", None),
        P(),
        P(None, None, "dp", "tensor"),
        P(None, "tensor", "dp"),
        P(),
        P(None, None, "dp", "tensor"),
        P(None, "tensor", "dp"),
        P(None, None, None, "dp", "tensor"),
        P(None, None, "tensor", "dp"),
    )
    return jax.shard_map(
        functools.partial(on_device, mesh.shape["dp"]),
        mesh=mesh,
        in_specs=placed,
        out_specs=(
            P(("dp", "tensor"), None),
            P(("dp", "tensor"), None),
            P(),
            P(None, None, "dp", "tensor"),
            P(None, "tensor", "dp"),
            P(),
            P(None, None, "dp", "tensor"),
            P(None, "tensor", "dp"),
            P(None, None, None, "dp", "tensor"),
            P(None, None, "tensor", "dp"),
        ),
        check_vma=False,
    )
```

```python
import functools
import math
import types

import jax
import jax.numpy as jnp
from jax import lax
from jax.experimental import pallas as pl
from jax.experimental.pallas import tpu as pltpu
from jax.sharding import PartitionSpec as P

HEAD = 64
CAP = 640
LANES = 128
BF16 = jnp.bfloat16
F32 = jnp.float32
QKV, PRJ, SH, EX = range(4)
NRM, TURNED, MOE, SHARED, ROUTED, ACT = range(6)
GET_Z, GET_X, SUM_X, SUM_Z = range(4)
VMEM_LIMIT = 63 * 1024 * 1024


def nn(left, right):
    return lax.dot_general(left, right, (((1,), (0,)), ((), ())), preferred_element_type=F32)


def nt(left, right):
    return lax.dot_general(left, right, (((1,), (1,)), ((), ())), preferred_element_type=F32)


def tn(left, right):
    return lax.dot_general(left, right, (((0,), (0,)), ((), ())), preferred_element_type=F32)


class Place:
    def __init__(self):
        self.dp = lax.axis_index("dp")
        self.me = lax.axis_index("tensor")
        core = lax.rem(self.me, 2)
        self.core_peer = self.me + 1 - 2 * core
        self.y_peer = lax.rem(self.me + 2, 4)
        self.far_peer = lax.rem(self.core_peer + 2, 4)
        self.z = lax.div(self.dp, 2)
        self.x = lax.rem(self.dp, 2)
        self.half = lax.rem(self.z, 2)

    def member(self, tensor):
        return (self.dp, tensor)

    def row(self, away, x):
        return lax.rem(self.z + away + 4, 4) * 2 + x

    def beyond(self, away):
        return (self.row(away, self.x), self.me)

    def beside(self):
        return (self.row(0, 1 - self.x), self.me)

    def partner(self):
        return ((self.z + 1 - 2 * self.half) * 2 + self.x, self.me)

    def greet(self, peers):
        barrier = pltpu.get_barrier_semaphore()
        for peer in peers:
            pl.semaphore_signal(barrier, inc=1, device_id=peer, device_id_type=pl.DeviceIdType.MESH)
        pl.semaphore_wait(barrier, len(peers))

    def greet_sequence(self):
        return [self.member(self.core_peer), self.member(self.y_peer)]

    def greet_all(self):
        return [self.beside(), self.beyond(1), self.beyond(2), self.beyond(3)]


def send(source, target, send_sem, recv_sem, device):
    copy = pltpu.make_async_remote_copy(
        src_ref=source,
        dst_ref=target,
        send_sem=send_sem,
        recv_sem=recv_sem,
        device_id=device,
        device_id_type=pl.DeviceIdType.MESH,
    )
    copy.start()
    return copy


class Local:
    def __init__(self, sems):
        self.sems, self.used, self.open = sems, 0, []

    def start(self, source, target, keep=False):
        copy = pltpu.make_async_copy(source, target, self.sems.at[self.used])
        self.used += 1
        copy.start()
        if keep:
            self.open.append(copy)
        return copy

    def close(self):
        for copy in self.open:
            copy.wait()


def quarter_rows(length, member):
    quarter = length // 4
    return pl.ds(pl.multiple_of(member * quarter, quarter), quarter)


class TokenGather:
    def __init__(self, place, buf, sems):
        self.place, self.buf = place, buf
        self.sems = (sems["send_sem"], sems["recv_sem"])

    def rows(self, member):
        return quarter_rows(self.buf.shape[0], member)

    def pass_on(self, owner, target, slot):
        block = self.buf.at[self.rows(owner)]
        return send(block, block, self.sems[0].at[slot], self.sems[1].at[slot], self.place.member(target))

    def start(self):
        place = self.place
        self.far = self.pass_on(place.me, place.y_peer, 1)
        self.near = self.pass_on(place.me, place.core_peer, 0)

    def arrivals(self):
        place = self.place
        yield place.me
        self.near.wait_recv()
        yield place.core_peer
        self.far.wait_recv()
        self.onward = self.pass_on(place.y_peer, place.core_peer, 2)
        yield place.y_peer
        self.onward.wait_recv()
        yield place.far_peer
        self.near.wait_send()
        self.far.wait_send()
        self.onward.wait_send()


class TokenScatter:
    def __init__(self, place, refs):
        self.place = place
        refs = types.SimpleNamespace(**refs)
        self.part, self.landing, self.summed, self.crossed = refs.part, refs.landing, refs.summed, refs.crossed
        self.sems = (refs.send_sem, refs.recv_sem)

    def push(self, source, target, slot, member):
        return send(source, target, self.sems[0].at[slot], self.sems[1].at[slot], self.place.member(member))

    def begin(self, block_of):
        place, part = self.place, self.part
        part[0] = block_of(place.far_peer).astype(BF16)
        self.first = self.push(part.at[0], self.landing.at[0], 0, place.core_peer)
        crossing = block_of(place.y_peer)
        self.first.wait_recv()
        self.summed[...] = (crossing + self.landing[0].astype(F32)).astype(BF16)
        self.across = self.push(self.summed, self.crossed, 1, place.y_peer)
        part[1] = block_of(place.core_peer).astype(BF16)
        self.second = self.push(part.at[1], self.landing.at[1], 2, place.core_peer)
        self.own = block_of(place.me)

    def total(self):
        self.second.wait_recv()
        own = self.own + self.landing[1].astype(F32)
        self.across.wait_recv()
        own = own + self.crossed[...].astype(F32)
        self.first.wait_send()
        self.second.wait_send()
        self.across.wait_send()
        return own


def scatter_scratch(length, width):
    quarter = length // 4
    return dict(
        part=pltpu.VMEM((2, quarter, width), BF16),
        landing=pltpu.VMEM((2, quarter, width), BF16),
        summed=pltpu.VMEM((quarter, width), BF16),
        crossed=pltpu.VMEM((quarter, width), BF16),
        send_sem=pltpu.SemaphoreType.DMA((3,)),
        recv_sem=pltpu.SemaphoreType.DMA((3,)),
    )


def gather_scratch():
    return dict(send_sem=pltpu.SemaphoreType.DMA((3,)), recv_sem=pltpu.SemaphoreType.DMA((3,)))


class Straight:
    def __init__(self, place, source, target, rows, sems):
        self.place, self.source, self.target, self.rows = place, source, target, rows
        self.send_sem, self.recv_sem, self.local_sem = sems

    def part_for(self, away):
        source = self.source
        if len(source.shape) == 3:
            source = source.at[lax.rem(self.place.z + away, 2)]
        return source.at[pl.ds(*self.rows)]

    def start(self):
        place, mine = self.place, self.target.at[self.place.z]
        self.own = pltpu.make_async_copy(self.part_for(0), mine, self.local_sem.at[0])
        self.own.start()
        self.copies = [
            send(self.part_for(away), mine, self.send_sem.at[away], self.recv_sem.at[away], place.beyond(away))
            for away in (2, 1, 3)
        ]

    def arrived(self):
        self.own.wait()
        for copy in self.copies:
            copy.wait_recv()

    def close(self):
        for copy in self.copies:
            copy.wait_send()


class Aside:
    def __init__(self, place, source, target, sems):
        self.place, self.source, self.target = place, source, target
        self.send_sem, self.recv_sem = sems

    def start(self):
        self.copy = send(
            self.source, self.target, self.send_sem.at[0], self.recv_sem.at[0], self.place.beside()
        )

    def arrived(self):
        self.copy.wait_recv()

    def close(self):
        self.copy.wait_send()


class AsideSum:
    def __init__(self, place, source, own, landing, out, sems):
        self.place, self.source, self.own, self.landing, self.out = place, source, own, landing, out
        self.send_sem, self.recv_sem, self.local_sem = sems

    def start(self):
        place = self.place
        self.copy = send(
            self.source.at[:, 1 - place.x], self.landing, self.send_sem.at[0], self.recv_sem.at[0], place.beside()
        )
        if self.own is not None:
            self.load = pltpu.make_async_copy(self.source.at[:, place.x], self.own, self.local_sem.at[0])
            self.load.start()

    def arrived(self):
        self.copy.wait_recv()
        if self.own is not None:
            self.load.wait()
        for at in range(4):
            own = self.source[at, self.place.x] if self.own is None else self.own[at]
            self.landing[at] = (own.astype(F32) + self.landing[at].astype(F32)).astype(BF16)
        if self.out is not None:
            self.store = pltpu.make_async_copy(self.landing, self.out, self.local_sem.at[1])
            self.store.start()

    def close(self):
        self.copy.wait_send()
        if self.out is not None:
            self.store.wait()


class StraightSum:
    def __init__(self, place, source, landing, totals, sems):
        self.place, self.source, self.landing, self.totals = place, source, landing, totals
        self.send_sem, self.recv_sem, self.local_sem = sems

    def start(self):
        place = self.place
        self.copies = [
            send(
                self.source.at[lax.rem(place.z + away, 4)],
                self.landing.at[away],
                self.send_sem.at[away],
                self.recv_sem.at[away],
                place.beyond(away),
            )
            for away in (2, 1, 3)
        ]
        self.own = pltpu.make_async_copy(self.source.at[place.z], self.landing.at[0], self.local_sem.at[0])
        self.own.start()

    def arrived(self):
        for copy in self.copies:
            copy.wait_recv()
        self.own.wait()
        blocks = [self.landing[away].astype(F32) for away in range(4)]
        if len(self.totals) == 1:
            self.totals[0][...] = ((blocks[0] + blocks[2]) + (blocks[1] + blocks[3])).astype(BF16)
        else:
            self.totals[0][...] = (blocks[0] + blocks[2]).astype(BF16)
            self.totals[1][...] = (blocks[1] + blocks[3]).astype(BF16)

    def close(self):
        for copy in self.copies:
            copy.wait_send()


def normalise(values, gain):
    factor = lax.rsqrt(jnp.mean(values * values, axis=-1, keepdims=True) + 1e-06)
    return values * factor * gain


def normalise_back(values, gain, upstream):
    factor = lax.rsqrt(jnp.mean(values * values, axis=-1, keepdims=True) + 1e-06)
    scaled = upstream * gain
    inward = factor * scaled - values * factor * factor * factor * jnp.mean(
        scaled * values, axis=-1, keepdims=True
    )
    return inward, jnp.sum(upstream * values * factor, axis=0, keepdims=True)


def swap_halves(values):
    width = values.shape[1]
    lane = lax.broadcasted_iota(jnp.int32, values.shape, 1)
    return jnp.where(
        lax.rem(lane, HEAD) < HEAD // 2,
        pltpu.roll(values, width - HEAD // 2, 1),
        pltpu.roll(values, HEAD // 2, 1),
    )


def turn(values, cosine, sine):
    times = values.shape[1] // cosine.shape[1]
    return values * jnp.concatenate([cosine] * times, axis=1) + swap_halves(
        values
    ) * jnp.concatenate([sine] * times, axis=1)


def allowed_keys(seg_row, seg_col, offset, rows, extent):
    row_index = offset + lax.broadcasted_iota(jnp.int32, (rows, extent), 0)
    column_index = lax.broadcasted_iota(jnp.int32, (rows, extent), 1)
    return (column_index <= row_index) & (
        seg_row[:, :extent] == seg_col[offset : offset + rows, :]
    )


def softmax_rows(query, keys, allowed):
    masked = jnp.where(allowed, nt(query, keys), -1e30)
    exponent = jnp.exp(masked - jnp.max(masked, axis=-1, keepdims=True))
    return exponent * (1.0 / jnp.sum(exponent, axis=-1, keepdims=True))


def sigmoid(values):
    return 1.0 / (1.0 + jnp.exp(-values))


def attention_forward(k):
    length = k.kept[TURNED].shape[0]
    wide = k.kept[TURNED].shape[1] // 4
    heads = wide // HEAD
    place = k.place
    normed, turned = k.kept[NRM], k.kept[TURNED]
    k.early(QKV, PRJ)
    gather = TokenGather(place, normed, k.gather)
    normed[gather.rows(place.me), :] = normalise(k.x[...], k.gains[0:1, :]).astype(BF16)
    gather.start()
    k.at(1)
    k.weight(QKV)
    for owner in gather.arrivals():
        rows = gather.rows(owner)
        projected = nn(normed[rows, :], k.matrix(QKV, 0, 3 * wide))
        turned[rows, : 2 * wide] = turn(projected[:, : 2 * wide], k.cosine[rows, :], k.sine[rows, :]).astype(BF16)
        turned[rows, 2 * wide : 3 * wide] = projected[:, 2 * wide :].astype(BF16)
    k.local.start(normed, k.kept_out[NRM], True)
    k.at(2)
    block = 128
    for offset in range(0, length, block):
        extent = offset + block
        allowed = allowed_keys(k.seg_row, k.seg_col, offset, block, extent)
        for head in range(heads):
            first = head * HEAD
            query = turned[offset:extent, first : first + HEAD] * BF16(HEAD**-0.5)
            keys = turned[:extent, wide + first : wide + first + HEAD]
            values = turned[:extent, 2 * wide + first : 2 * wide + first + HEAD]
            probability = softmax_rows(query, keys, allowed).astype(BF16)
            turned[offset:extent, 3 * wide + first : 3 * wide + first + HEAD] = nn(probability, values).astype(BF16)
        if extent % 256 == 0:
            k.at(2 + extent // 256)
    k.local.start(turned, k.kept_out[TURNED], True)
    scatter = TokenScatter(place, k.scatter)
    k.weight(PRJ)
    scatter.begin(lambda owner: nt(turned[quarter_rows(length, owner), 3 * wide :], k.matrix(PRJ, 0, wide)))
    k.at(7)
    k.mid[...] = k.x[...] + scatter.total()


def attention_backward(k):
    sequences, length, width = k.up.shape
    wide = width // 4
    heads = wide // HEAD
    place = k.place
    up, normed = k.up.at[0], k.kept[MOE].at[0]
    turned, grads = (k.kept[MOE].at[1], k.up.at[1]) if sequences > 1 else (k.spare.at[0], k.spare.at[1])
    sums = k.moe_grad.at[0]
    load_turned = k.local.start(k.kept_in[TURNED], turned)
    load_normed = k.local.start(k.kept_in[NRM], normed)
    gather = TokenGather(place, up, k.own_gather)
    up[gather.rows(place.me), :] = k.grad[...].astype(BF16)
    load_rows = k.local.start(k.x, k.rows)
    gather.start()
    k.at(10)
    k.weight(QKV)
    k.weight(PRJ)
    sums[...] = jnp.zeros((length, width), F32)
    for owner in gather.arrivals():
        rows = gather.rows(owner)
        grads[rows, 3 * wide :] = nn(up[rows, :], k.matrix(PRJ, 0, wide)).astype(BF16)
    load_turned.wait()
    block = 128
    for offset in range(0, length, block):
        if offset % 256 == 0:
            k.at(11 + offset // 256)
        extent = offset + block
        allowed = allowed_keys(k.seg_row, k.seg_col, offset, block, extent)
        for head in range(heads):
            own, key, value, out = (slice(n * wide + head * HEAD, n * wide + (head + 1) * HEAD) for n in range(4))
            query = turned[offset:extent, own] * BF16(HEAD**-0.5)
            keys = turned[:extent, key]
            outer = grads[offset:extent, out]
            probability = softmax_rows(query, keys, allowed)
            inner = nt(outer, turned[:extent, value])
            score = probability * (inner - jnp.sum(probability * inner, axis=-1, keepdims=True))
            score = score.astype(BF16)
            sums[offset:extent, own] = nn(score, keys) * HEAD**-0.5
            sums[:extent, key] += tn(score, query)
            sums[:extent, value] += tn(probability.astype(BF16), outer)
    load_normed.wait()
    k.put_product(PRJ, 0, (up, turned, slice(3 * wide, 4 * wide)))
    k.made(PRJ)
    for offset in range(0, length, block):
        rows = slice(offset, offset + block)
        both = turn(sums[rows, : 2 * wide], k.cosine[rows, :], -k.sine[rows, :])
        grads[rows, : 2 * wide] = both.astype(BF16)
        grads[rows, 2 * wide : 3 * wide] = sums[rows, 2 * wide : 3 * wide].astype(BF16)
    scatter = TokenScatter(place, k.scatters[0])
    scatter.begin(lambda owner: nt(grads[quarter_rows(length, owner), : 3 * wide], k.matrix(QKV, 0, 3 * wide)))
    k.at(15)
    k.put_product(QKV, 0, (normed, grads, slice(0, 3 * wide)))
    k.made(QKV)
    k.at(16)
    load_rows.wait()
    inward, k.gain_att[...] = normalise_back(k.rows[...], k.gains[0:1, :], scatter.total())
    k.grad[...] += inward


def pick_softmax(logits, chosen, axis):
    highest = jnp.max(jnp.where(chosen > 0, logits, -1e30), axis=axis, keepdims=True)
    exponent = chosen * jnp.exp(jnp.where(chosen > 0, logits - highest, 0.0))
    return exponent / jnp.sum(exponent, axis=axis, keepdims=True)


def slot_halves():
    return [(0, CAP // 2), (CAP // 2, CAP)]


def slots_by_token(slot_row, first, last):
    shape = (last - first, slot_row.shape[1])
    return lax.broadcasted_iota(jnp.int32, shape, 0) == slot_row - first


def tokens_by_slot(slot_column):
    shape = (slot_column.shape[0], CAP)
    return (lax.broadcasted_iota(jnp.int32, shape, 1) == slot_column).astype(F32).astype(BF16)


def hidden_of(inner):
    units = inner.shape[1] // 2
    gate = inner[:, :units]
    return (gate * sigmoid(gate) * inner[:, units:]).astype(BF16)


def swiglu_back(down, inner):
    units = inner.shape[1] // 2
    gate, raised = inner[:, :units], inner[:, units:]
    squashed = sigmoid(gate)
    gate_grad = down * raised * squashed * (1.0 + gate * (1.0 - squashed))
    up_grad = down * gate * squashed
    return jnp.concatenate([gate_grad.astype(BF16), up_grad.astype(BF16)], axis=1)


def expert_order(sequences, experts):
    if sequences == 1:
        return [(0, e) for e in range(experts)]
    return [(0, 0), (1, 0), (1, 1), (0, 1)]


def both_arrivals(k, buf, on_rows, between, point):
    place = k.place
    sequences = buf.shape[0]
    own = TokenGather(place, buf.at[0], k.own_gather)
    quarter = own.rows(place.me)
    if sequences > 1:
        crossing = send(
            buf.at[0, quarter], buf.at[1, quarter], k.pair_send.at[0], k.pair_recv.at[0], place.partner()
        )
    own.start()
    k.at(point)
    for count, owner in enumerate(own.arrivals()):
        on_rows(0, own.rows(owner))
        if count == 1:
            k.at(point + 1)
    k.at(point + 2)
    if sequences > 1:
        crossing.wait_recv()
        other = TokenGather(place, buf.at[1], k.other_gather)
        other.start()
        between()
        k.at(point + 3)
        for owner in other.arrivals():
            on_rows(1, other.rows(owner))
        crossing.wait_send()
    else:
        between()
    k.at(point + 4)


def give_back(k, total):
    k.pair_sum[...] = total.astype(BF16)
    return send(k.pair_sum, k.pair_land, k.pair_send.at[1], k.pair_recv.at[1], k.place.partner())


def ffn_forward(k):
    sequences, length = k.kept[MOE].shape[:2]
    experts = k.kept[ROUTED].shape[0]
    place = k.place
    moe, branch = k.kept[MOE], k.branch
    k.early(SH, *(EX + e for e in range(experts)))
    moe[0, quarter_rows(length, place.me), :] = normalise(k.mid[...], k.gains[1:2, :]).astype(BF16)
    units = k.w[SH].shape[-1] // 3
    wide = k.w[EX].shape[-1] // 3

    def on_rows(s, rows):
        k.weight(SH)
        inner = nn(moe[s, rows, :], k.matrix(SH, 0, 2 * units))
        k.kept[SHARED][s, rows, :] = inner.astype(BF16)
        branch[s, rows, :] = nt(hidden_of(inner), k.matrix(SH, 2 * units, 3 * units))
        logits = nn(moe[s, rows, :], k.router[...])
        k.gates[s, rows, :] = pick_softmax(logits, k.chosen_cols[s, rows, :], 1)

    scatters = [TokenScatter(place, refs) for refs in k.scatters]

    def dispatch(s, e):
        index = s * experts + e
        for first, last in slot_halves():
            held = slots_by_token(k.slot_rows[index : index + 1, :], first, last).astype(F32).astype(BF16)
            k.kept[ROUTED][e, s * CAP + first : s * CAP + last, :] = nn(held, moe[s]).astype(BF16)

    def expert(s, e):
        k.weight(EX + e)
        index = s * experts + e
        for first, last in slot_halves():
            slots = slice(s * CAP + first, s * CAP + last)
            inner = nn(k.kept[ROUTED][e, slots, :], k.matrix(EX + e, 0, 2 * wide))
            k.kept[ACT][e, slots, :] = inner.astype(BF16)
            k.outs[first:last, :] = nt(hidden_of(inner), k.matrix(EX + e, 2 * wide, 3 * wide)).astype(BF16)
        if e < experts - 1:
            for first in range(0, length, length // 2):
                rows = slice(first, first + length // 2)
                combine = tokens_by_slot(k.slot_cols[rows, index : index + 1])
                branch[s, rows, :] += k.gates[s, rows, e : e + 1] * nn(combine, k.outs[...])
            return

        def block_of(owner):
            rows = quarter_rows(length, owner)
            combine = tokens_by_slot(k.slot_cols[rows, index : index + 1])
            return branch[s, rows, :] + k.gates[s, rows, e : e + 1] * nn(combine, k.outs[...])

        scatters[s].begin(block_of)

    order = expert_order(sequences, experts)

    def between():
        for e in range(experts):
            dispatch(0, e)
        k.gate_rows[0] = pick_softmax(nt(k.router_t[...], moe[0]), k.chosen_rows[0], 0)
        expert(*order[0])

    both_arrivals(k, moe, on_rows, between, 8)
    k.local.start(moe, k.kept_out[MOE], True)
    k.local.start(k.kept[SHARED], k.kept_out[SHARED], True)
    for step, (s, e) in enumerate(order[1:]):
        if s > 0:
            dispatch(s, e)
        expert(s, e)
        k.at(13 + step)
    for s in range(1, sequences):
        k.gate_rows[s] = pick_softmax(nt(k.router_t[...], moe[s]), k.chosen_rows[s], 0)
    k.local.start(k.kept[ROUTED], k.kept_out[ROUTED], True)
    k.local.start(k.kept[ACT], k.kept_out[ACT], True)
    if sequences > 1:
        returned = give_back(k, scatters[1].total())
    following = k.mid[...] + scatters[0].total()
    if sequences > 1:
        returned.wait_recv()
        following = following + k.pair_land[...].astype(F32)
        returned.wait_send()
    k.following[...] = following


def ffn_backward(k):
    sequences, length = k.kept[MOE].shape[:2]
    experts = k.kept_in[ROUTED].shape[0]
    place = k.place
    moe, up, moe_grad = k.kept[MOE], k.up, k.moe_grad
    routed, act, shared = k.kept[ROUTED], k.kept[ACT], k.kept[SHARED]
    load_shared = k.local.start(k.kept_in[SHARED], shared)
    load_upstream = k.local.start(k.upstream, k.grad)
    load_rows = k.local.start(k.mid, k.rows)
    k.early(SH, *(EX + e for e in range(experts)))

    def load_expert(e):
        return [k.local.start(k.kept_in[name].at[e], k.kept[name]) for name in (ACT, ROUTED)]

    loads = {0: load_expert(0)}
    load_moe = k.local.start(k.kept_in[MOE], moe)
    k.early(QKV, PRJ)
    load_upstream.wait()
    up[0, quarter_rows(length, place.me), :] = k.grad[...].astype(BF16)
    units = k.w[SH].shape[-1] // 3
    wide = k.w[EX].shape[-1] // 3
    fresh = {SH}

    def on_rows(s, rows):
        k.weight(SH)
        if SH in fresh:
            fresh.remove(SH)
            load_shared.wait()
        inner = shared[s, rows, :].astype(F32)
        k.hidden_all[s, rows, :] = hidden_of(inner)
        down = nn(up[s, rows, :], k.matrix(SH, 2 * units, 3 * units))
        inner_grad = swiglu_back(down, inner)
        shared[s, rows, :] = inner_grad
        moe_grad[s, rows, :] = nt(inner_grad, k.matrix(SH, 0, 2 * units))

    scatters = [TokenScatter(place, refs) for refs in k.scatters]
    for s in range(sequences):
        k.slot_sums[s] = jnp.zeros_like(k.slot_sums[s])
    done = [0] * experts

    def expert(s, e):
        k.weight(EX + e)
        index = s * experts + e
        holding = k.slot_rows[index : index + 1, :]
        gate_row = k.gate_rows[s, e : e + 1, :]
        token_dots = jnp.zeros((1, length), F32)
        for first, last in slot_halves():
            slots = slice(s * CAP + first, s * CAP + last)
            held = slots_by_token(holding, first, last)
            gate_slot = jnp.sum(jnp.where(held, gate_row, 0.0), axis=1, keepdims=True)
            arrived = nn(held.astype(F32).astype(BF16), up[s]).astype(BF16)
            k.slot_grad[slots, :] = (arrived.astype(F32) * gate_slot).astype(BF16)
            down = nn(arrived, k.matrix(EX + e, 2 * wide, 3 * wide))
            for copy in loads.pop(e, ()):
                copy.wait()
            inner = act[slots, :].astype(F32)
            hidden = hidden_of(inner)
            k.hidden[slots, :] = hidden
            slot_dot = jnp.sum(hidden.astype(F32) * down, axis=1, keepdims=True)
            token_dots += jnp.sum(jnp.where(held, slot_dot, 0.0), axis=0, keepdims=True)
            inner_grad = swiglu_back(down * gate_slot, inner)
            act[slots, :] = inner_grad
            k.outs[first:last, :] = nt(inner_grad, k.matrix(EX + e, 0, 2 * wide)).astype(BF16)
        k.slot_sums[s, e : e + 1, :] = token_dots
        if e < experts - 1:
            for first in range(0, length, length // 2):
                rows = slice(first, first + length // 2)
                combine = tokens_by_slot(k.slot_cols[rows, index : index + 1])
                moe_grad[s, rows, :] += nn(combine, k.outs[...])
        else:
            gates = k.gate_rows[s]
            pair = jnp.sum(gates, axis=0, keepdims=True)
            product = 0.5 * (pair * pair - jnp.sum(gates * gates, axis=0, keepdims=True))
            sums = k.slot_sums[s]
            logit_grad = k.chosen_rows[s] * product * (2.0 * sums - jnp.sum(sums, axis=0, keepdims=True))
            k.logit_grad[s] = logit_grad.astype(BF16)

            def block_of(owner):
                rows = quarter_rows(length, owner)
                combine = tokens_by_slot(k.slot_cols[rows, index : index + 1])
                turned = tn(k.logit_grad[s, :, rows], k.router_t[...])
                return moe_grad[s, rows, :] + nn(combine, k.outs[...]) + turned

            scatters[s].begin(block_of)
        done[e] += 1
        if done[e] == sequences:
            k.put_product(EX + e, 0, (routed, act, slice(None)))
            k.put_product(EX + e, 2 * wide, (k.slot_grad, k.hidden, slice(None)))
            k.made(EX + e)
            if e + 1 < experts:
                loads[e + 1] = load_expert(e + 1)

    order = expert_order(sequences, experts)
    both_arrivals(k, up, on_rows, lambda: expert(*order[0]), 1)
    load_moe.wait()
    every = range(sequences)
    k.put_product(SH, 0, *((moe.at[s], shared.at[s], slice(None)) for s in every))
    k.put_product(SH, 2 * units, *((up.at[s], k.hidden_all.at[s], slice(None)) for s in every))
    k.made(SH)
    k.at(6)
    for step, (s, e) in enumerate(order[1:]):
        expert(s, e)
        k.at(7 + step)
    k.router_grad[...] = sum(nn(k.logit_grad[s], moe[s]) for s in range(sequences))
    if sequences > 1:
        returned = give_back(k, scatters[1].total())
    total = scatters[0].total()
    if sequences > 1:
        returned.wait_recv()
        total = total + k.pair_land[...].astype(F32)
        returned.wait_send()
    load_rows.wait()
    inward, k.gain_ffn[...] = normalise_back(k.rows[...], k.gains[1:2, :], total)
    k.grad[...] += inward


def layer_forward(k):
    attention_forward(k)
    ffn_forward(k)


def layer_backward(k):
    ffn_backward(k)
    attention_backward(k)


def last_backward(k):
    layer_backward(k)
    place, stage = k.place, k.stage
    half = k.slot_rows.shape[0] // 2
    stage[0] = jnp.zeros_like(stage[0])
    for at, row in enumerate((k.gain_att, k.gain_ffn, *k.later[:2])):
        stage[0, at : at + 1, :] = row[...]
    for at, part in enumerate((k.router_grad, k.later[2])):
        first, second = part[:half, :], part[half : 2 * half, :]
        upper = place.half == 1
        stage[0, 8 * (at + 1) : 8 * (at + 1) + half, :] = jnp.where(upper, second, first)
        stage[0, 8 * (at + 1) + half : 8 * (at + 1) + 2 * half, :] = jnp.where(upper, first, second)
    partners = (place.member(place.core_peer), place.member(place.y_peer), place.beside())
    for step, partner in enumerate(partners):
        copy = send(stage.at[step], k.land.at[step], k.small_send.at[step], k.small_recv.at[step], partner)
        copy.wait_recv()
        stage[step + 1] = stage[step] + k.land[step]
        copy.wait_send()
    k.at(17)
    last = len(partners)
    copies = []
    for away in (1, 2, 3):
        copies.append(
            send(
                stage.at[last],
                k.rows_z.at[place.z],
                k.small_send.at[last + away - 1],
                k.small_recv.at[last + away - 1],
                place.beyond(away),
            )
        )
    k.rows_z[place.z] = stage[last]
    for copy in copies:
        copy.wait_recv()
    k.small_sum[...] = (k.rows_z[0] + k.rows_z[1]) + (k.rows_z[2] + k.rows_z[3])
    for copy in copies:
        copy.wait_send()


class Far:
    def __init__(self, array):
        self.array = array


class Out:
    def __init__(self, shape, kind=F32, far=False):
        self.shape, self.kind, self.far = shape, kind, far


class Store:
    def __init__(self, height, width, columns, parts, paired):
        self.height, self.width, self.columns, self.parts, self.paired = height, width, columns, parts, paired
        self.source, self.full = {}, {}
        self.z, self.x = {}, {}
        self.made, self.sums, self.totals = {}, {}, {}

    def keys(self, layer, matrix):
        return [(layer, matrix, part) for part in range(len(self.parts[matrix]))]

    def shape_of(self, matrix):
        if self.paired:
            return (4, 2, self.height, self.columns[matrix])
        return (1, 1, self.width, self.columns[matrix])


def is_leaf(value):
    return not isinstance(value, (dict, list))


def call(store, body, collective_id, ins, outs, scratch, layer, weights=(), made=(), plan=(), tokens=True):
    ins, outs, scratch = dict(ins), dict(outs), dict(scratch)
    dma, vmem = pltpu.SemaphoreType.DMA, pltpu.VMEM
    width = store.width
    starts = [(kind, key) for _, kind, key, *end in plan if not end]
    starts += [(SUM_X, (layer, matrix)) for matrix in made if (layer, matrix) in store.own_sums]
    keys = [[key for own, key in starts if own == kind] for kind in range(4)]
    keys_in = [key for matrix in weights for key in store.keys(layer, matrix)]
    ins["src"] = {key: Far(store.source[key[:2]]) for key in keys[GET_Z]}
    ins["full_in"] = {m: Far(store.full[layer, m]) for m in weights if not store.paired}
    ins["z_in"], ins["x_in"] = {}, {}
    if store.paired:
        wanted = set(keys_in) | set(keys[GET_X])
        ins["z_in"] = {key: Far(store.z[key]) for key in sorted(wanted - set(keys[GET_Z]))}
        ins["x_in"] = {key: Far(store.x[key]) for key in sorted(set(keys_in) - set(keys[GET_X]))}
    ins["made_in"] = {key: Far(store.made[key]) for key in keys[SUM_X] if key in store.made}
    ins["sums_in"] = {key: Far(store.sums[key]) for key in keys[SUM_Z] if key not in keys[SUM_X]}

    def part_shape(key):
        return (4, store.parts[key[1]][key[2]][1], store.columns[key[1]])

    def block_shape(key):
        return (4, store.height, store.columns[key[1]])

    outs["z_out"] = {key: Out(part_shape(key), BF16, True) for key in keys[GET_Z]}
    outs["x_out"] = {key: Out(part_shape(key), BF16, True) for key in keys[GET_X]}
    outs["sums_out"] = {key: Out(block_shape(key), BF16, True) for key in keys[SUM_X] if key not in keys[SUM_Z]}
    outs["totals"] = {key: [Out(block_shape(key)[1:], BF16)] * (1 if key[1] in (QKV, PRJ) else 2) for key in keys[SUM_Z]}
    outs["made_out"] = {
        m: Out(store.shape_of(m), BF16, True) for m in made if (layer, m) not in store.own_sums
    }
    scratch["w"] = {m: vmem(store.shape_of(m), BF16) for m in weights}
    scratch["sems"] = {
        GET_Z: {key: [dma((4,)), dma((4,)), dma((1,))] for key in keys[GET_Z]},
        GET_X: {key: [dma((1,)), dma((1,))] for key in keys[GET_X]},
        SUM_X: {key: [dma((1,)), dma((1,)), dma((2,))] for key in keys[SUM_X]},
        SUM_Z: {key: [dma((4,)), dma((4,)), dma((1,))] for key in keys[SUM_Z]},
    }
    scratch["blocks"] = {key: vmem(block_shape(key), BF16) for key in keys[SUM_X]}
    scratch["own"] = {key: vmem(block_shape(key), BF16) for key in keys[SUM_X] if key in store.made}
    scratch["lands"] = {key: vmem(block_shape(key), BF16) for key in keys[SUM_Z]}
    scratch["lsem"] = dma((2 * len(keys_in) + 20,))
    trees = [jax.tree.flatten(tree, is_leaf=is_leaf) for tree in (ins, outs, scratch)]
    (ins_flat, _), (outs_flat, outs_tree), (scratch_flat, _) = trees
    around = bool(starts)

    def kernel(*refs):
        k = types.SimpleNamespace()
        at = 0
        for flat, tree in trees:
            for name, value in jax.tree.unflatten(tree, refs[at : at + len(flat)]).items():
                setattr(k, name, value)
            at += len(flat)
        place = k.place = Place()
        k.local = Local(k.lsem)
        peers = place.greet_sequence() if tokens else []
        if around:
            peers += place.greet_all()
        elif store.paired:
            peers += [place.partner()]
        place.greet(peers)

        def job(kind, key):
            sems = k.sems[kind][key]
            if kind == GET_Z:
                return Straight(place, k.src[key], k.z_out[key], store.parts[key[1]][key[2]], sems)
            if kind == GET_X:
                source = k.z_out[key] if key in k.z_out else k.z_in[key]
                return Aside(place, source, k.x_out[key], sems)
            if kind == SUM_X:
                source = k.made_in[key] if key in k.made_in else k.w[key[1]]
                return AsideSum(place, source, k.own.get(key), k.blocks[key], k.sums_out.get(key), sems)
            source = k.blocks[key] if key in k.blocks else k.sums_in[key]
            return StraightSum(place, source, k.lands[key], k.totals[key], sems)

        running, ended = {}, set()

        def start(kind, key):
            running[kind, key] = job(kind, key)
            running[kind, key].start()

        def end(kind, key):
            if (kind, key) not in ended:
                ended.add((kind, key))
                running[kind, key].arrived()

        def at_point(point):
            for own, kind, key, *is_end in plan:
                if own == point:
                    (end if is_end else start)(kind, key)

        loads, loaded = {}, set()

        def parts_of(matrix):
            return [(key, *store.parts[matrix][key[2]]) for key in store.keys(layer, matrix)]

        def load_part(key, first, rows):
            w = k.w[key[1]]
            span = pl.ds(first, rows)
            for got, landed, kind, x in (
                (k.z_in, k.z_out, GET_Z, place.x),
                (k.x_in, k.x_out, GET_X, 1 - place.x),
            ):
                if key in landed:
                    end(kind, key)
                source = landed[key] if key in landed else got[key]
                loads.setdefault(key, []).append(k.local.start(source, w.at[:, x, span]))

        def early(*matrices):
            for matrix in matrices:
                if not store.paired:
                    loads[matrix] = [k.local.start(k.full_in[matrix], k.w[matrix])]
                    continue
                for key, first, rows in parts_of(matrix):
                    if key in k.z_in and key in k.x_in:
                        load_part(key, first, rows)

        def weight(matrix):
            if matrix in loaded:
                return
            loaded.add(matrix)
            if not store.paired:
                for copy in loads[matrix]:
                    copy.wait()
                return
            for key, first, rows in parts_of(matrix):
                if key not in loads:
                    load_part(key, first, rows)
            for key, *_ in parts_of(matrix):
                for copy in loads[key]:
                    copy.wait()

        def matrix_of(matrix, first, last):
            value = k.w[matrix][:, :, :, first:last]
            return value.reshape(width, last - first)

        def put_product(matrix, first, *pairs):
            ref, half = k.w[matrix], width // 2
            blocks = ref.shape[0] // 2
            for part in range(2):
                cut = slice(part * half, (part + 1) * half)
                value = sum(tn(left[:, cut], right[:, taken]) for left, right, taken in pairs).astype(BF16)
                count, columns = value.shape[1], slice(first, first + value.shape[1])
                if blocks:
                    shape = (blocks, *ref.shape[1:3], count)
                    ref[part * blocks : (part + 1) * blocks, :, :, columns] = value.reshape(shape)
                else:
                    ref[0, 0, part * half : (part + 1) * half, columns] = value

        def finished(matrix):
            if (layer, matrix) in k.blocks:
                start(SUM_X, (layer, matrix))
            else:
                k.local.start(k.w[matrix], k.made_out[matrix], True)

        k.at, k.early, k.weight, k.matrix, k.made = at_point, early, weight, matrix_of, finished
        k.put_product = put_product
        at_point(0)
        body(k)
        for kind, key in running:
            end(kind, key)
        for transfer in running.values():
            transfer.close()
        k.local.close()

    hbm, near = pl.BlockSpec(memory_space=pl.ANY), pl.BlockSpec(memory_space=pltpu.VMEM)
    results = pl.pallas_call(
        kernel,
        out_shape=[jax.ShapeDtypeStruct(out.shape, out.kind) for out in outs_flat],
        in_specs=[hbm if isinstance(value, Far) else near for value in ins_flat],
        out_specs=[hbm if out.far else near for out in outs_flat],
        scratch_shapes=scratch_flat,
        compiler_params=pltpu.CompilerParams(
            collective_id=collective_id, has_side_effects=True, vmem_limit_bytes=VMEM_LIMIT
        ),
    )(*[value.array if isinstance(value, Far) else value for value in ins_flat])
    result = types.SimpleNamespace(**jax.tree.unflatten(outs_tree, results))
    store.z |= result.z_out
    store.x |= result.x_out
    store.sums |= result.sums_out
    store.totals |= result.totals
    store.made |= {(layer, m): value for m, value in result.made_out.items()}
    return result


def forward_plan(store, layer, last):
    qkv, (prj,), (sh,) = (store.keys(layer, matrix) for matrix in (QKV, PRJ, SH))
    low, high = store.keys(layer, EX), store.keys(layer, EX + 1)

    def pass_on(point, *keys):
        return [step for key in keys for step in ((point, GET_Z, key, True), (point, GET_X, key))]

    if layer == 0:
        plan = [(0, GET_Z, key) for key in (*qkv, prj, sh, *low)]
        plan += pass_on(1, *qkv) + pass_on(2, prj) + pass_on(6, sh) + pass_on(7, low[0]) + pass_on(8, low[1])
        plan += [(8, GET_Z, key) for key in high] + pass_on(9, low[2])
    else:
        plan = [(0, GET_X, sh)] + [(0, GET_Z, key) for key in (*low, high[0])]
        plan += pass_on(3, low[0]) + pass_on(4, low[1]) + pass_on(7, low[2]) + pass_on(8, high[0])
        plan += [(8, GET_Z, key) for key in high[1:]]
    if layer < last:
        qkv, (prj,), (sh,) = (store.keys(layer + 1, matrix) for matrix in (QKV, PRJ, SH))
        plan += [(8, GET_Z, key) for key in (*qkv, prj, sh)] + pass_on(15, *qkv, prj)
    if layer == 0:
        plan += pass_on(11, high[0]) + pass_on(12, high[1]) + pass_on(13, high[2])
    else:
        plan += pass_on(11, high[1]) + pass_on(12, high[2])
    return plan


def on_device(
    ring, stream, cotangent, segments, expert_pick, slot_index, norm_gains,
    attention, projection, router, widening, narrowing, expansion, contraction,
):
    layers = attention.shape[0]
    segment = segments[0]
    length = segment.shape[0]
    all_experts = expansion.shape[1]
    width = stream.shape[1]
    quarter = stream.shape[0]
    wide = attention.shape[3]
    units = widening.shape[3]
    height = attention.shape[2]
    paired = ring == 8
    sequences = 2 if paired else 1
    experts = all_experts // sequences
    shared_units = units // sequences
    dp = lax.axis_index("dp")
    upper = (dp // 2) % 2 == 1

    halfway = HEAD // 2
    inverse = jnp.exp(jnp.arange(halfway, dtype=F32) * (-2.0 * math.log(10000.0) / HEAD))
    phases = jnp.arange(length, dtype=F32)[:, None] * inverse[None, :]
    cosine, sine = jnp.cos(phases), jnp.sin(phases)
    cosine = jnp.concatenate([cosine] * 4, axis=1)
    sine = jnp.concatenate([-sine, sine] * 2, axis=1)
    places = dict(cosine=cosine, sine=sine, seg_row=segment[None, :], seg_col=segment[:, None])

    def local_first(values, axis):
        if not paired:
            return values
        return jnp.where(upper, jnp.roll(values, -experts, axis), values)

    picks = jnp.concatenate([expert_pick, slot_index], axis=2)[:, None]
    if paired:
        swap = [(at, (at // 4) * 4 + (at % 4 + 2) % 4) for at in range(ring)]
        picks = jnp.concatenate([picks, lax.ppermute(picks, "dp", swap)], axis=1)
    expert_of, slot_of = picks[..., :2], picks[..., 2:]
    held = expert_of[..., None] == jnp.arange(all_experts, dtype=jnp.int32)
    slots = local_first(jnp.sum(jnp.where(held, slot_of[..., None] + 1, 0), axis=3) - 1, 3)
    chosen = local_first(jnp.any(held, axis=3).astype(F32), 3)
    slots = slots[..., :experts]
    slot_rows = jnp.swapaxes(slots, 2, 3).reshape(layers, sequences * experts, length)
    slot_cols = jnp.swapaxes(slots, 1, 2).reshape(layers, length, sequences * experts)
    chosen_cols = jnp.pad(chosen, ((0, 0), (0, 0), (0, 0), (0, LANES - all_experts)))
    chosen_rows = jnp.pad(jnp.swapaxes(chosen, 2, 3), ((0, 0), (0, 0), (0, 8 - all_experts), (0, 0)))
    router_own = local_first(router, 2)
    router_wide = jnp.pad(router_own, ((0, 0), (0, 0), (0, LANES - all_experts)))
    router_t = jnp.pad(jnp.swapaxes(router_own, 1, 2), ((0, 0), (0, 8 - all_experts), (0, 0)))

    projection_t = jnp.swapaxes(projection, 1, 2)
    narrowing_t = jnp.swapaxes(narrowing, 1, 2)
    contraction_t = jnp.swapaxes(contraction, 2, 3)
    columns = {QKV: 3 * wide, PRJ: wide, SH: 3 * shared_units} | {EX + e: 3 * units for e in range(experts)}
    parts = {matrix: [(0, height)] for matrix in columns}
    if paired:
        third = height // 3
        parts[QKV] = parts[EX] = [(at, third) for at in (0, third, 2 * third)]
        parts[EX + 1] = [(0, height // 2), (height // 2, third), (height // 2 + third, height - height // 2 - third)]
    store = Store(height, width, columns, parts, paired)
    for layer in range(layers):
        store.source[layer, QKV] = jnp.concatenate([*attention[layer]], axis=-1)
        store.source[layer, PRJ] = projection_t[layer]
        thirds = (widening[layer, 0], widening[layer, 1], narrowing_t[layer])
        whole = [
            jnp.concatenate([expansion[layer, e, 0], expansion[layer, e, 1], contraction_t[layer, e]], axis=-1)
            for e in range(all_experts)
        ]
        if paired:
            store.source[layer, SH] = jnp.stack(
                [
                    jnp.concatenate([third[:, a * shared_units : (a + 1) * shared_units] for third in thirds], axis=-1)
                    for a in range(2)
                ]
            )
            for e in range(experts):
                store.source[layer, EX + e] = jnp.stack([whole[e], whole[experts + e]])
        else:
            store.source[layer, SH] = jnp.concatenate(thirds, axis=-1)
            for e in range(experts):
                store.source[layer, EX + e] = whole[e]
    if not paired:
        store.full = {
            key: lax.all_gather(source, "dp", axis=0, tiled=True)[None, None] for key, source in store.source.items()
        }

    vmem = pltpu.VMEM
    token_scatter = scatter_scratch(length, width)
    pair_scratch = dict(scatters=[token_scatter] * sequences, own_gather=gather_scratch())
    if paired:
        pair_scratch |= dict(
            other_gather=gather_scratch(),
            pair_send=pltpu.SemaphoreType.DMA((2,)),
            pair_recv=pltpu.SemaphoreType.DMA((2,)),
            pair_sum=vmem((quarter, width), BF16),
            pair_land=vmem((quarter, width), BF16),
        )
    attention_shapes = {NRM: (length, width), TURNED: (length, 4 * wide)}
    ffn_shapes = {
        MOE: (sequences, length, width),
        SHARED: (sequences, length, 2 * shared_units),
        ROUTED: (experts, sequences * CAP, width),
        ACT: (experts, sequences * CAP, 2 * units),
    }
    ffn_matrices = [SH, *(EX + e for e in range(experts))]
    rows_out = Out((quarter, width))
    gain_out = Out((1, width))
    last = layers - 1

    def kept_scratch(shapes):
        return {name: vmem(shape, BF16) for name, shape in shapes.items()}

    def kept_outs(shapes):
        return {name: Out(shape, BF16, True) for name, shape in shapes.items()}

    store.own_sums = set()
    saved = []
    current = stream
    next_id = 0
    for layer in range(layers):
        result = call(
            store,
            layer_forward,
            next_id,
            dict(
                x=current,
                gains=norm_gains[layer],
                router=router_wide[layer],
                router_t=router_t[layer],
                slot_rows=slot_rows[layer],
                slot_cols=slot_cols[layer],
                chosen_rows=chosen_rows[layer],
                chosen_cols=chosen_cols[layer],
                **places,
            ),
            dict(
                mid=rows_out,
                following=rows_out,
                gate_rows=Out((sequences, 8, length)),
                kept_out=kept_outs(attention_shapes | ffn_shapes),
            ),
            dict(
                kept=kept_scratch(attention_shapes | ffn_shapes),
                branch=vmem((sequences, length, width), F32),
                outs=vmem((CAP, width), BF16),
                gates=vmem((sequences, length, LANES), F32),
                gather=gather_scratch(),
                scatter=token_scatter,
                **pair_scratch,
            ),
            layer,
            [QKV, PRJ, *ffn_matrices],
            plan=forward_plan(store, layer, last) if paired else (),
        )
        saved.append((current, result.mid, result.kept_out, result.gate_rows))
        current = result.following
        next_id += 1

    upstream = cotangent
    parts_small = [None] * layers
    for layer in reversed(range(layers)):
        x_in, mid, kept, gate_rows = saved[layer]
        plan = [
            (8, SUM_X, (layer, SH), True), (8, SUM_Z, (layer, SH)), (11, SUM_X, (layer, EX), True), (11, SUM_Z, (layer, EX))
        ]
        made = [SH, EX, EX + 1]
        if layer < last:
            above = [(layer + 1, PRJ), (layer + 1, QKV)]
            plan += [(0, SUM_X, key) for key in above] + [(1, SUM_Z, (layer + 1, EX + 1))]
            plan += [step for key in above for step in ((6, SUM_X, key, True), (6, SUM_Z, key))]
        finish = paired and layer == 0
        if finish:
            made += [PRJ, QKV]
            plan += [(15, SUM_X, (0, EX + 1), True), (15, SUM_Z, (0, EX + 1))]
            plan += [step for m in (PRJ, QKV) for step in ((17, SUM_X, (0, m), True), (17, SUM_Z, (0, m)))]
        store.own_sums = {(layer, matrix) for matrix in made} if paired else set()
        ins = dict(
            upstream=Far(upstream),
            x=Far(x_in),
            mid=Far(mid),
            gains=norm_gains[layer],
            router_t=router_t[layer],
            slot_rows=slot_rows[layer],
            slot_cols=slot_cols[layer],
            chosen_rows=chosen_rows[layer],
            gate_rows=gate_rows,
            kept_in={name: Far(array) for name, array in kept.items()},
            **places,
        )
        outs = dict(grad=rows_out, gain_att=gain_out, gain_ffn=gain_out, router_grad=Out((8, width)))
        work = dict(
            kept={
                MOE: vmem((sequences, length, width), BF16),
                SHARED: vmem((sequences, length, 2 * shared_units), BF16),
                ROUTED: vmem((sequences * CAP, width), BF16),
                ACT: vmem((sequences * CAP, 2 * units), BF16),
            },
            hidden_all=vmem((sequences, length, shared_units), BF16),
            hidden=vmem((sequences * CAP, units), BF16),
            slot_grad=vmem((sequences * CAP, width), BF16),
            moe_grad=vmem((sequences, length, width), F32),
            slot_sums=vmem((sequences, 8, length), F32),
            logit_grad=vmem((sequences, 8, length), BF16),
            up=vmem((sequences, length, width), BF16),
            rows=vmem((quarter, width), F32),
            outs=vmem((CAP, width), BF16),
            **pair_scratch,
        )
        if not paired:
            work |= dict(spare=vmem((2, length, width), BF16))
        if finish:
            rows = 8 * (1 + layers)
            ins |= dict(later=list(parts_small[last]))
            outs |= dict(small_sum=Out((rows, width)))
            work |= dict(
                stage=vmem((4, rows, width), F32),
                land=vmem((3, rows, width), F32),
                rows_z=vmem((4, rows, width), F32),
                small_send=pltpu.SemaphoreType.DMA((6,)),
                small_recv=pltpu.SemaphoreType.DMA((6,)),
            )
        result = call(
            store,
            last_backward if finish else layer_backward,
            next_id,
            ins,
            outs,
            work,
            layer,
            [QKV, PRJ, *ffn_matrices],
            [QKV, PRJ, *ffn_matrices],
            plan=plan if paired else (),
        )
        upstream = result.grad
        parts_small[layer] = (result.gain_att, result.gain_ffn, result.router_grad)
        next_id += 1

    if paired:
        gains_grad = result.small_sum[: 2 * layers].reshape(layers, 2, width)
        router_grad = result.small_sum[8:].reshape(layers, 8, width)[:, :all_experts]
    else:
        gains_grad, router_grad = lax.psum(
            (
                jnp.stack([jnp.concatenate(part[:2], axis=0) for part in parts_small]),
                jnp.stack([part[2][:all_experts] for part in parts_small]),
            ),
            ("dp", "tensor"),
        )
        store.totals = {
            key: [lax.psum_scatter(part[0, 0], "dp", scatter_dimension=0, tiled=True).astype(F32)]
            for key, part in store.made.items()
        }

    def split(pieces):
        mine, theirs = pieces
        return jnp.where(upper, theirs, mine), jnp.where(upper, mine, theirs)

    attention_grad, projection_grad, widening_grad, narrowing_grad, expansion_grad, contraction_grad = (
        [] for _ in range(6)
    )
    for layer in range(layers):
        totals = {matrix: [part.astype(F32) for part in store.totals[layer, matrix]] for matrix in columns}
        (whole,) = totals[QKV]
        attention_grad.append(jnp.stack([whole[:, n * wide : (n + 1) * wide] for n in range(3)]))
        projection_grad.append(totals[PRJ][0].T)
        if paired:
            halves = split(totals[SH])
            shared = [
                jnp.concatenate([half[:, n * shared_units : (n + 1) * shared_units] for half in halves], axis=1)
                for n in range(3)
            ]
            by_expert = [split(totals[EX + e]) for e in range(experts)]
            wholes = [by_expert[e][a] for a in range(2) for e in range(experts)]
        else:
            (whole,) = totals[SH]
            shared = [whole[:, n * units : (n + 1) * units] for n in range(3)]
            wholes = [totals[EX + e][0] for e in range(experts)]
        widening_grad.append(jnp.stack(shared[:2]))
        narrowing_grad.append(shared[2].T)
        expansion_grad.append(
            jnp.stack([jnp.stack([one[:, :units], one[:, units : 2 * units]]) for one in wholes])
        )
        contraction_grad.append(jnp.stack([one[:, 2 * units :].T for one in wholes]))
    return (
        current,
        upstream,
        gains_grad,
        jnp.stack(attention_grad),
        jnp.stack(projection_grad),
        jnp.swapaxes(router_grad, 1, 2),
        jnp.stack(widening_grad),
        jnp.stack(narrowing_grad),
        jnp.stack(expansion_grad),
        jnp.stack(contraction_grad),
    )


def solution(mesh):
    placed = (
        P(("dp", "tensor"), None),
        P(("dp", "tensor"), None),
        P("dp", None),
        P(None, "dp", None),
        P(None, "dp", None),
        P(),
        P(None, None, "dp", "tensor"),
        P(None, "tensor", "dp"),
        P(),
        P(None, None, "dp", "tensor"),
        P(None, "tensor", "dp"),
        P(None, None, None, "dp", "tensor"),
        P(None, None, "tensor", "dp"),
    )
    return jax.shard_map(
        functools.partial(on_device, mesh.shape["dp"]),
        mesh=mesh,
        in_specs=placed,
        out_specs=(
            P(("dp", "tensor"), None),
            P(("dp", "tensor"), None),
            P(),
            P(None, None, "dp", "tensor"),
            P(None, "tensor", "dp"),
            P(),
            P(None, None, "dp", "tensor"),
            P(None, "tensor", "dp"),
            P(None, None, None, "dp", "tensor"),
            P(None, None, "tensor", "dp"),
        ),
        check_vma=False,
    )
```

```python
import functools
import math
import types

import jax
import jax.numpy as jnp
import numpy as np
from jax import lax
from jax.experimental import pallas as pl
from jax.experimental.pallas import tpu as pltpu
from jax.sharding import PartitionSpec as P

HEAD = 64
CAP = 640
LANES = 128
BF16 = jnp.bfloat16
F32 = jnp.float32
QKV, PRJ, SH, EX = range(4)
NRM, TURNED, MOE, SHARED, ROUTED, ACT = range(6)
GET_Z, GET_X, SUM_X, SUM_Z = range(4)
VMEM_LIMIT = 63 * 1024 * 1024


def nn(left, right):
    return lax.dot_general(left, right, (((1,), (0,)), ((), ())), preferred_element_type=F32)


def nt(left, right):
    return lax.dot_general(left, right, (((1,), (1,)), ((), ())), preferred_element_type=F32)


def tn(left, right):
    return lax.dot_general(left, right, (((0,), (0,)), ((), ())), preferred_element_type=F32)


class Place:
    def __init__(self):
        self.dp = lax.axis_index("dp")
        self.me = lax.axis_index("tensor")
        core = lax.rem(self.me, 2)
        self.core_peer = self.me + 1 - 2 * core
        self.y_peer = lax.rem(self.me + 2, 4)
        self.far_peer = lax.rem(self.core_peer + 2, 4)
        self.z = lax.div(self.dp, 2)
        self.x = lax.rem(self.dp, 2)
        self.half = lax.rem(self.z, 2)

    def member(self, tensor):
        return (self.dp, tensor)

    def row(self, away, x):
        return lax.rem(self.z + away + 4, 4) * 2 + x

    def beyond(self, away):
        return (self.row(away, self.x), self.me)

    def beside(self):
        return (self.row(0, 1 - self.x), self.me)

    def partner(self):
        return ((self.z + 1 - 2 * self.half) * 2 + self.x, self.me)

    def greet(self, peers):
        barrier = pltpu.get_barrier_semaphore()
        for peer in peers:
            pl.semaphore_signal(barrier, inc=1, device_id=peer, device_id_type=pl.DeviceIdType.MESH)
        pl.semaphore_wait(barrier, len(peers))

    def greet_sequence(self):
        return [self.member(self.core_peer), self.member(self.y_peer)]

    def greet_all(self):
        return [self.beside(), self.beyond(1), self.beyond(2), self.beyond(3)]


def send(source, target, send_sem, recv_sem, device):
    copy = pltpu.make_async_remote_copy(
        src_ref=source,
        dst_ref=target,
        send_sem=send_sem,
        recv_sem=recv_sem,
        device_id=device,
        device_id_type=pl.DeviceIdType.MESH,
    )
    copy.start()
    return copy


class Local:
    def __init__(self, sems):
        self.sems, self.used, self.open = sems, 0, []

    def start(self, source, target, keep=False):
        copy = pltpu.make_async_copy(source, target, self.sems.at[self.used])
        self.used += 1
        copy.start()
        if keep:
            self.open.append(copy)
        return copy

    def close(self):
        for copy in self.open:
            copy.wait()


def quarter_rows(length, member):
    quarter = length // 4
    return pl.ds(pl.multiple_of(member * quarter, quarter), quarter)


class TokenGather:
    def __init__(self, place, buf, sems):
        self.place, self.buf = place, buf
        self.sems = (sems["send_sem"], sems["recv_sem"])

    def rows(self, member):
        return quarter_rows(self.buf.shape[0], member)

    def pass_on(self, owner, target, slot):
        block = self.buf.at[self.rows(owner)]
        return send(block, block, self.sems[0].at[slot], self.sems[1].at[slot], self.place.member(target))

    def start(self):
        place = self.place
        self.far = self.pass_on(place.me, place.y_peer, 1)
        self.near = self.pass_on(place.me, place.core_peer, 0)

    def arrivals(self):
        place = self.place
        yield place.me
        self.near.wait_recv()
        yield place.core_peer
        self.far.wait_recv()
        self.onward = self.pass_on(place.y_peer, place.core_peer, 2)
        yield place.y_peer
        self.onward.wait_recv()
        yield place.far_peer
        self.near.wait_send()
        self.far.wait_send()
        self.onward.wait_send()


class TokenScatter:
    def __init__(self, place, refs):
        self.place = place
        refs = types.SimpleNamespace(**refs)
        self.part, self.landing, self.summed, self.crossed = refs.part, refs.landing, refs.summed, refs.crossed
        self.sems = (refs.send_sem, refs.recv_sem)

    def push(self, source, target, slot, member):
        return send(source, target, self.sems[0].at[slot], self.sems[1].at[slot], self.place.member(member))

    def begin(self, block_of):
        place, part = self.place, self.part
        part[0] = block_of(place.far_peer).astype(BF16)
        self.first = self.push(part.at[0], self.landing.at[0], 0, place.core_peer)
        crossing = block_of(place.y_peer)
        self.first.wait_recv()
        self.summed[...] = (crossing + self.landing[0].astype(F32)).astype(BF16)
        self.across = self.push(self.summed, self.crossed, 1, place.y_peer)
        part[1] = block_of(place.core_peer).astype(BF16)
        self.second = self.push(part.at[1], self.landing.at[1], 2, place.core_peer)
        self.own = block_of(place.me)

    def total(self):
        self.second.wait_recv()
        own = self.own + self.landing[1].astype(F32)
        self.across.wait_recv()
        own = own + self.crossed[...].astype(F32)
        self.first.wait_send()
        self.second.wait_send()
        self.across.wait_send()
        return own


def scatter_scratch(length, width):
    quarter = length // 4
    return dict(
        part=pltpu.VMEM((2, quarter, width), BF16),
        landing=pltpu.VMEM((2, quarter, width), BF16),
        summed=pltpu.VMEM((quarter, width), BF16),
        crossed=pltpu.VMEM((quarter, width), BF16),
        send_sem=pltpu.SemaphoreType.DMA((3,)),
        recv_sem=pltpu.SemaphoreType.DMA((3,)),
    )


def gather_scratch():
    return dict(send_sem=pltpu.SemaphoreType.DMA((3,)), recv_sem=pltpu.SemaphoreType.DMA((3,)))


class Straight:
    def __init__(self, place, source, target, rows, sems):
        self.place, self.source, self.target, self.rows = place, source, target, rows
        self.send_sem, self.recv_sem, self.local_sem = sems

    def part_for(self, away):
        source = self.source
        if len(source.shape) == 3:
            source = source.at[lax.rem(self.place.z + away, 2)]
        return source.at[pl.ds(*self.rows)]

    def start(self):
        place, mine = self.place, self.target.at[self.place.z]
        self.own = pltpu.make_async_copy(self.part_for(0), mine, self.local_sem.at[0])
        self.own.start()
        self.copies = [
            send(self.part_for(away), mine, self.send_sem.at[away], self.recv_sem.at[away], place.beyond(away))
            for away in (2, 1, 3)
        ]

    def arrived(self):
        self.own.wait()
        for copy in self.copies:
            copy.wait_recv()

    def close(self):
        for copy in self.copies:
            copy.wait_send()


class Aside:
    def __init__(self, place, source, target, sems):
        self.place, self.source, self.target = place, source, target
        self.send_sem, self.recv_sem = sems

    def start(self):
        self.copy = send(
            self.source, self.target, self.send_sem.at[0], self.recv_sem.at[0], self.place.beside()
        )

    def arrived(self):
        self.copy.wait_recv()

    def close(self):
        self.copy.wait_send()


class AsideSum:
    def __init__(self, place, source, own, landing, out, onward, sems):
        self.place, self.source, self.own, self.landing = place, source, own, landing
        self.out, self.onward = out, onward
        self.send_sem, self.recv_sem, self.local_sem = sems
        self.left = [2, 1, 3, 0]

    def start(self):
        place = self.place
        self.copies = {}
        for away in self.left:
            at = lax.rem(place.z + away, 4)
            self.copies[away] = send(
                self.source.at[at, 1 - place.x],
                self.landing.at[at],
                self.send_sem.at[away],
                self.recv_sem.at[away],
                place.beside(),
            )
        self.load = None
        if self.own is not None:
            self.load = pltpu.make_async_copy(self.source.at[:, place.x], self.own, self.local_sem.at[0])
            self.load.start()

    def take(self, count):
        for away in self.left[:count]:
            at = lax.rem(self.place.z + away, 4)
            self.copies[away].wait_recv()
            if self.load is not None:
                self.load.wait()
                self.load = None
            own = self.source[at, self.place.x] if self.own is None else self.own[at]
            self.landing[at] = (own.astype(F32) + self.landing[at].astype(F32)).astype(BF16)
            if self.onward is not None:
                self.onward.push(away)
        self.left = self.left[count:]

    def arrived(self):
        self.take(len(self.left))
        if self.out is not None:
            self.store = pltpu.make_async_copy(self.landing, self.out, self.local_sem.at[1])
            self.store.start()

    def close(self):
        for copy in self.copies.values():
            copy.wait_send()
        if self.out is not None:
            self.store.wait()


class StraightSum:
    def __init__(self, place, source, landing, totals, sems):
        self.place, self.source, self.landing, self.totals = place, source, landing, totals
        self.send_sem, self.recv_sem, self.local_sem = sems
        self.copies = []

    def push(self, away):
        block = self.source.at[lax.rem(self.place.z + away, 4)]
        if away == 0:
            self.own = pltpu.make_async_copy(block, self.landing.at[0], self.local_sem.at[0])
            self.own.start()
            return
        sems = self.send_sem.at[away], self.recv_sem.at[away]
        self.copies.append(send(block, self.landing.at[away], *sems, self.place.beyond(away)))

    def start(self):
        for away in (2, 1, 3, 0):
            self.push(away)

    def arrived(self):
        for copy in self.copies:
            copy.wait_recv()
        self.own.wait()
        blocks = [self.landing[away].astype(F32) for away in range(4)]
        if len(self.totals) == 1:
            self.totals[0][...] = ((blocks[0] + blocks[2]) + (blocks[1] + blocks[3])).astype(BF16)
        else:
            self.totals[0][...] = (blocks[0] + blocks[2]).astype(BF16)
            self.totals[1][...] = (blocks[1] + blocks[3]).astype(BF16)

    def close(self):
        for copy in self.copies:
            copy.wait_send()


def normalise(values, gain):
    factor = lax.rsqrt(jnp.mean(values * values, axis=-1, keepdims=True) + 1e-06)
    return values * factor * gain


def normalise_back(values, gain, upstream):
    factor = lax.rsqrt(jnp.mean(values * values, axis=-1, keepdims=True) + 1e-06)
    scaled = upstream * gain
    inward = factor * scaled - values * factor * factor * factor * jnp.mean(
        scaled * values, axis=-1, keepdims=True
    )
    return inward, jnp.sum(upstream * values * factor, axis=0, keepdims=True)


def swap_halves(values):
    width = values.shape[1]
    lane = lax.broadcasted_iota(jnp.int32, values.shape, 1)
    return jnp.where(
        lax.rem(lane, HEAD) < HEAD // 2,
        pltpu.roll(values, width - HEAD // 2, 1),
        pltpu.roll(values, HEAD // 2, 1),
    )


def turn(values, cosine, sine):
    times = values.shape[1] // cosine.shape[1]
    return values * jnp.concatenate([cosine] * times, axis=1) + swap_halves(
        values
    ) * jnp.concatenate([sine] * times, axis=1)


def allowed_keys(seg_row, seg_col, offset):
    shape = (seg_col.shape[0], seg_row.shape[1])
    row_index = offset + lax.broadcasted_iota(jnp.int32, shape, 0)
    column_index = lax.broadcasted_iota(jnp.int32, shape, 1)
    return (column_index <= row_index) & (seg_row == seg_col)


def softmax_rows(query, keys, allowed):
    masked = jnp.where(allowed, nt(query, keys), -1e30)
    exponent = jnp.exp(masked - jnp.max(masked, axis=-1, keepdims=True))
    return exponent * (1.0 / jnp.sum(exponent, axis=-1, keepdims=True))


def sigmoid(values):
    return 1.0 / (1.0 + jnp.exp(-values))


def make_tables(k, forward):
    sequences = len(k.picks)
    experts, length = k.slot_rows.shape[0] // sequences, k.slot_rows.shape[1]
    count = sequences * experts
    total = k.router.shape[0]
    if k.exchange:
        k.picks_sent.wait()
        k.picks_out[...] = k.picks[1][...]
    first = experts * k.place.half if sequences > 1 else 0
    for s, picks in enumerate(k.picks):
        pick_a, pick_b, slot_a, slot_b = (picks[4 * k.layer + n : 4 * k.layer + n + 1, :] for n in range(4))
        rows = []
        for e in range(total):
            expert = lax.rem(e + first, total)
            by_a, by_b = pick_a == expert, pick_b == expert
            rows.append(jnp.where(by_a | by_b, 1.0, 0.0))
            if e < experts:
                k.slot_rows[s * experts + e : s * experts + e + 1, :] = jnp.where(
                    by_a, slot_a, jnp.where(by_b, slot_b, -1)
                )
        chosen = jnp.concatenate(rows + [jnp.zeros((8 - total, length), F32)], axis=0)
        k.chosen_rows[s] = chosen
        if forward:
            k.chosen_cols[s] = jnp.transpose(
                jnp.concatenate([chosen, jnp.zeros((LANES - 8, length), F32)], axis=0)
            )
    rows = [
        k.slot_rows[...].astype(F32),
        jnp.zeros((8 - count, length), F32),
        k.seg_row[...].astype(F32),
        jnp.zeros((LANES - 9, length), F32),
    ]
    k.columns[...] = jnp.transpose(jnp.concatenate(rows, axis=0)).astype(jnp.int32)
    router = k.router[...].astype(F32)
    if sequences > 1:
        turned = jnp.concatenate([router[experts:], router[:experts]], axis=0)
        router = jnp.where(k.place.half == 1, turned, router)
    k.router_rows[...] = jnp.zeros_like(k.router_rows)
    k.router_rows[0:8, :] = jnp.concatenate(
        [router, jnp.zeros((8 - total, router.shape[1]), F32)], axis=0
    ).astype(BF16)


def attention_forward(k):
    length = k.kept[TURNED].shape[0]
    wide = k.kept[TURNED].shape[1] // 4
    heads = wide // HEAD
    place = k.place
    normed, turned = k.kept[NRM], k.kept[TURNED]
    k.early(QKV, PRJ)
    gather = TokenGather(place, normed, k.gather)
    normed[gather.rows(place.me), :] = normalise(k.x[...], k.gains[0:1, :]).astype(BF16)
    gather.start()
    make_tables(k, True)
    k.at(1)
    k.weight(QKV)
    for owner in gather.arrivals():
        rows = gather.rows(owner)
        projected = nn(normed[rows, :], k.matrix(QKV, 0, 3 * wide))
        turned[rows, : 2 * wide] = turn(projected[:, : 2 * wide], k.cosine[rows, :], k.sine[rows, :]).astype(BF16)
        turned[rows, 2 * wide : 3 * wide] = projected[:, 2 * wide :].astype(BF16)
    k.local.start(normed, k.kept_out[NRM], True)
    k.at(2)
    block = 128
    for offset in range(0, length, block):
        extent = offset + block
        allowed = allowed_keys(k.seg_row[:, :extent], k.columns[offset:extent, 8:9], offset)
        for head in range(heads):
            first = head * HEAD
            query = turned[offset:extent, first : first + HEAD] * BF16(HEAD**-0.5)
            keys = turned[:extent, wide + first : wide + first + HEAD]
            values = turned[:extent, 2 * wide + first : 2 * wide + first + HEAD]
            probability = softmax_rows(query, keys, allowed).astype(BF16)
            turned[offset:extent, 3 * wide + first : 3 * wide + first + HEAD] = nn(probability, values).astype(BF16)
        if extent % 256 == 0:
            k.at(2 + extent // 256)
    k.local.start(turned, k.kept_out[TURNED], True)
    scatter = TokenScatter(place, k.scatter)
    k.weight(PRJ)
    scatter.begin(lambda owner: nt(turned[quarter_rows(length, owner), 3 * wide :], k.matrix(PRJ, 0, wide)))
    k.at(7)
    k.mid[...] = k.x[...] + scatter.total()


def attention_backward(k):
    sequences, length, width = k.up.shape
    wide = width // 4
    heads = wide // HEAD
    place = k.place
    up, normed = k.up.at[0], k.kept[MOE].at[0]
    turned, grads = (k.kept[MOE].at[1], k.up.at[1]) if sequences > 1 else (k.spare.at[0], k.spare.at[1])
    sums = k.moe_grad.at[0]
    load_turned = k.local.start(k.kept_in[TURNED], turned)
    load_normed = k.local.start(k.kept_in[NRM], normed)
    gather = TokenGather(place, up, k.own_gather)
    up[gather.rows(place.me), :] = k.grad[...].astype(BF16)
    load_rows = k.local.start(k.x, k.rows)
    gather.start()
    k.at(10)
    k.weight(QKV)
    k.weight(PRJ)
    sums[...] = jnp.zeros((length, width), F32)
    for owner in gather.arrivals():
        rows = gather.rows(owner)
        grads[rows, 3 * wide :] = nn(up[rows, :], k.matrix(PRJ, 0, wide)).astype(BF16)
    load_turned.wait()
    block = 128
    for offset in range(0, length, block):
        if offset % 256 == 0:
            k.at(11 + offset // 256)
        extent = offset + block
        allowed = allowed_keys(k.seg_row[:, :extent], k.columns[offset:extent, 8:9], offset)
        for head in range(heads):
            own, key, value, out = (slice(n * wide + head * HEAD, n * wide + (head + 1) * HEAD) for n in range(4))
            query = turned[offset:extent, own] * BF16(HEAD**-0.5)
            keys = turned[:extent, key]
            outer = grads[offset:extent, out]
            probability = softmax_rows(query, keys, allowed)
            inner = nt(outer, turned[:extent, value])
            score = probability * (inner - jnp.sum(probability * inner, axis=-1, keepdims=True))
            score = score.astype(BF16)
            sums[offset:extent, own] = nn(score, keys) * HEAD**-0.5
            sums[:extent, key] += tn(score, query)
            sums[:extent, value] += tn(probability.astype(BF16), outer)
    load_normed.wait()
    k.put_product(PRJ, 0, (up, turned, slice(3 * wide, 4 * wide)))
    k.made(PRJ)
    for offset in range(0, length, block):
        rows = slice(offset, offset + block)
        both = turn(sums[rows, : 2 * wide], k.cosine[rows, :], -k.sine[rows, :])
        grads[rows, : 2 * wide] = both.astype(BF16)
        grads[rows, 2 * wide : 3 * wide] = sums[rows, 2 * wide : 3 * wide].astype(BF16)
    scatter = TokenScatter(place, k.scatters[0])
    scatter.begin(lambda owner: nt(grads[quarter_rows(length, owner), : 3 * wide], k.matrix(QKV, 0, 3 * wide)))
    k.at(15)
    k.put_product(QKV, 0, (normed, grads, slice(0, 3 * wide)))
    k.made(QKV)
    k.at(16)
    load_rows.wait()
    inward, k.gain_att[...] = normalise_back(k.rows[...], k.gains[0:1, :], scatter.total())
    k.grad[...] += inward


def pick_softmax(logits, chosen, axis):
    highest = jnp.max(jnp.where(chosen > 0, logits, -1e30), axis=axis, keepdims=True)
    exponent = chosen * jnp.exp(jnp.where(chosen > 0, logits - highest, 0.0))
    return exponent / jnp.sum(exponent, axis=axis, keepdims=True)


def slot_halves():
    return [(0, CAP // 2), (CAP // 2, CAP)]


def slots_by_token(slot_row, first, last):
    shape = (last - first, slot_row.shape[1])
    return lax.broadcasted_iota(jnp.int32, shape, 0) == slot_row - first


def tokens_by_slot(slot_column):
    shape = (slot_column.shape[0], CAP)
    return (lax.broadcasted_iota(jnp.int32, shape, 1) == slot_column).astype(F32).astype(BF16)


def hidden_of(inner):
    units = inner.shape[1] // 2
    gate = inner[:, :units]
    return (gate * sigmoid(gate) * inner[:, units:]).astype(BF16)


def swiglu_back(down, inner):
    units = inner.shape[1] // 2
    gate, raised = inner[:, :units], inner[:, units:]
    squashed = sigmoid(gate)
    gate_grad = down * raised * squashed * (1.0 + gate * (1.0 - squashed))
    up_grad = down * gate * squashed
    return jnp.concatenate([gate_grad.astype(BF16), up_grad.astype(BF16)], axis=1)


def expert_order(sequences, experts):
    if sequences == 1:
        return [(0, e) for e in range(experts)]
    return [(0, 0), (1, 0), (1, 1), (0, 1)]


def both_arrivals(k, buf, on_rows, between, point):
    place = k.place
    sequences = buf.shape[0]
    own = TokenGather(place, buf.at[0], k.own_gather)
    quarter = own.rows(place.me)
    if sequences > 1:
        crossing = send(
            buf.at[0, quarter], buf.at[1, quarter], k.pair_send.at[0], k.pair_recv.at[0], place.partner()
        )
    own.start()
    k.at(point)
    for count, owner in enumerate(own.arrivals()):
        on_rows(0, own.rows(owner))
        if count == 1:
            k.at(point + 1)
    k.at(point + 2)
    if sequences > 1:
        crossing.wait_recv()
        other = TokenGather(place, buf.at[1], k.other_gather)
        other.start()
        between()
        k.at(point + 3)
        for owner in other.arrivals():
            on_rows(1, other.rows(owner))
        crossing.wait_send()
    else:
        between()
    k.at(point + 4)


def give_back(k, total):
    k.pair_sum[...] = total.astype(BF16)
    return send(k.pair_sum, k.pair_land, k.pair_send.at[1], k.pair_recv.at[1], k.place.partner())


def ffn_forward(k):
    sequences, length = k.kept[MOE].shape[:2]
    experts = k.kept[ROUTED].shape[0]
    place = k.place
    moe, branch = k.kept[MOE], k.branch
    k.early(SH, *(EX + e for e in range(experts)))
    moe[0, quarter_rows(length, place.me), :] = normalise(k.mid[...], k.gains[1:2, :]).astype(BF16)
    units = k.w[SH].shape[-1] // 3
    wide = k.w[EX].shape[-1] // 3

    def shared(s, rows):
        k.weight(SH)
        inner = nn(moe[s, rows, :], k.matrix(SH, 0, 2 * units))
        k.kept[SHARED][s, rows, :] = inner.astype(BF16)
        return nt(hidden_of(inner), k.matrix(SH, 2 * units, 3 * units))

    def on_rows(s, rows):
        if not k.shared_last:
            branch[s, rows, :] = shared(s, rows)
        logits = nt(moe[s, rows, :], k.router_rows[...])
        k.gates[s, rows, :] = pick_softmax(logits, k.chosen_cols[s, rows, :], 1)

    scatters = [TokenScatter(place, refs) for refs in k.scatters]

    def dispatch(s, e):
        index = s * experts + e
        for first, last in slot_halves():
            held = slots_by_token(k.slot_rows[index : index + 1, :], first, last).astype(F32).astype(BF16)
            k.kept[ROUTED][e, s * CAP + first : s * CAP + last, :] = nn(held, moe[s]).astype(BF16)

    def expert(s, e):
        k.weight(EX + e)
        index = s * experts + e
        for first, last in slot_halves():
            slots = slice(s * CAP + first, s * CAP + last)
            inner = nn(k.kept[ROUTED][e, slots, :], k.matrix(EX + e, 0, 2 * wide))
            k.kept[ACT][e, slots, :] = inner.astype(BF16)
            k.outs[first:last, :] = nt(hidden_of(inner), k.matrix(EX + e, 2 * wide, 3 * wide)).astype(BF16)
        if e < experts - 1 or k.shared_last:
            for first in range(0, length, length // 2):
                rows = slice(first, first + length // 2)
                combine = tokens_by_slot(k.columns[rows, index : index + 1])
                value = k.gates[s, rows, e : e + 1] * nn(combine, k.outs[...])
                branch[s, rows, :] = value if k.shared_last and e == 0 else branch[s, rows, :] + value
            return

        def block_of(owner):
            rows = quarter_rows(length, owner)
            combine = tokens_by_slot(k.columns[rows, index : index + 1])
            return branch[s, rows, :] + k.gates[s, rows, e : e + 1] * nn(combine, k.outs[...])

        scatters[s].begin(block_of)

    def shared_block(s, owner):
        rows = quarter_rows(length, owner)
        return branch[s, rows, :] + shared(s, rows)

    order = expert_order(sequences, experts)

    def between():
        for e in range(experts):
            dispatch(0, e)
        k.gate_rows[0] = pick_softmax(nt(k.router_rows[0:8, :], moe[0]), k.chosen_rows[0], 0)
        expert(*order[0])

    both_arrivals(k, moe, on_rows, between, 8)
    k.local.start(moe, k.kept_out[MOE], True)
    for step, (s, e) in enumerate(order[1:]):
        if s > 0:
            dispatch(s, e)
        expert(s, e)
        k.at(13 + step)
    if k.shared_last:
        for s in reversed(range(sequences)):
            scatters[s].begin(functools.partial(shared_block, s))
    k.local.start(k.kept[SHARED], k.kept_out[SHARED], True)
    for s in range(1, sequences):
        k.gate_rows[s] = pick_softmax(nt(k.router_rows[0:8, :], moe[s]), k.chosen_rows[s], 0)
    k.local.start(k.kept[ROUTED], k.kept_out[ROUTED], True)
    k.local.start(k.kept[ACT], k.kept_out[ACT], True)
    if sequences > 1:
        returned = give_back(k, scatters[1].total())
        k.at(16)
    following = k.mid[...] + scatters[0].total()
    if sequences > 1:
        returned.wait_recv()
        following = following + k.pair_land[...].astype(F32)
        returned.wait_send()
    k.following[...] = following


def ffn_backward(k):
    sequences, length = k.kept[MOE].shape[:2]
    experts = k.kept_in[ROUTED].shape[0]
    place = k.place
    moe, up, moe_grad = k.kept[MOE], k.up, k.moe_grad
    routed, act, shared = k.kept[ROUTED], k.kept[ACT], k.kept[SHARED]
    load_shared = k.local.start(k.kept_in[SHARED], shared)
    load_upstream = k.local.start(k.upstream, k.grad)
    load_rows = k.local.start(k.mid, k.rows)
    k.early(SH, *(EX + e for e in range(experts)))

    def load_expert(e):
        return [k.local.start(k.kept_in[name].at[e], k.kept[name]) for name in (ACT, ROUTED)]

    loads = {0: load_expert(0)}
    load_moe = k.local.start(k.kept_in[MOE], moe)
    k.early(QKV, PRJ)
    make_tables(k, False)
    load_upstream.wait()
    up[0, quarter_rows(length, place.me), :] = k.grad[...].astype(BF16)
    units = k.w[SH].shape[-1] // 3
    wide = k.w[EX].shape[-1] // 3
    fresh = {SH}

    def on_rows(s, rows):
        k.weight(SH)
        if SH in fresh:
            fresh.remove(SH)
            load_shared.wait()
        inner = shared[s, rows, :].astype(F32)
        k.hidden_all[s, rows, :] = hidden_of(inner)
        down = nn(up[s, rows, :], k.matrix(SH, 2 * units, 3 * units))
        inner_grad = swiglu_back(down, inner)
        shared[s, rows, :] = inner_grad
        moe_grad[s, rows, :] = nt(inner_grad, k.matrix(SH, 0, 2 * units))

    scatters = [TokenScatter(place, refs) for refs in k.scatters]
    for s in range(sequences):
        k.slot_sums[s] = jnp.zeros_like(k.slot_sums[s])
    done = [0] * experts

    def expert(s, e):
        k.weight(EX + e)
        index = s * experts + e
        holding = k.slot_rows[index : index + 1, :]
        gate_row = k.gate_rows[s, e : e + 1, :]
        token_dots = jnp.zeros((1, length), F32)
        for first, last in slot_halves():
            slots = slice(s * CAP + first, s * CAP + last)
            held = slots_by_token(holding, first, last)
            gate_slot = jnp.sum(jnp.where(held, gate_row, 0.0), axis=1, keepdims=True)
            arrived = nn(held.astype(F32).astype(BF16), up[s]).astype(BF16)
            k.slot_grad[slots, :] = (arrived.astype(F32) * gate_slot).astype(BF16)
            down = nn(arrived, k.matrix(EX + e, 2 * wide, 3 * wide))
            for copy in loads.pop(e, ()):
                copy.wait()
            inner = act[slots, :].astype(F32)
            hidden = hidden_of(inner)
            k.hidden[slots, :] = hidden
            slot_dot = jnp.sum(hidden.astype(F32) * down, axis=1, keepdims=True)
            token_dots += jnp.sum(jnp.where(held, slot_dot, 0.0), axis=0, keepdims=True)
            inner_grad = swiglu_back(down * gate_slot, inner)
            act[slots, :] = inner_grad
            k.outs[first:last, :] = nt(inner_grad, k.matrix(EX + e, 0, 2 * wide)).astype(BF16)
        k.slot_sums[s, e : e + 1, :] = token_dots
        if e < experts - 1:
            for first in range(0, length, length // 2):
                rows = slice(first, first + length // 2)
                combine = tokens_by_slot(k.columns[rows, index : index + 1])
                moe_grad[s, rows, :] += nn(combine, k.outs[...])
        else:
            gates = k.gate_rows[s]
            pair = jnp.sum(gates, axis=0, keepdims=True)
            product = 0.5 * (pair * pair - jnp.sum(gates * gates, axis=0, keepdims=True))
            sums = k.slot_sums[s]
            logit_grad = k.chosen_rows[s] * product * (2.0 * sums - jnp.sum(sums, axis=0, keepdims=True))
            k.logit_grad[s] = logit_grad.astype(BF16)

            def block_of(owner):
                rows = quarter_rows(length, owner)
                combine = tokens_by_slot(k.columns[rows, index : index + 1])
                turned = tn(k.logit_grad[s, :, rows], k.router_rows[0:8, :])
                return moe_grad[s, rows, :] + nn(combine, k.outs[...]) + turned

            scatters[s].begin(block_of)
        done[e] += 1
        if done[e] == sequences:
            k.put_product(EX + e, 0, (routed, act, slice(None)))
            k.put_product(EX + e, 2 * wide, (k.slot_grad, k.hidden, slice(None)))
            k.made(EX + e)
            if e + 1 < experts:
                loads[e + 1] = load_expert(e + 1)

    order = expert_order(sequences, experts)
    both_arrivals(k, up, on_rows, lambda: expert(*order[0]), 1)
    load_moe.wait()
    every = range(sequences)
    k.put_product(SH, 0, *((moe.at[s], shared.at[s], slice(None)) for s in every))
    k.put_product(SH, 2 * units, *((up.at[s], k.hidden_all.at[s], slice(None)) for s in every))
    k.made(SH)
    k.at(6)
    for step, (s, e) in enumerate(order[1:]):
        expert(s, e)
        k.at(7 + step)
    k.router_grad[...] = sum(nn(k.logit_grad[s], moe[s]) for s in range(sequences))
    if sequences > 1:
        returned = give_back(k, scatters[1].total())
    k.at(18)
    total = scatters[0].total()
    if sequences > 1:
        returned.wait_recv()
        total = total + k.pair_land[...].astype(F32)
        returned.wait_send()
    load_rows.wait()
    inward, k.gain_ffn[...] = normalise_back(k.rows[...], k.gains[1:2, :], total)
    k.grad[...] += inward


def layer_forward(k):
    attention_forward(k)
    ffn_forward(k)


def layer_backward(k):
    ffn_backward(k)
    attention_backward(k)


def last_backward(k):
    layer_backward(k)
    place, stage = k.place, k.stage
    half = k.slot_rows.shape[0] // 2
    stage[0] = jnp.zeros_like(stage[0])
    for at, row in enumerate((k.gain_att, k.gain_ffn, *k.later[:2])):
        stage[0, at : at + 1, :] = row[...]
    for at, part in enumerate((k.router_grad, k.later[2])):
        first, second = part[:half, :], part[half : 2 * half, :]
        upper = place.half == 1
        stage[0, 8 * (at + 1) : 8 * (at + 1) + half, :] = jnp.where(upper, second, first)
        stage[0, 8 * (at + 1) + half : 8 * (at + 1) + 2 * half, :] = jnp.where(upper, first, second)
    partners = (place.member(place.core_peer), place.member(place.y_peer), place.beside())
    for step, partner in enumerate(partners):
        copy = send(stage.at[step], k.land.at[step], k.small_send.at[step], k.small_recv.at[step], partner)
        copy.wait_recv()
        stage[step + 1] = stage[step] + k.land[step]
        copy.wait_send()
    k.at(17)
    last = len(partners)
    copies = []
    for away in (1, 2, 3):
        copies.append(
            send(
                stage.at[last],
                k.rows_z.at[place.z],
                k.small_send.at[last + away - 1],
                k.small_recv.at[last + away - 1],
                place.beyond(away),
            )
        )
    k.rows_z[place.z] = stage[last]
    for copy in copies:
        copy.wait_recv()
    k.small_sum[...] = (k.rows_z[0] + k.rows_z[1]) + (k.rows_z[2] + k.rows_z[3])
    for copy in copies:
        copy.wait_send()


class Far:
    def __init__(self, array):
        self.array = array


class Out:
    def __init__(self, shape, kind=F32, far=False):
        self.shape, self.kind, self.far = shape, kind, far


class Store:
    def __init__(self, height, width, columns, parts, paired):
        self.height, self.width, self.columns, self.parts, self.paired = height, width, columns, parts, paired
        self.source, self.full = {}, {}
        self.z, self.x = {}, {}
        self.made, self.sums, self.totals = {}, {}, {}
        self.own_sums, self.straight_on = set(), []

    def keys(self, layer, matrix):
        return [(layer, matrix, part) for part in range(len(self.parts[matrix]))]

    def shape_of(self, matrix):
        if self.paired:
            return (4, 2, self.height, self.columns[matrix])
        return (1, 1, self.width, self.columns[matrix])


def is_leaf(value):
    return not isinstance(value, (dict, list))


def call(store, body, collective_id, ins, outs, scratch, layer, weights=(), made=(), plan=(), tokens=True):
    ins, outs, scratch = dict(ins), dict(outs), dict(scratch)
    dma, vmem = pltpu.SemaphoreType.DMA, pltpu.VMEM
    width = store.width
    starts = [(kind, key) for _, kind, key, *taken in plan if not taken]
    starts += [(SUM_X, (layer, matrix)) for matrix in made if (layer, matrix) in store.own_sums]
    starts += [(SUM_Z, key) for key in store.straight_on]
    keys = [[key for own, key in starts if own == kind] for kind in range(4)]
    keys_in = [key for matrix in weights for key in store.keys(layer, matrix)]
    ins["src"] = {key: Far(store.source[key[:2]]) for key in keys[GET_Z]}
    ins["full_in"] = {m: Far(store.full[layer, m]) for m in weights if not store.paired}
    ins["z_in"], ins["x_in"] = {}, {}
    if store.paired:
        wanted = set(keys_in) | set(keys[GET_X])
        ins["z_in"] = {key: Far(store.z[key]) for key in sorted(wanted - set(keys[GET_Z]))}
        ins["x_in"] = {key: Far(store.x[key]) for key in sorted(set(keys_in) - set(keys[GET_X]))}
    ins["made_in"] = {key: Far(store.made[key]) for key in keys[SUM_X] if key in store.made}
    ins["sums_in"] = {key: Far(store.sums[key]) for key in keys[SUM_Z] if key not in keys[SUM_X]}

    def part_shape(key):
        return (4, store.parts[key[1]][key[2]][1], store.columns[key[1]])

    def block_shape(key):
        return (4, store.height, store.columns[key[1]])

    outs["z_out"] = {key: Out(part_shape(key), BF16, True) for key in keys[GET_Z]}
    outs["x_out"] = {key: Out(part_shape(key), BF16, True) for key in keys[GET_X]}
    outs["sums_out"] = {key: Out(block_shape(key), BF16, True) for key in keys[SUM_X] if key not in keys[SUM_Z]}
    outs["totals"] = {key: [Out(block_shape(key)[1:], BF16)] * (1 if key[1] in (QKV, PRJ) else 2) for key in keys[SUM_Z]}
    outs["made_out"] = {
        m: Out(store.shape_of(m), BF16, True) for m in made if (layer, m) not in store.own_sums
    }
    scratch["w"] = {m: vmem(store.shape_of(m), BF16) for m in weights}
    scratch["sems"] = {
        GET_Z: {key: [dma((4,)), dma((4,)), dma((1,))] for key in keys[GET_Z]},
        GET_X: {key: [dma((1,)), dma((1,))] for key in keys[GET_X]},
        SUM_X: {key: [dma((4,)), dma((4,)), dma((2,))] for key in keys[SUM_X]},
        SUM_Z: {key: [dma((4,)), dma((4,)), dma((1,))] for key in keys[SUM_Z]},
    }
    scratch["blocks"] = {key: vmem(block_shape(key), BF16) for key in keys[SUM_X]}
    scratch["own"] = {key: vmem(block_shape(key), BF16) for key in keys[SUM_X] if key in store.made}
    scratch["lands"] = {key: vmem(block_shape(key), BF16) for key in keys[SUM_Z]}
    scratch["lsem"] = dma((2 * len(keys_in) + 20,))
    trees = [jax.tree.flatten(tree, is_leaf=is_leaf) for tree in (ins, outs, scratch)]
    (ins_flat, _), (outs_flat, outs_tree), (scratch_flat, _) = trees
    around = bool(starts)

    def kernel(*refs):
        k = types.SimpleNamespace()
        at = 0
        for flat, tree in trees:
            for name, value in jax.tree.unflatten(tree, refs[at : at + len(flat)]).items():
                setattr(k, name, value)
            at += len(flat)
        place = k.place = Place()
        k.local = Local(k.lsem)
        k.layer = layer
        k.shared_last = store.paired and layer == 0
        peers = place.greet_sequence() if tokens else []
        if around:
            peers += place.greet_all()
        elif store.paired:
            peers += [place.partner()]
        place.greet(peers)
        k.exchange = hasattr(k, "news")
        if k.exchange:
            k.picks_sent = send(k.picks[0], k.news, k.news_send.at[0], k.news_recv.at[0], place.partner())
            k.picks = [k.picks[0], k.news]

        def job(kind, key):
            sems = k.sems[kind][key]
            if kind == GET_Z:
                return Straight(place, k.src[key], k.z_out[key], store.parts[key[1]][key[2]], sems)
            if kind == GET_X:
                source = k.z_out[key] if key in k.z_out else k.z_in[key]
                return Aside(place, source, k.x_out[key], sems)
            if kind == SUM_X:
                source = k.made_in[key] if key in k.made_in else k.w[key[1]]
                onward = None
                if key in k.lands:
                    onward = running[SUM_Z, key] = job(SUM_Z, key)
                return AsideSum(place, source, k.own.get(key), k.blocks[key], k.sums_out.get(key), onward, sems)
            source = k.blocks[key] if key in k.blocks else k.sums_in[key]
            return StraightSum(place, source, k.lands[key], k.totals[key], sems)

        running, ended = {}, set()

        def start(kind, key):
            transfer = running[kind, key] = job(kind, key)
            transfer.start()

        def end(kind, key):
            if (kind, key) not in ended:
                ended.add((kind, key))
                running[kind, key].arrived()

        def at_point(point):
            for own, kind, key, *taken in plan:
                if own != point:
                    continue
                if kind == SUM_X and taken:
                    running[kind, key].take(*taken)
                else:
                    (end if taken else start)(kind, key)

        loads, loaded = {}, set()

        def parts_of(matrix):
            return [(key, *store.parts[matrix][key[2]]) for key in store.keys(layer, matrix)]

        def load_part(key, first, rows):
            w = k.w[key[1]]
            span = pl.ds(first, rows)
            for got, landed, kind, x in (
                (k.z_in, k.z_out, GET_Z, place.x),
                (k.x_in, k.x_out, GET_X, 1 - place.x),
            ):
                if key in landed:
                    end(kind, key)
                source = landed[key] if key in landed else got[key]
                loads.setdefault(key, []).append(k.local.start(source, w.at[:, x, span]))

        def early(*matrices):
            for matrix in matrices:
                if not store.paired:
                    loads[matrix] = [k.local.start(k.full_in[matrix], k.w[matrix])]
                    continue
                for key, first, rows in parts_of(matrix):
                    if key in k.z_in and key in k.x_in:
                        load_part(key, first, rows)

        def weight(matrix):
            if matrix in loaded:
                return
            loaded.add(matrix)
            if not store.paired:
                for copy in loads[matrix]:
                    copy.wait()
                return
            for key, first, rows in parts_of(matrix):
                if key not in loads:
                    load_part(key, first, rows)
            for key, *_ in parts_of(matrix):
                for copy in loads[key]:
                    copy.wait()

        def matrix_of(matrix, first, last):
            value = k.w[matrix][:, :, :, first:last]
            return value.reshape(width, last - first)

        def put_product(matrix, first, *pairs):
            ref, half = k.w[matrix], width // 2
            blocks = ref.shape[0] // 2
            for part in range(2):
                cut = slice(part * half, (part + 1) * half)
                value = sum(tn(left[:, cut], right[:, taken]) for left, right, taken in pairs).astype(BF16)
                count, columns = value.shape[1], slice(first, first + value.shape[1])
                if blocks:
                    shape = (blocks, *ref.shape[1:3], count)
                    ref[part * blocks : (part + 1) * blocks, :, :, columns] = value.reshape(shape)
                else:
                    ref[0, 0, part * half : (part + 1) * half, columns] = value

        def finished(matrix):
            if (layer, matrix) in k.blocks:
                start(SUM_X, (layer, matrix))
            else:
                k.local.start(k.w[matrix], k.made_out[matrix], True)

        k.at, k.early, k.weight, k.matrix, k.made = at_point, early, weight, matrix_of, finished
        k.put_product = put_product
        at_point(0)
        body(k)
        for kind, key in sorted(running):
            end(kind, key)
        for transfer in running.values():
            transfer.close()
        k.local.close()

    hbm, near = pl.BlockSpec(memory_space=pl.ANY), pl.BlockSpec(memory_space=pltpu.VMEM)
    results = pl.pallas_call(
        kernel,
        out_shape=[jax.ShapeDtypeStruct(out.shape, out.kind) for out in outs_flat],
        in_specs=[hbm if isinstance(value, Far) else near for value in ins_flat],
        out_specs=[hbm if out.far else near for out in outs_flat],
        scratch_shapes=scratch_flat,
        compiler_params=pltpu.CompilerParams(
            collective_id=collective_id, has_side_effects=True, vmem_limit_bytes=VMEM_LIMIT
        ),
    )(*[value.array if isinstance(value, Far) else value for value in ins_flat])
    result = types.SimpleNamespace(**jax.tree.unflatten(outs_tree, results))
    store.z |= result.z_out
    store.x |= result.x_out
    store.sums |= result.sums_out
    store.totals |= result.totals
    store.made |= {(layer, m): value for m, value in result.made_out.items()}
    return result


def plain(body, outs, *arrays):
    near = pl.BlockSpec(memory_space=pltpu.VMEM)
    return pl.pallas_call(
        body,
        out_shape=[jax.ShapeDtypeStruct(out.shape, out.kind) for out in outs],
        in_specs=[near] * len(arrays),
        out_specs=[near] * len(outs),
        compiler_params=pltpu.CompilerParams(vmem_limit_bytes=VMEM_LIMIT),
    )(*arrays)


def turned_over(value):
    return jnp.transpose(value.astype(F32))


def pack_all(attention, projection, widening, narrowing, expansion, contraction, experts, shared_units):
    layers, _, height, wide = attention.shape
    units = widening.shape[3]
    keys, outs = [], []
    for layer in range(layers):
        shapes = {QKV: (height, 3 * wide), PRJ: (height, wide), SH: (2, height, 3 * shared_units)}
        shapes |= {EX + e: (2, height, 3 * units) for e in range(experts)}
        keys += [(layer, matrix) for matrix in shapes]
        outs += [Out(shape, BF16) for shape in shapes.values()]

    def body(att, prj, wid, nar, exp, con, *results):
        results = dict(zip(keys, results, strict=True))
        for layer in range(layers):
            for n in range(3):
                results[layer, QKV][:, n * wide : (n + 1) * wide] = att[layer, n]
            results[layer, PRJ][...] = turned_over(prj[layer]).astype(BF16)
            for half in range(2):
                cut = slice(half * shared_units, (half + 1) * shared_units)
                shared = results[layer, SH]
                shared[half, :, : 2 * shared_units] = jnp.concatenate([wid[layer, n, :, cut] for n in range(2)], axis=1)
                shared[half, :, 2 * shared_units :] = nar[layer, :, cut]
                for e in range(experts):
                    whole, given = results[layer, EX + e], half * experts + e
                    for n in range(2):
                        whole[half, :, n * units : (n + 1) * units] = exp[layer, given, n]
                    whole[half, :, 2 * units :] = con[layer, given]

    narrowing, contraction = jnp.swapaxes(narrowing, 1, 2), jnp.swapaxes(contraction, 2, 3)
    results = plain(body, outs, attention, projection, widening, narrowing, expansion, contraction)
    return dict(zip(keys, results, strict=True))


def unpack_all(current, upstream, small, totals, layers, all_experts, experts, shared_units, units, wide):
    width = current.shape[1]
    height = totals[0, QKV][0].shape[0]
    keys = sorted(totals)
    counts = [len(totals[key]) for key in keys]
    outs = [
        Out(current.shape),
        Out(upstream.shape),
        Out((layers, 2, width)),
        Out((layers, 3, height, wide)),
        Out((layers, wide, height)),
        Out((layers, all_experts, width)),
        Out((layers, 2, height, units)),
        Out((layers, height, units)),
        Out((layers, all_experts, 2, height, units)),
        Out((layers, all_experts, height, units)),
    ]

    def body(*refs):
        now, up, sums = refs[:3]
        parts, at = {}, 3
        for key, count in zip(keys, counts, strict=True):
            parts[key] = refs[at : at + count]
            at += count
        now_out, up_out, gains, att, prj, router, wid, nar, exp, con = refs[at:]
        upper = Place().half == 1
        now_out[...] = now[...]
        up_out[...] = up[...]

        def halves(key):
            mine, theirs = (part[...].astype(F32) for part in parts[key])
            return jnp.where(upper, theirs, mine), jnp.where(upper, mine, theirs)

        for layer in range(layers):
            gains[layer] = sums[2 * layer : 2 * layer + 2, :]
            router[layer] = sums[8 * layer + 8 : 8 * layer + 8 + all_experts, :]
            whole = parts[layer, QKV][0]
            for n in range(3):
                att[layer, n] = whole[:, n * wide : (n + 1) * wide].astype(F32)
            prj[layer] = turned_over(parts[layer, PRJ][0][...])
            for half, value in enumerate(halves((layer, SH))):
                cut = slice(half * shared_units, (half + 1) * shared_units)
                for n in range(2):
                    wid[layer, n, :, cut] = value[:, n * shared_units : (n + 1) * shared_units]
                nar[layer, :, cut] = value[:, 2 * shared_units :]
            for e in range(experts):
                for half, value in enumerate(halves((layer, EX + e))):
                    for n in range(2):
                        exp[layer, half * experts + e, n] = value[:, n * units : (n + 1) * units]
                    con[layer, half * experts + e] = value[:, 2 * units :]

    arrays = [current, upstream, small, *(part for key in keys for part in totals[key])]
    now, up, gains, att, prj, router, wid, nar, exp, con = plain(body, outs, *arrays)
    return now, up, gains, att, prj, jnp.swapaxes(router, 1, 2), wid, jnp.swapaxes(nar, 1, 2), exp, jnp.swapaxes(con, 2, 3)


def forward_plan(store, layer, last):
    qkv, (prj,), sh = (store.keys(layer, matrix) for matrix in (QKV, PRJ, SH))
    low, high = store.keys(layer, EX), store.keys(layer, EX + 1)

    def pass_on(point, *keys):
        return [step for key in keys for step in ((point, GET_Z, key, True), (point, GET_X, key))]

    if layer == 0:
        plan = [(0, GET_Z, key) for key in (*qkv, prj, *low)]
        plan += pass_on(1, *qkv) + pass_on(2, prj) + [(2, GET_Z, high[0])]
        plan += pass_on(5, low[0]) + pass_on(7, low[1]) + pass_on(8, low[2])
        plan += [(8, GET_Z, key) for key in (*high[1:], *sh)]
        plan += pass_on(9, high[0]) + pass_on(11, high[1]) + pass_on(12, high[2]) + pass_on(13, sh[0]) + pass_on(14, sh[1])
    else:
        plan = [(0, GET_X, low[0])] + [(0, GET_Z, key) for key in (*low[1:], *high)]
        plan += pass_on(2, low[1]) + pass_on(4, low[2]) + pass_on(7, high[0]) + pass_on(8, high[1]) + pass_on(9, high[2])
    if layer < last:
        qkv, (prj,), sh = (store.keys(layer + 1, matrix) for matrix in (QKV, PRJ, SH))
        early = store.keys(layer + 1, EX)[0]
        plan += [(8, GET_Z, key) for key in (*qkv, prj, *sh)] + [(12, GET_Z, early)]
        plan += pass_on(15, *qkv, prj) + pass_on(16, *sh)
    return plan


def backward_plan(layer, last):
    sh, low, high, prj, qkv = ((layer, matrix) for matrix in (SH, EX, EX + 1, PRJ, QKV))
    plan = [(7, SUM_X, sh, 2), (8, SUM_X, sh, 2), (18, SUM_X, low, 2), (10, SUM_X, low, 1), (11, SUM_X, low, 1)]
    own, onward = [sh, low, high], [sh, low]
    if layer < last:
        above = [(layer + 1, PRJ), (layer + 1, QKV)]
        plan += [(0, SUM_X, key) for key in above] + [(1, SUM_Z, (layer + 1, EX + 1))]
        plan += [(6, SUM_X, key, 4) for key in above]
        onward += above
    if layer == 0:
        plan += [(12, SUM_X, high, 1), (14, SUM_X, high, 1), (15, SUM_X, high, 2), (16, SUM_X, prj, 4)]
        plan += [(17, SUM_X, qkv, 4)]
        own, onward = [*own, prj, qkv], [*onward, high, prj, qkv]
    return plan, own, onward


def on_device(
    ring, stream, cotangent, segments, expert_pick, slot_index, norm_gains,
    attention, projection, router, widening, narrowing, expansion, contraction,
):
    layers = attention.shape[0]
    segment = segments[0]
    length = segment.shape[0]
    all_experts = expansion.shape[1]
    width = stream.shape[1]
    quarter = stream.shape[0]
    wide = attention.shape[3]
    units = widening.shape[3]
    height = attention.shape[2]
    paired = ring == 8
    sequences = 2 if paired else 1
    experts = all_experts // sequences
    shared_units = units // sequences
    inverse = np.exp(np.arange(HEAD // 2, dtype=np.float32) * np.float32(-2.0 * math.log(10000.0) / HEAD))
    phases = np.arange(length, dtype=np.float32)[:, None] * inverse[None, :]
    cosine, sine = np.cos(phases), np.sin(phases)
    places = dict(
        cosine=jnp.asarray(np.concatenate([cosine] * 4, axis=1)),
        sine=jnp.asarray(np.concatenate([-sine, sine] * 2, axis=1)),
        seg_row=segment[None, :],
    )
    picks = [jnp.swapaxes(jnp.concatenate([expert_pick, slot_index], axis=2), 1, 2).reshape(4 * layers, length)]
    router_rows = jnp.swapaxes(router, 1, 2)

    columns = {QKV: 3 * wide, PRJ: wide, SH: 3 * shared_units} | {EX + e: 3 * units for e in range(experts)}
    parts = {matrix: [(0, height)] for matrix in columns}
    if paired:
        third = height // 3
        parts[QKV] = parts[EX] = [(at, third) for at in (0, third, 2 * third)]
        parts[SH] = [(0, height // 2), (height // 2, height - height // 2)]
        parts[EX + 1] = [(0, height // 2), (height // 2, third), (height // 2 + third, height - height // 2 - third)]
    store = Store(height, width, columns, parts, paired)
    if paired:
        store.source = pack_all(
            attention, projection, widening, narrowing, expansion, contraction, experts, shared_units
        )
    else:
        whole = jnp.concatenate([expansion[:, :, 0], expansion[:, :, 1], jnp.swapaxes(contraction, 2, 3)], axis=-1)
        shared = jnp.concatenate([widening[:, 0], widening[:, 1], jnp.swapaxes(narrowing, 1, 2)], axis=-1)
        for layer in range(layers):
            store.source[layer, QKV] = jnp.concatenate([*attention[layer]], axis=-1)
            store.source[layer, PRJ] = projection[layer].T
            store.source[layer, SH] = shared[layer]
            for e in range(experts):
                store.source[layer, EX + e] = whole[layer, e]
    if not paired:
        store.full = {
            key: lax.all_gather(source, "dp", axis=0, tiled=True)[None, None] for key, source in store.source.items()
        }

    vmem = pltpu.VMEM
    token_scatter = scatter_scratch(length, width)
    pair_scratch = dict(scatters=[token_scatter] * sequences, own_gather=gather_scratch())
    if paired:
        pair_scratch |= dict(
            other_gather=gather_scratch(),
            pair_send=pltpu.SemaphoreType.DMA((2,)),
            pair_recv=pltpu.SemaphoreType.DMA((2,)),
            pair_sum=vmem((quarter, width), BF16),
            pair_land=vmem((quarter, width), BF16),
        )
    attention_shapes = {NRM: (length, width), TURNED: (length, 4 * wide)}
    ffn_shapes = {
        MOE: (sequences, length, width),
        SHARED: (sequences, length, 2 * shared_units),
        ROUTED: (experts, sequences * CAP, width),
        ACT: (experts, sequences * CAP, 2 * units),
    }
    ffn_matrices = [SH, *(EX + e for e in range(experts))]
    rows_out = Out((quarter, width))
    gain_out = Out((1, width))
    last = layers - 1

    def kept_scratch(shapes):
        return {name: vmem(shape, BF16) for name, shape in shapes.items()}

    def kept_outs(shapes):
        return {name: Out(shape, BF16, True) for name, shape in shapes.items()}

    tables = dict(
        slot_rows=vmem((sequences * experts, length), jnp.int32),
        chosen_rows=vmem((sequences, 8, length), F32),
        columns=vmem((length, LANES), jnp.int32),
        router_rows=vmem((LANES, width), BF16),
    )
    news = dict(
        news=vmem((4 * layers, length), jnp.int32),
        news_send=pltpu.SemaphoreType.DMA((1,)),
        news_recv=pltpu.SemaphoreType.DMA((1,)),
    )
    saved = []
    current = stream
    next_id = 0
    for layer in range(layers):
        result = call(
            store,
            layer_forward,
            next_id,
            dict(
                x=current,
                gains=norm_gains[layer],
                router=router_rows[layer],
                picks=picks,
                **places,
            ),
            dict(
                mid=rows_out,
                following=rows_out,
                gate_rows=Out((sequences, 8, length)),
                kept_out=kept_outs(attention_shapes | ffn_shapes),
                **(dict(picks_out=Out((4 * layers, length), jnp.int32)) if len(picks) < sequences else {}),
            ),
            dict(
                chosen_cols=vmem((sequences, length, LANES), F32),
                **tables,
                **(news if len(picks) < sequences else {}),
                kept=kept_scratch(attention_shapes | ffn_shapes),
                branch=vmem((sequences, length, width), F32),
                outs=vmem((CAP, width), BF16),
                gates=vmem((sequences, length, LANES), F32),
                gather=gather_scratch(),
                scatter=token_scatter,
                **pair_scratch,
            ),
            layer,
            [QKV, PRJ, *ffn_matrices],
            plan=forward_plan(store, layer, last) if paired else (),
        )
        if len(picks) < sequences:
            picks = [*picks, result.picks_out]
        saved.append((current, result.mid, result.kept_out, result.gate_rows))
        current = result.following
        next_id += 1

    upstream = cotangent
    parts_small = [None] * layers
    for layer in reversed(range(layers)):
        x_in, mid, kept, gate_rows = saved[layer]
        finish = paired and layer == 0
        plan, store.own_sums, store.straight_on = backward_plan(layer, last) if paired else ((), (), ())
        ins = dict(
            upstream=Far(upstream),
            x=Far(x_in),
            mid=Far(mid),
            gains=norm_gains[layer],
            router=router_rows[layer],
            picks=picks,
            gate_rows=gate_rows,
            kept_in={name: Far(array) for name, array in kept.items()},
            **places,
        )
        outs = dict(grad=rows_out, gain_att=gain_out, gain_ffn=gain_out, router_grad=Out((8, width)))
        work = dict(
            **tables,
            kept={
                MOE: vmem((sequences, length, width), BF16),
                SHARED: vmem((sequences, length, 2 * shared_units), BF16),
                ROUTED: vmem((sequences * CAP, width), BF16),
                ACT: vmem((sequences * CAP, 2 * units), BF16),
            },
            hidden_all=vmem((sequences, length, shared_units), BF16),
            hidden=vmem((sequences * CAP, units), BF16),
            slot_grad=vmem((sequences * CAP, width), BF16),
            moe_grad=vmem((sequences, length, width), F32),
            slot_sums=vmem((sequences, 8, length), F32),
            logit_grad=vmem((sequences, 8, length), BF16),
            up=vmem((sequences, length, width), BF16),
            rows=vmem((quarter, width), F32),
            outs=vmem((CAP, width), BF16),
            **pair_scratch,
        )
        if not paired:
            work |= dict(spare=vmem((2, length, width), BF16))
        if finish:
            rows = 8 * (1 + layers)
            ins |= dict(later=list(parts_small[last]))
            outs |= dict(small_sum=Out((rows, width)))
            work |= dict(
                stage=vmem((4, rows, width), F32),
                land=vmem((3, rows, width), F32),
                rows_z=vmem((4, rows, width), F32),
                small_send=pltpu.SemaphoreType.DMA((6,)),
                small_recv=pltpu.SemaphoreType.DMA((6,)),
            )
        result = call(
            store,
            last_backward if finish else layer_backward,
            next_id,
            ins,
            outs,
            work,
            layer,
            [QKV, PRJ, *ffn_matrices],
            [QKV, PRJ, *ffn_matrices],
            plan=plan if paired else (),
        )
        upstream = result.grad
        parts_small[layer] = (result.gain_att, result.gain_ffn, result.router_grad)
        next_id += 1

    if paired:
        return unpack_all(
            current, upstream, result.small_sum, store.totals, layers, all_experts, experts, shared_units, units, wide
        )
    gains_grad, router_grad = lax.psum(
        (
            jnp.stack([jnp.concatenate(part[:2], axis=0) for part in parts_small]),
            jnp.stack([part[2][:all_experts] for part in parts_small]),
        ),
        ("dp", "tensor"),
    )
    totals = {
        key: lax.psum_scatter(part[0, 0], "dp", scatter_dimension=0, tiled=True).astype(F32)
        for key, part in store.made.items()
    }
    att = jnp.stack([totals[layer, QKV] for layer in range(layers)])
    prj = jnp.stack([totals[layer, PRJ] for layer in range(layers)])
    shared = jnp.stack([totals[layer, SH] for layer in range(layers)])
    whole = jnp.stack([jnp.stack([totals[layer, EX + e] for e in range(experts)]) for layer in range(layers)])
    return (
        current,
        upstream,
        gains_grad,
        jnp.stack([att[..., n * wide : (n + 1) * wide] for n in range(3)], axis=1),
        jnp.swapaxes(prj, 1, 2),
        jnp.swapaxes(router_grad, 1, 2),
        jnp.stack([shared[..., n * units : (n + 1) * units] for n in range(2)], axis=1),
        jnp.swapaxes(shared[..., 2 * units :], 1, 2),
        jnp.stack([whole[..., n * units : (n + 1) * units] for n in range(2)], axis=2),
        jnp.swapaxes(whole[..., 2 * units :], 2, 3),
    )


def solution(mesh):
    placed = (
        P(("dp", "tensor"), None),
        P(("dp", "tensor"), None),
        P("dp", None),
        P(None, "dp", None),
        P(None, "dp", None),
        P(),
        P(None, None, "dp", "tensor"),
        P(None, "tensor", "dp"),
        P(),
        P(None, None, "dp", "tensor"),
        P(None, "tensor", "dp"),
        P(None, None, None, "dp", "tensor"),
        P(None, None, "tensor", "dp"),
    )
    return jax.shard_map(
        functools.partial(on_device, mesh.shape["dp"]),
        mesh=mesh,
        in_specs=placed,
        out_specs=(
            P(("dp", "tensor"), None),
            P(("dp", "tensor"), None),
            P(),
            P(None, None, "dp", "tensor"),
            P(None, "tensor", "dp"),
            P(),
            P(None, None, "dp", "tensor"),
            P(None, "tensor", "dp"),
            P(None, None, None, "dp", "tensor"),
            P(None, None, "tensor", "dp"),
        ),
        check_vma=False,
    )
```

```python
import functools
import math
import types

import jax
import jax.numpy as jnp
import numpy as np
from jax import lax
from jax.experimental import pallas as pl
from jax.experimental.pallas import tpu as pltpu
from jax.sharding import PartitionSpec as P

HEAD = 64
CAP = 640
LANES = 128
BF16 = jnp.bfloat16
F32 = jnp.float32
QKV, PRJ, SH, EX = range(4)
NRM, TURNED, MOE, SHARED, ROUTED, ACT = range(6)
GET_Z, GET_X, SUM_X, SUM_Z = range(4)
VMEM_LIMIT = 63 * 1024 * 1024


def nn(left, right):
    return lax.dot_general(left, right, (((1,), (0,)), ((), ())), preferred_element_type=F32)


def nt(left, right):
    return lax.dot_general(left, right, (((1,), (1,)), ((), ())), preferred_element_type=F32)


def tn(left, right):
    return lax.dot_general(left, right, (((0,), (0,)), ((), ())), preferred_element_type=F32)


class Place:
    def __init__(self):
        self.dp = lax.axis_index("dp")
        self.me = lax.axis_index("tensor")
        core = lax.rem(self.me, 2)
        self.core_peer = self.me + 1 - 2 * core
        self.y_peer = lax.rem(self.me + 2, 4)
        self.far_peer = lax.rem(self.core_peer + 2, 4)
        self.z = lax.div(self.dp, 2)
        self.x = lax.rem(self.dp, 2)
        self.half = lax.rem(self.z, 2)

    def member(self, tensor):
        return (self.dp, tensor)

    def row(self, away, x):
        return lax.rem(self.z + away + 4, 4) * 2 + x

    def beyond(self, away):
        return (self.row(away, self.x), self.me)

    def beside(self):
        return (self.row(0, 1 - self.x), self.me)

    def partner(self):
        return ((self.z + 1 - 2 * self.half) * 2 + self.x, self.me)

    def greet(self, peers):
        barrier = pltpu.get_barrier_semaphore()
        for peer in peers:
            pl.semaphore_signal(barrier, inc=1, device_id=peer, device_id_type=pl.DeviceIdType.MESH)
        pl.semaphore_wait(barrier, len(peers))

    def greet_sequence(self):
        return [self.member(self.core_peer), self.member(self.y_peer)]

    def greet_all(self):
        return [self.beside(), self.beyond(1), self.beyond(2), self.beyond(3)]


def send(source, target, send_sem, recv_sem, device):
    copy = pltpu.make_async_remote_copy(
        src_ref=source,
        dst_ref=target,
        send_sem=send_sem,
        recv_sem=recv_sem,
        device_id=device,
        device_id_type=pl.DeviceIdType.MESH,
    )
    copy.start()
    return copy


class Local:
    def __init__(self, sems):
        self.sems, self.used, self.open = sems, 0, []

    def start(self, source, target, keep=False):
        copy = pltpu.make_async_copy(source, target, self.sems.at[self.used])
        self.used += 1
        copy.start()
        if keep:
            self.open.append(copy)
        return copy

    def close(self):
        for copy in self.open:
            copy.wait()


def quarter_rows(length, member):
    quarter = length // 4
    return pl.ds(pl.multiple_of(member * quarter, quarter), quarter)


class TokenGather:
    def __init__(self, place, buf, sems):
        self.place, self.buf = place, buf
        self.sems = (sems["send_sem"], sems["recv_sem"])

    def rows(self, member):
        return quarter_rows(self.buf.shape[0], member)

    def pass_on(self, owner, target, slot):
        block = self.buf.at[self.rows(owner)]
        return send(block, block, self.sems[0].at[slot], self.sems[1].at[slot], self.place.member(target))

    def start(self):
        place = self.place
        self.far = self.pass_on(place.me, place.y_peer, 1)
        self.near = self.pass_on(place.me, place.core_peer, 0)

    def arrivals(self):
        place = self.place
        yield place.me
        self.near.wait_recv()
        yield place.core_peer
        self.far.wait_recv()
        self.onward = self.pass_on(place.y_peer, place.core_peer, 2)
        yield place.y_peer
        self.onward.wait_recv()
        yield place.far_peer
        self.near.wait_send()
        self.far.wait_send()
        self.onward.wait_send()


class TokenScatter:
    def __init__(self, place, refs):
        self.place = place
        refs = types.SimpleNamespace(**refs)
        self.part, self.landing, self.summed, self.crossed = refs.part, refs.landing, refs.summed, refs.crossed
        self.sems = (refs.send_sem, refs.recv_sem)

    def push(self, source, target, slot, member):
        return send(source, target, self.sems[0].at[slot], self.sems[1].at[slot], self.place.member(member))

    def begin(self, block_of):
        place, part = self.place, self.part
        part[0] = block_of(place.far_peer).astype(BF16)
        self.first = self.push(part.at[0], self.landing.at[0], 0, place.core_peer)
        crossing = block_of(place.y_peer)
        self.first.wait_recv()
        self.summed[...] = (crossing + self.landing[0].astype(F32)).astype(BF16)
        self.across = self.push(self.summed, self.crossed, 1, place.y_peer)
        part[1] = block_of(place.core_peer).astype(BF16)
        self.second = self.push(part.at[1], self.landing.at[1], 2, place.core_peer)
        self.own = block_of(place.me)

    def total(self):
        self.second.wait_recv()
        own = self.own + self.landing[1].astype(F32)
        self.across.wait_recv()
        own = own + self.crossed[...].astype(F32)
        self.first.wait_send()
        self.second.wait_send()
        self.across.wait_send()
        return own


def scatter_scratch(length, width):
    quarter = length // 4
    return dict(
        part=pltpu.VMEM((2, quarter, width), BF16),
        landing=pltpu.VMEM((2, quarter, width), BF16),
        summed=pltpu.VMEM((quarter, width), BF16),
        crossed=pltpu.VMEM((quarter, width), BF16),
        send_sem=pltpu.SemaphoreType.DMA((3,)),
        recv_sem=pltpu.SemaphoreType.DMA((3,)),
    )


def gather_scratch():
    return dict(send_sem=pltpu.SemaphoreType.DMA((3,)), recv_sem=pltpu.SemaphoreType.DMA((3,)))


class Straight:
    def __init__(self, place, source, target, rows, sems):
        self.place, self.source, self.target, self.rows = place, source, target, rows
        self.send_sem, self.recv_sem, self.local_sem = sems

    def part_for(self, away):
        source = self.source
        if len(source.shape) == 3:
            source = source.at[lax.rem(self.place.z + away, 2)]
        return source.at[pl.ds(*self.rows)]

    def start(self):
        place, mine = self.place, self.target.at[self.place.z]
        self.own = pltpu.make_async_copy(self.part_for(0), mine, self.local_sem.at[0])
        self.own.start()
        self.copies = [
            send(self.part_for(away), mine, self.send_sem.at[away], self.recv_sem.at[away], place.beyond(away))
            for away in (2, 1, 3)
        ]

    def arrived(self):
        self.own.wait()
        for copy in self.copies:
            copy.wait_recv()

    def close(self):
        for copy in self.copies:
            copy.wait_send()


class Aside:
    def __init__(self, place, source, target, sems):
        self.place, self.source, self.target = place, source, target
        self.send_sem, self.recv_sem = sems

    def start(self):
        self.copy = send(
            self.source, self.target, self.send_sem.at[0], self.recv_sem.at[0], self.place.beside()
        )

    def arrived(self):
        self.copy.wait_recv()

    def close(self):
        self.copy.wait_send()


class AsideSum:
    def __init__(self, place, source, own, landing, out, onward, sems):
        self.place, self.source, self.own, self.landing = place, source, own, landing
        self.out, self.onward = out, onward
        self.send_sem, self.recv_sem, self.local_sem = sems
        self.left = [2, 1, 3, 0]

    def start(self):
        place = self.place
        self.copies = {}
        for away in self.left:
            at = lax.rem(place.z + away, 4)
            self.copies[away] = send(
                self.source.at[at, 1 - place.x],
                self.landing.at[at],
                self.send_sem.at[away],
                self.recv_sem.at[away],
                place.beside(),
            )
        self.load = None
        if self.own is not None:
            self.load = pltpu.make_async_copy(self.source.at[:, place.x], self.own, self.local_sem.at[0])
            self.load.start()

    def take(self, count):
        for away in self.left[:count]:
            at = lax.rem(self.place.z + away, 4)
            self.copies[away].wait_recv()
            if self.load is not None:
                self.load.wait()
                self.load = None
            own = self.source[at, self.place.x] if self.own is None else self.own[at]
            self.landing[at] = (own.astype(F32) + self.landing[at].astype(F32)).astype(BF16)
            if self.onward is not None:
                self.onward.push(away)
        self.left = self.left[count:]

    def arrived(self):
        self.take(len(self.left))
        if self.out is not None:
            self.store = pltpu.make_async_copy(self.landing, self.out, self.local_sem.at[1])
            self.store.start()

    def close(self):
        for copy in self.copies.values():
            copy.wait_send()
        if self.out is not None:
            self.store.wait()


class StraightSum:
    def __init__(self, place, source, landing, totals, sems):
        self.place, self.source, self.landing, self.totals = place, source, landing, totals
        self.send_sem, self.recv_sem, self.local_sem = sems
        self.copies = []

    def push(self, away):
        block = self.source.at[lax.rem(self.place.z + away, 4)]
        if away == 0:
            self.own = pltpu.make_async_copy(block, self.landing.at[0], self.local_sem.at[0])
            self.own.start()
            return
        sems = self.send_sem.at[away], self.recv_sem.at[away]
        self.copies.append(send(block, self.landing.at[away], *sems, self.place.beyond(away)))

    def start(self):
        for away in (2, 1, 3, 0):
            self.push(away)

    def arrived(self):
        for copy in self.copies:
            copy.wait_recv()
        self.own.wait()
        blocks = [self.landing[away].astype(F32) for away in range(4)]
        if len(self.totals) == 1:
            self.totals[0][...] = ((blocks[0] + blocks[2]) + (blocks[1] + blocks[3])).astype(BF16)
        else:
            self.totals[0][...] = (blocks[0] + blocks[2]).astype(BF16)
            self.totals[1][...] = (blocks[1] + blocks[3]).astype(BF16)

    def close(self):
        for copy in self.copies:
            copy.wait_send()


def normalise(values, gain):
    factor = lax.rsqrt(jnp.mean(values * values, axis=-1, keepdims=True) + 1e-06)
    return values * factor * gain


def normalise_back(values, gain, upstream):
    factor = lax.rsqrt(jnp.mean(values * values, axis=-1, keepdims=True) + 1e-06)
    scaled = upstream * gain
    inward = factor * scaled - values * factor * factor * factor * jnp.mean(
        scaled * values, axis=-1, keepdims=True
    )
    return inward, jnp.sum(upstream * values * factor, axis=0, keepdims=True)


def swap_halves(values):
    width = values.shape[1]
    lane = lax.broadcasted_iota(jnp.int32, values.shape, 1)
    return jnp.where(
        lax.rem(lane, HEAD) < HEAD // 2,
        pltpu.roll(values, width - HEAD // 2, 1),
        pltpu.roll(values, HEAD // 2, 1),
    )


def turn(values, cosine, sine):
    times = values.shape[1] // cosine.shape[1]
    return values * jnp.concatenate([cosine] * times, axis=1) + swap_halves(
        values
    ) * jnp.concatenate([sine] * times, axis=1)


def allowed_keys(seg_row, seg_col, offset):
    shape = (seg_col.shape[0], seg_row.shape[1])
    row_index = offset + lax.broadcasted_iota(jnp.int32, shape, 0)
    column_index = lax.broadcasted_iota(jnp.int32, shape, 1)
    return (column_index <= row_index) & (seg_row == seg_col)


def softmax_rows(query, keys, allowed):
    masked = jnp.where(allowed, nt(query, keys), -1e30)
    exponent = jnp.exp(masked - jnp.max(masked, axis=-1, keepdims=True))
    return exponent * (1.0 / jnp.sum(exponent, axis=-1, keepdims=True))


def sigmoid(values):
    return 1.0 / (1.0 + jnp.exp(-values))


def make_tables(k, forward):
    sequences = len(k.picks)
    experts, length = k.slot_rows.shape[0] // sequences, k.slot_rows.shape[1]
    count = sequences * experts
    total = k.router.shape[0]
    if k.exchange and k.layer == 0:
        k.picks_sent.wait()
        k.picks_out[...] = k.picks[1][...]
    first = experts * k.place.half if sequences > 1 else 0
    for s, picks in enumerate(k.picks):
        pick_a, pick_b, slot_a, slot_b = (picks[4 * k.layer + n : 4 * k.layer + n + 1, :] for n in range(4))
        rows = []
        for e in range(total):
            expert = lax.rem(e + first, total)
            by_a, by_b = pick_a == expert, pick_b == expert
            rows.append(jnp.where(by_a | by_b, 1.0, 0.0))
            if e < experts:
                k.slot_rows[s * experts + e : s * experts + e + 1, :] = jnp.where(
                    by_a, slot_a, jnp.where(by_b, slot_b, -1)
                )
        chosen = jnp.concatenate(rows + [jnp.zeros((8 - total, length), F32)], axis=0)
        k.chosen_rows[s] = chosen
        if forward:
            k.chosen_cols[s] = jnp.transpose(
                jnp.concatenate([chosen, jnp.zeros((LANES - 8, length), F32)], axis=0)
            )
    rows = [
        k.slot_rows[...].astype(F32),
        jnp.zeros((8 - count, length), F32),
        k.seg_row[...].astype(F32),
        jnp.zeros((LANES - 9, length), F32),
    ]
    k.columns[...] = jnp.transpose(jnp.concatenate(rows, axis=0)).astype(jnp.int32)
    router = k.router[...].astype(F32)
    if sequences > 1:
        turned = jnp.concatenate([router[experts:], router[:experts]], axis=0)
        router = jnp.where(k.place.half == 1, turned, router)
    k.router_rows[...] = jnp.zeros_like(k.router_rows)
    k.router_rows[0:8, :] = jnp.concatenate(
        [router, jnp.zeros((8 - total, router.shape[1]), F32)], axis=0
    ).astype(BF16)


def attention_forward(k):
    length = k.kept[TURNED].shape[0]
    wide = k.kept[TURNED].shape[1] // 4
    heads = wide // HEAD
    place = k.place
    normed, turned = k.kept[NRM], k.kept[TURNED]
    k.early(QKV, PRJ)
    gather = TokenGather(place, normed, k.gather)
    normed[gather.rows(place.me), :] = normalise(k.x_in[...], k.gains_now[0:1, :]).astype(BF16)
    gather.start()
    make_tables(k, True)
    k.at(1)
    k.weight(QKV)
    for owner in gather.arrivals():
        rows = gather.rows(owner)
        projected = nn(normed[rows, :], k.matrix(QKV, 0, 3 * wide))
        turned[rows, : 2 * wide] = turn(projected[:, : 2 * wide], k.cosine[rows, :], k.sine[rows, :]).astype(BF16)
        turned[rows, 2 * wide : 3 * wide] = projected[:, 2 * wide :].astype(BF16)
    k.keep(NRM)
    k.at(2)
    block = 128
    for offset in range(0, length, block):
        extent = offset + block
        allowed = allowed_keys(k.seg_row[:, :extent], k.columns[offset:extent, 8:9], offset)
        for head in range(heads):
            first = head * HEAD
            query = turned[offset:extent, first : first + HEAD] * BF16(HEAD**-0.5)
            keys = turned[:extent, wide + first : wide + first + HEAD]
            values = turned[:extent, 2 * wide + first : 2 * wide + first + HEAD]
            probability = softmax_rows(query, keys, allowed).astype(BF16)
            turned[offset:extent, 3 * wide + first : 3 * wide + first + HEAD] = nn(probability, values).astype(BF16)
        if extent % 256 == 0:
            k.at(2 + extent // 256)
    k.keep(TURNED)
    scatter = TokenScatter(place, k.scatter)
    k.weight(PRJ)
    scatter.begin(lambda owner: nt(turned[quarter_rows(length, owner), 3 * wide :], k.matrix(PRJ, 0, wide)))
    k.at(7)
    k.mid_now[...] = k.x_in[...] + scatter.total()


def attention_backward(k):
    sequences, length, width = k.up.shape
    wide = width // 4
    heads = wide // HEAD
    place = k.place
    up, normed = k.up.at[0], k.kept[MOE].at[0]
    turned, grads = (k.kept[MOE].at[1], k.up.at[1]) if sequences > 1 else (k.spare.at[0], k.spare.at[1])
    sums = k.moe_grad.at[0]
    load_turned = k.local.start(k.kept_in[TURNED], turned)
    load_normed = k.local.start(k.kept_in[NRM], normed)
    gather = TokenGather(place, up, k.own_gather)
    up[gather.rows(place.me), :] = k.grad[...].astype(BF16)
    load_rows = k.local.start(k.x, k.rows)
    gather.start()
    k.at(10)
    k.weight(QKV)
    k.weight(PRJ)
    sums[...] = jnp.zeros((length, width), F32)
    for owner in gather.arrivals():
        rows = gather.rows(owner)
        grads[rows, 3 * wide :] = nn(up[rows, :], k.matrix(PRJ, 0, wide)).astype(BF16)
    load_turned.wait()
    block = 128
    for offset in range(0, length, block):
        if offset % 256 == 0:
            k.at(11 + offset // 256)
        extent = offset + block
        allowed = allowed_keys(k.seg_row[:, :extent], k.columns[offset:extent, 8:9], offset)
        for head in range(heads):
            own, key, value, out = (slice(n * wide + head * HEAD, n * wide + (head + 1) * HEAD) for n in range(4))
            query = turned[offset:extent, own] * BF16(HEAD**-0.5)
            keys = turned[:extent, key]
            outer = grads[offset:extent, out]
            probability = softmax_rows(query, keys, allowed)
            inner = nt(outer, turned[:extent, value])
            score = probability * (inner - jnp.sum(probability * inner, axis=-1, keepdims=True))
            score = score.astype(BF16)
            sums[offset:extent, own] = nn(score, keys) * HEAD**-0.5
            sums[:extent, key] += tn(score, query)
            sums[:extent, value] += tn(probability.astype(BF16), outer)
    load_normed.wait()
    k.put_product(PRJ, 0, (up, turned, slice(3 * wide, 4 * wide)))
    k.made(PRJ)
    for offset in range(0, length, block):
        rows = slice(offset, offset + block)
        both = turn(sums[rows, : 2 * wide], k.cosine[rows, :], -k.sine[rows, :])
        grads[rows, : 2 * wide] = both.astype(BF16)
        grads[rows, 2 * wide : 3 * wide] = sums[rows, 2 * wide : 3 * wide].astype(BF16)
    scatter = TokenScatter(place, k.scatters[0])
    scatter.begin(lambda owner: nt(grads[quarter_rows(length, owner), : 3 * wide], k.matrix(QKV, 0, 3 * wide)))
    k.at(15)
    k.put_product(QKV, 0, (normed, grads, slice(0, 3 * wide)))
    k.made(QKV)
    k.at(16)
    load_rows.wait()
    inward, k.gain_att[...] = normalise_back(k.rows[...], k.gains[0:1, :], scatter.total())
    k.grad[...] += inward


def pick_softmax(logits, chosen, axis):
    highest = jnp.max(jnp.where(chosen > 0, logits, -1e30), axis=axis, keepdims=True)
    exponent = chosen * jnp.exp(jnp.where(chosen > 0, logits - highest, 0.0))
    return exponent / jnp.sum(exponent, axis=axis, keepdims=True)


def slot_halves():
    return [(0, CAP // 2), (CAP // 2, CAP)]


def slots_by_token(slot_row, first, last):
    shape = (last - first, slot_row.shape[1])
    return lax.broadcasted_iota(jnp.int32, shape, 0) == slot_row - first


def tokens_by_slot(slot_column):
    shape = (slot_column.shape[0], CAP)
    return (lax.broadcasted_iota(jnp.int32, shape, 1) == slot_column).astype(F32).astype(BF16)


def hidden_of(inner):
    units = inner.shape[1] // 2
    gate = inner[:, :units]
    return (gate * sigmoid(gate) * inner[:, units:]).astype(BF16)


def swiglu_back(down, inner):
    units = inner.shape[1] // 2
    gate, raised = inner[:, :units], inner[:, units:]
    squashed = sigmoid(gate)
    gate_grad = down * raised * squashed * (1.0 + gate * (1.0 - squashed))
    up_grad = down * gate * squashed
    return jnp.concatenate([gate_grad.astype(BF16), up_grad.astype(BF16)], axis=1)


def expert_order(sequences, experts):
    if sequences == 1:
        return [(0, e) for e in range(experts)]
    return [(0, 0), (1, 0), (1, 1), (0, 1)]


def both_arrivals(k, buf, on_rows, between, point):
    place = k.place
    sequences = buf.shape[0]
    own = TokenGather(place, buf.at[0], k.own_gather)
    quarter = own.rows(place.me)
    if sequences > 1:
        crossing = send(
            buf.at[0, quarter], buf.at[1, quarter], k.pair_send.at[0], k.pair_recv.at[0], place.partner()
        )
    own.start()
    k.at(point)
    for count, owner in enumerate(own.arrivals()):
        on_rows(0, own.rows(owner))
        if count == 1:
            k.at(point + 1)
    k.at(point + 2)
    if sequences > 1:
        crossing.wait_recv()
        other = TokenGather(place, buf.at[1], k.other_gather)
        other.start()
        between()
        k.at(point + 3)
        for owner in other.arrivals():
            on_rows(1, other.rows(owner))
        crossing.wait_send()
    else:
        between()
    k.at(point + 4)


def give_back(k, total):
    k.pair_sum[...] = total.astype(BF16)
    return send(k.pair_sum, k.pair_land, k.pair_send.at[1], k.pair_recv.at[1], k.place.partner())


def ffn_forward(k):
    sequences, length = k.kept[MOE].shape[:2]
    experts = k.kept[ROUTED].shape[0]
    place = k.place
    moe, branch = k.kept[MOE], k.branch
    k.early(SH, *(EX + e for e in range(experts)))
    moe[0, quarter_rows(length, place.me), :] = normalise(k.mid_now[...], k.gains_now[1:2, :]).astype(BF16)
    units = k.w[SH].shape[-1] // 3
    wide = k.w[EX].shape[-1] // 3

    def shared(s, rows):
        k.weight(SH)
        inner = nn(moe[s, rows, :], k.matrix(SH, 0, 2 * units))
        k.kept[SHARED][s, rows, :] = inner.astype(BF16)
        return nt(hidden_of(inner), k.matrix(SH, 2 * units, 3 * units))

    def on_rows(s, rows):
        if not k.shared_last:
            branch[s, rows, :] = shared(s, rows)
        logits = nt(moe[s, rows, :], k.router_rows[...])
        k.gates[s, rows, :] = pick_softmax(logits, k.chosen_cols[s, rows, :], 1)

    scatters = [TokenScatter(place, refs) for refs in k.scatters]

    def dispatch(s, e):
        index = s * experts + e
        for first, last in slot_halves():
            held = slots_by_token(k.slot_rows[index : index + 1, :], first, last).astype(F32).astype(BF16)
            k.kept[ROUTED][e, s * CAP + first : s * CAP + last, :] = nn(held, moe[s]).astype(BF16)

    def expert(s, e):
        k.weight(EX + e)
        index = s * experts + e
        for first, last in slot_halves():
            slots = slice(s * CAP + first, s * CAP + last)
            inner = nn(k.kept[ROUTED][e, slots, :], k.matrix(EX + e, 0, 2 * wide))
            k.kept[ACT][e, slots, :] = inner.astype(BF16)
            k.outs[first:last, :] = nt(hidden_of(inner), k.matrix(EX + e, 2 * wide, 3 * wide)).astype(BF16)
        if e < experts - 1 or k.shared_last:
            for first in range(0, length, length // 2):
                rows = slice(first, first + length // 2)
                combine = tokens_by_slot(k.columns[rows, index : index + 1])
                value = k.gates[s, rows, e : e + 1] * nn(combine, k.outs[...])
                branch[s, rows, :] = value if k.shared_last and e == 0 else branch[s, rows, :] + value
            return

        def block_of(owner):
            rows = quarter_rows(length, owner)
            combine = tokens_by_slot(k.columns[rows, index : index + 1])
            return branch[s, rows, :] + k.gates[s, rows, e : e + 1] * nn(combine, k.outs[...])

        if s == 0:
            k.settle()
        scatters[s].begin(block_of)

    def shared_block(s, owner):
        rows = quarter_rows(length, owner)
        return branch[s, rows, :] + shared(s, rows)

    order = expert_order(sequences, experts)

    def between():
        for e in range(experts):
            dispatch(0, e)
        k.gates_out[0] = pick_softmax(nt(k.router_rows[0:8, :], moe[0]), k.chosen_rows[0], 0)
        expert(*order[0])

    both_arrivals(k, moe, on_rows, between, 8)
    k.keep(MOE)
    for step, (s, e) in enumerate(order[1:]):
        if s > 0:
            dispatch(s, e)
        expert(s, e)
        k.at(13 + step)
    if k.shared_last:
        for s in reversed(range(sequences)):
            if s == 0:
                k.settle()
            scatters[s].begin(functools.partial(shared_block, s))
    k.keep(SHARED)
    for s in range(1, sequences):
        k.gates_out[s] = pick_softmax(nt(k.router_rows[0:8, :], moe[s]), k.chosen_rows[s], 0)
    k.keep(ROUTED)
    k.keep(ACT)
    if sequences > 1:
        returned = give_back(k, scatters[1].total())
        k.at(16)
    following = k.mid_now[...] + scatters[0].total()
    if sequences > 1:
        returned.wait_recv()
        following = following + k.pair_land[...].astype(F32)
        returned.wait_send()
    k.following_now[...] = following
    k.settle()


def ffn_backward(k):
    sequences, length = k.kept[MOE].shape[:2]
    experts = k.kept_in[ROUTED].shape[0]
    place = k.place
    moe, up, moe_grad = k.kept[MOE], k.up, k.moe_grad
    routed, act, shared = k.kept[ROUTED], k.kept[ACT], k.kept[SHARED]
    load_shared = k.local.start(k.kept_in[SHARED], shared)
    load_upstream = k.local.start(k.upstream, k.grad)
    load_rows = k.local.start(k.mid, k.rows)
    k.early(SH, *(EX + e for e in range(experts)))

    def load_expert(e):
        return [k.local.start(k.kept_in[name].at[e], k.kept[name]) for name in (ACT, ROUTED)]

    loads = {0: load_expert(0)}
    load_moe = k.local.start(k.kept_in[MOE], moe)
    k.early(QKV, PRJ)
    make_tables(k, False)
    load_upstream.wait()
    up[0, quarter_rows(length, place.me), :] = k.grad[...].astype(BF16)
    units = k.w[SH].shape[-1] // 3
    wide = k.w[EX].shape[-1] // 3
    fresh = {SH}

    def on_rows(s, rows):
        k.weight(SH)
        if SH in fresh:
            fresh.remove(SH)
            load_shared.wait()
        inner = shared[s, rows, :].astype(F32)
        k.hidden_all[s, rows, :] = hidden_of(inner)
        down = nn(up[s, rows, :], k.matrix(SH, 2 * units, 3 * units))
        inner_grad = swiglu_back(down, inner)
        shared[s, rows, :] = inner_grad
        moe_grad[s, rows, :] = nt(inner_grad, k.matrix(SH, 0, 2 * units))

    scatters = [TokenScatter(place, refs) for refs in k.scatters]
    for s in range(sequences):
        k.slot_sums[s] = jnp.zeros_like(k.slot_sums[s])
    done = [0] * experts

    def expert(s, e):
        k.weight(EX + e)
        index = s * experts + e
        holding = k.slot_rows[index : index + 1, :]
        gate_row = k.gate_rows[s, e : e + 1, :]
        token_dots = jnp.zeros((1, length), F32)
        for first, last in slot_halves():
            slots = slice(s * CAP + first, s * CAP + last)
            held = slots_by_token(holding, first, last)
            gate_slot = jnp.sum(jnp.where(held, gate_row, 0.0), axis=1, keepdims=True)
            arrived = nn(held.astype(F32).astype(BF16), up[s]).astype(BF16)
            k.slot_grad[slots, :] = (arrived.astype(F32) * gate_slot).astype(BF16)
            down = nn(arrived, k.matrix(EX + e, 2 * wide, 3 * wide))
            for copy in loads.pop(e, ()):
                copy.wait()
            inner = act[slots, :].astype(F32)
            hidden = hidden_of(inner)
            k.hidden[slots, :] = hidden
            slot_dot = jnp.sum(hidden.astype(F32) * down, axis=1, keepdims=True)
            token_dots += jnp.sum(jnp.where(held, slot_dot, 0.0), axis=0, keepdims=True)
            inner_grad = swiglu_back(down * gate_slot, inner)
            act[slots, :] = inner_grad
            k.outs[first:last, :] = nt(inner_grad, k.matrix(EX + e, 0, 2 * wide)).astype(BF16)
        k.slot_sums[s, e : e + 1, :] = token_dots
        if e < experts - 1:
            for first in range(0, length, length // 2):
                rows = slice(first, first + length // 2)
                combine = tokens_by_slot(k.columns[rows, index : index + 1])
                moe_grad[s, rows, :] += nn(combine, k.outs[...])
        else:
            gates = k.gate_rows[s]
            pair = jnp.sum(gates, axis=0, keepdims=True)
            product = 0.5 * (pair * pair - jnp.sum(gates * gates, axis=0, keepdims=True))
            sums = k.slot_sums[s]
            logit_grad = k.chosen_rows[s] * product * (2.0 * sums - jnp.sum(sums, axis=0, keepdims=True))
            k.logit_grad[s] = logit_grad.astype(BF16)

            def block_of(owner):
                rows = quarter_rows(length, owner)
                combine = tokens_by_slot(k.columns[rows, index : index + 1])
                turned = tn(k.logit_grad[s, :, rows], k.router_rows[0:8, :])
                return moe_grad[s, rows, :] + nn(combine, k.outs[...]) + turned

            scatters[s].begin(block_of)
        done[e] += 1
        if done[e] == sequences:
            k.put_product(EX + e, 0, (routed, act, slice(None)))
            k.put_product(EX + e, 2 * wide, (k.slot_grad, k.hidden, slice(None)))
            k.made(EX + e)
            if e + 1 < experts:
                loads[e + 1] = load_expert(e + 1)

    order = expert_order(sequences, experts)
    both_arrivals(k, up, on_rows, lambda: expert(*order[0]), 1)
    load_moe.wait()
    every = range(sequences)
    k.put_product(SH, 0, *((moe.at[s], shared.at[s], slice(None)) for s in every))
    k.put_product(SH, 2 * units, *((up.at[s], k.hidden_all.at[s], slice(None)) for s in every))
    k.made(SH)
    k.at(6)
    for step, (s, e) in enumerate(order[1:]):
        expert(s, e)
        k.at(7 + step)
    k.router_grad[...] = sum(nn(k.logit_grad[s], moe[s]) for s in range(sequences))
    if sequences > 1:
        returned = give_back(k, scatters[1].total())
    k.at(18)
    total = scatters[0].total()
    if sequences > 1:
        returned.wait_recv()
        total = total + k.pair_land[...].astype(F32)
        returned.wait_send()
    load_rows.wait()
    inward, k.gain_ffn[...] = normalise_back(k.rows[...], k.gains[1:2, :], total)
    k.grad[...] += inward


def forward(k):
    for layer in range(len(k.gains)):
        k.layer, k.base = layer, 20 * layer
        k.shared_last = k.sharing and layer == 0
        k.gains_now, k.router = k.gains[layer], k.routers[layer]
        k.x_in = k.following[layer - 1] if layer else k.x
        k.mid_now, k.following_now, k.gates_out = k.mid[layer], k.following[layer], k.gate_rows[layer]
        attention_forward(k)
        ffn_forward(k)


def layer_backward(k):
    ffn_backward(k)
    attention_backward(k)


def last_backward(k):
    layer_backward(k)
    place, stage = k.place, k.stage
    half = k.slot_rows.shape[0] // 2
    stage[0] = jnp.zeros_like(stage[0])
    for at, row in enumerate((k.gain_att, k.gain_ffn, *k.later[:2])):
        stage[0, at : at + 1, :] = row[...]
    for at, part in enumerate((k.router_grad, k.later[2])):
        first, second = part[:half, :], part[half : 2 * half, :]
        upper = place.half == 1
        stage[0, 8 * (at + 1) : 8 * (at + 1) + half, :] = jnp.where(upper, second, first)
        stage[0, 8 * (at + 1) + half : 8 * (at + 1) + 2 * half, :] = jnp.where(upper, first, second)
    partners = (place.member(place.core_peer), place.member(place.y_peer), place.beside())
    for step, partner in enumerate(partners):
        copy = send(stage.at[step], k.land.at[step], k.small_send.at[step], k.small_recv.at[step], partner)
        copy.wait_recv()
        stage[step + 1] = stage[step] + k.land[step]
        copy.wait_send()
    k.at(17)
    last = len(partners)
    copies = []
    for away in (1, 2, 3):
        copies.append(
            send(
                stage.at[last],
                k.rows_z.at[place.z],
                k.small_send.at[last + away - 1],
                k.small_recv.at[last + away - 1],
                place.beyond(away),
            )
        )
    k.rows_z[place.z] = stage[last]
    for copy in copies:
        copy.wait_recv()
    k.small_sum[...] = (k.rows_z[0] + k.rows_z[1]) + (k.rows_z[2] + k.rows_z[3])
    for copy in copies:
        copy.wait_send()


class Far:
    def __init__(self, array):
        self.array = array


class Out:
    def __init__(self, shape, kind=F32, far=False):
        self.shape, self.kind, self.far = shape, kind, far


class Store:
    def __init__(self, height, width, columns, parts, paired):
        self.height, self.width, self.columns, self.parts, self.paired = height, width, columns, parts, paired
        self.source, self.full = {}, {}
        self.z, self.x = {}, {}
        self.made, self.sums, self.totals = {}, {}, {}
        self.own_sums, self.straight_on = set(), []

    def keys(self, layer, matrix):
        return [(layer, matrix, part) for part in range(len(self.parts[matrix]))]

    def shape_of(self, matrix):
        if self.paired:
            return (4, 2, self.height, self.columns[matrix])
        return (1, 1, self.width, self.columns[matrix])


def is_leaf(value):
    return not isinstance(value, (dict, list))


def call(store, body, collective_id, ins, outs, scratch, layers, weights=(), made=(), plan=()):
    ins, outs, scratch = dict(ins), dict(outs), dict(scratch)
    layer = layers[0]
    dma, vmem = pltpu.SemaphoreType.DMA, pltpu.VMEM
    width = store.width
    starts = [(kind, key) for _, kind, key, *taken in plan if not taken]
    starts += [(SUM_X, (layer, matrix)) for matrix in made if (layer, matrix) in store.own_sums]
    starts += [(SUM_Z, key) for key in store.straight_on]
    keys = [[key for own, key in starts if own == kind] for kind in range(4)]
    keys_in = [key for own in layers for matrix in weights for key in store.keys(own, matrix)]
    ins["src"] = {key: Far(store.source[key[:2]]) for key in keys[GET_Z]}
    ins["full_in"] = {(own, m): Far(store.full[own, m]) for own in layers for m in weights if not store.paired}
    ins["z_in"], ins["x_in"] = {}, {}
    if store.paired:
        wanted = set(keys_in) | set(keys[GET_X])
        ins["z_in"] = {key: Far(store.z[key]) for key in sorted(wanted - set(keys[GET_Z]))}
        ins["x_in"] = {key: Far(store.x[key]) for key in sorted(set(keys_in) - set(keys[GET_X]))}
    ins["made_in"] = {key: Far(store.made[key]) for key in keys[SUM_X] if key in store.made}
    ins["sums_in"] = {key: Far(store.sums[key]) for key in keys[SUM_Z] if key not in keys[SUM_X]}

    def part_shape(key):
        return (4, store.parts[key[1]][key[2]][1], store.columns[key[1]])

    def block_shape(key):
        return (4, store.height, store.columns[key[1]])

    outs["z_out"] = {key: Out(part_shape(key), BF16, True) for key in keys[GET_Z]}
    outs["x_out"] = {key: Out(part_shape(key), BF16, True) for key in keys[GET_X]}
    outs["sums_out"] = {key: Out(block_shape(key), BF16, True) for key in keys[SUM_X] if key not in keys[SUM_Z]}
    outs["totals"] = {key: [Out(block_shape(key)[1:], BF16)] * (1 if key[1] in (QKV, PRJ) else 2) for key in keys[SUM_Z]}
    outs["made_out"] = {
        m: Out(store.shape_of(m), BF16, True) for m in made if (layer, m) not in store.own_sums
    }
    scratch["w"] = {m: vmem(store.shape_of(m), BF16) for m in weights}
    scratch["sems"] = {
        GET_Z: {key: [dma((4,)), dma((4,)), dma((1,))] for key in keys[GET_Z]},
        GET_X: {key: [dma((1,)), dma((1,))] for key in keys[GET_X]},
        SUM_X: {key: [dma((4,)), dma((4,)), dma((2,))] for key in keys[SUM_X]},
        SUM_Z: {key: [dma((4,)), dma((4,)), dma((1,))] for key in keys[SUM_Z]},
    }
    scratch["blocks"] = {key: vmem(block_shape(key), BF16) for key in keys[SUM_X]}
    scratch["own"] = {key: vmem(block_shape(key), BF16) for key in keys[SUM_X] if key in store.made}
    scratch["lands"] = {key: vmem(block_shape(key), BF16) for key in keys[SUM_Z]}
    scratch["lsem"] = dma((2 * len(keys_in) + 20,))
    trees = [jax.tree.flatten(tree, is_leaf=is_leaf) for tree in (ins, outs, scratch)]
    (ins_flat, _), (outs_flat, outs_tree), (scratch_flat, _) = trees
    around = bool(starts)

    def kernel(*refs):
        k = types.SimpleNamespace()
        at = 0
        for flat, tree in trees:
            for name, value in jax.tree.unflatten(tree, refs[at : at + len(flat)]).items():
                setattr(k, name, value)
            at += len(flat)
        place = k.place = Place()
        k.local = Local(k.lsem)
        k.layer, k.base, k.sharing = layer, 0, store.paired
        k.stores = []
        peers = place.greet_sequence()
        if around:
            peers += place.greet_all()
        elif store.paired:
            peers += [place.partner()]
        place.greet(peers)
        k.exchange = hasattr(k, "news")
        if k.exchange:
            k.picks_sent = send(k.picks[0], k.news, k.news_send.at[0], k.news_recv.at[0], place.partner())
            k.picks = [k.picks[0], k.news]

        def job(kind, key):
            sems = k.sems[kind][key]
            if kind == GET_Z:
                return Straight(place, k.src[key], k.z_out[key], store.parts[key[1]][key[2]], sems)
            if kind == GET_X:
                source = k.z_out[key] if key in k.z_out else k.z_in[key]
                return Aside(place, source, k.x_out[key], sems)
            if kind == SUM_X:
                source = k.made_in[key] if key in k.made_in else k.w[key[1]]
                onward = None
                if key in k.lands:
                    onward = running[SUM_Z, key] = job(SUM_Z, key)
                return AsideSum(place, source, k.own.get(key), k.blocks[key], k.sums_out.get(key), onward, sems)
            source = k.blocks[key] if key in k.blocks else k.sums_in[key]
            return StraightSum(place, source, k.lands[key], k.totals[key], sems)

        running, ended = {}, set()

        def start(kind, key):
            transfer = running[kind, key] = job(kind, key)
            transfer.start()

        def end(kind, key):
            if (kind, key) not in ended:
                ended.add((kind, key))
                running[kind, key].arrived()

        def at_point(point):
            for own, kind, key, *taken in plan:
                if own != point + k.base:
                    continue
                if kind == SUM_X and taken:
                    running[kind, key].take(*taken)
                else:
                    (end if taken else start)(kind, key)

        loads, loaded = {}, set()

        def parts_of(matrix):
            return [(key, *store.parts[matrix][key[2]]) for key in store.keys(k.layer, matrix)]

        def load_part(key, first, rows):
            w = k.w[key[1]]
            span = pl.ds(first, rows)
            for got, landed, kind, x in (
                (k.z_in, k.z_out, GET_Z, place.x),
                (k.x_in, k.x_out, GET_X, 1 - place.x),
            ):
                if key in landed:
                    end(kind, key)
                source = landed[key] if key in landed else got[key]
                loads.setdefault(key, []).append(k.local.start(source, w.at[:, x, span]))

        def early(*matrices):
            for matrix in matrices:
                if not store.paired:
                    loads[k.layer, matrix] = [k.local.start(k.full_in[k.layer, matrix], k.w[matrix])]
                    continue
                for key, first, rows in parts_of(matrix):
                    if key in k.z_in and key in k.x_in:
                        load_part(key, first, rows)

        def weight(matrix):
            if (k.layer, matrix) in loaded:
                return
            loaded.add((k.layer, matrix))
            if not store.paired:
                for copy in loads[k.layer, matrix]:
                    copy.wait()
                return
            for key, first, rows in parts_of(matrix):
                if key not in loads:
                    load_part(key, first, rows)
            for key, *_ in parts_of(matrix):
                for copy in loads[key]:
                    copy.wait()

        def matrix_of(matrix, first, last):
            value = k.w[matrix][:, :, :, first:last]
            return value.reshape(width, last - first)

        def put_product(matrix, first, *pairs):
            ref, half = k.w[matrix], width // 2
            blocks = ref.shape[0] // 2
            for part in range(2):
                cut = slice(part * half, (part + 1) * half)
                value = sum(tn(left[:, cut], right[:, taken]) for left, right, taken in pairs).astype(BF16)
                count, columns = value.shape[1], slice(first, first + value.shape[1])
                if blocks:
                    shape = (blocks, *ref.shape[1:3], count)
                    ref[part * blocks : (part + 1) * blocks, :, :, columns] = value.reshape(shape)
                else:
                    ref[0, 0, part * half : (part + 1) * half, columns] = value

        def finished(matrix):
            if (layer, matrix) in k.blocks:
                start(SUM_X, (layer, matrix))
            else:
                k.local.start(k.w[matrix], k.made_out[matrix], True)

        k.at, k.early, k.weight, k.matrix, k.made = at_point, early, weight, matrix_of, finished
        k.put_product = put_product

        def keep(name):
            k.stores.append(k.local.start(k.kept[name], k.kept_out[k.layer][name]))

        def settle():
            while k.stores:
                k.stores.pop().wait()

        k.keep, k.settle = keep, settle
        at_point(0)
        body(k)
        for kind, key in sorted(running):
            end(kind, key)
        for transfer in running.values():
            transfer.close()
        k.local.close()

    hbm, near = pl.BlockSpec(memory_space=pl.ANY), pl.BlockSpec(memory_space=pltpu.VMEM)
    results = pl.pallas_call(
        kernel,
        out_shape=[jax.ShapeDtypeStruct(out.shape, out.kind) for out in outs_flat],
        in_specs=[hbm if isinstance(value, Far) else near for value in ins_flat],
        out_specs=[hbm if out.far else near for out in outs_flat],
        scratch_shapes=scratch_flat,
        compiler_params=pltpu.CompilerParams(
            collective_id=collective_id, has_side_effects=True, vmem_limit_bytes=VMEM_LIMIT
        ),
    )(*[value.array if isinstance(value, Far) else value for value in ins_flat])
    result = types.SimpleNamespace(**jax.tree.unflatten(outs_tree, results))
    store.z |= result.z_out
    store.x |= result.x_out
    store.sums |= result.sums_out
    store.totals |= result.totals
    store.made |= {(layer, m): value for m, value in result.made_out.items()}
    return result


def plain(body, outs, *arrays):
    near = pl.BlockSpec(memory_space=pltpu.VMEM)
    return pl.pallas_call(
        body,
        out_shape=[jax.ShapeDtypeStruct(out.shape, out.kind) for out in outs],
        in_specs=[near] * len(arrays),
        out_specs=[near] * len(outs),
        compiler_params=pltpu.CompilerParams(vmem_limit_bytes=VMEM_LIMIT),
    )(*arrays)


def turned_over(value):
    return jnp.transpose(value.astype(F32))


def pack_all(attention, projection, widening, narrowing, expansion, contraction, experts, shared_units):
    layers, _, height, wide = attention.shape
    units = widening.shape[3]
    keys, outs = [], []
    for layer in range(layers):
        shapes = {QKV: (height, 3 * wide), PRJ: (height, wide), SH: (2, height, 3 * shared_units)}
        shapes |= {EX + e: (2, height, 3 * units) for e in range(experts)}
        keys += [(layer, matrix) for matrix in shapes]
        outs += [Out(shape, BF16) for shape in shapes.values()]

    def body(att, prj, wid, nar, exp, con, *results):
        results = dict(zip(keys, results, strict=True))
        for layer in range(layers):
            for n in range(3):
                results[layer, QKV][:, n * wide : (n + 1) * wide] = att[layer, n]
            results[layer, PRJ][...] = turned_over(prj[layer]).astype(BF16)
            for half in range(2):
                cut = slice(half * shared_units, (half + 1) * shared_units)
                shared = results[layer, SH]
                shared[half, :, : 2 * shared_units] = jnp.concatenate([wid[layer, n, :, cut] for n in range(2)], axis=1)
                shared[half, :, 2 * shared_units :] = nar[layer, :, cut]
                for e in range(experts):
                    whole, given = results[layer, EX + e], half * experts + e
                    for n in range(2):
                        whole[half, :, n * units : (n + 1) * units] = exp[layer, given, n]
                    whole[half, :, 2 * units :] = con[layer, given]

    narrowing, contraction = jnp.swapaxes(narrowing, 1, 2), jnp.swapaxes(contraction, 2, 3)
    results = plain(body, outs, attention, projection, widening, narrowing, expansion, contraction)
    return dict(zip(keys, results, strict=True))


def unpack_all(current, upstream, small, totals, layers, all_experts, experts, shared_units, units, wide):
    width = current.shape[1]
    height = totals[0, QKV][0].shape[0]
    keys = sorted(totals)
    counts = [len(totals[key]) for key in keys]
    outs = [
        Out(current.shape),
        Out(upstream.shape),
        Out((layers, 2, width)),
        Out((layers, 3, height, wide)),
        Out((layers, wide, height)),
        Out((layers, all_experts, width)),
        Out((layers, 2, height, units)),
        Out((layers, height, units)),
        Out((layers, all_experts, 2, height, units)),
        Out((layers, all_experts, height, units)),
    ]

    def body(*refs):
        now, up, sums = refs[:3]
        parts, at = {}, 3
        for key, count in zip(keys, counts, strict=True):
            parts[key] = refs[at : at + count]
            at += count
        now_out, up_out, gains, att, prj, router, wid, nar, exp, con = refs[at:]
        upper = Place().half == 1
        now_out[...] = now[...]
        up_out[...] = up[...]

        def halves(key):
            mine, theirs = (part[...].astype(F32) for part in parts[key])
            return jnp.where(upper, theirs, mine), jnp.where(upper, mine, theirs)

        for layer in range(layers):
            gains[layer] = sums[2 * layer : 2 * layer + 2, :]
            router[layer] = sums[8 * layer + 8 : 8 * layer + 8 + all_experts, :]
            whole = parts[layer, QKV][0]
            for n in range(3):
                att[layer, n] = whole[:, n * wide : (n + 1) * wide].astype(F32)
            prj[layer] = turned_over(parts[layer, PRJ][0][...])
            for half, value in enumerate(halves((layer, SH))):
                cut = slice(half * shared_units, (half + 1) * shared_units)
                for n in range(2):
                    wid[layer, n, :, cut] = value[:, n * shared_units : (n + 1) * shared_units]
                nar[layer, :, cut] = value[:, 2 * shared_units :]
            for e in range(experts):
                for half, value in enumerate(halves((layer, EX + e))):
                    for n in range(2):
                        exp[layer, half * experts + e, n] = value[:, n * units : (n + 1) * units]
                    con[layer, half * experts + e] = value[:, 2 * units :]

    arrays = [current, upstream, small, *(part for key in keys for part in totals[key])]
    now, up, gains, att, prj, router, wid, nar, exp, con = plain(body, outs, *arrays)
    return now, up, gains, att, prj, jnp.swapaxes(router, 1, 2), wid, jnp.swapaxes(nar, 1, 2), exp, jnp.swapaxes(con, 2, 3)


def forward_plan(store, layers):
    def pass_on(point, *keys):
        return [step for key in keys for step in ((point, GET_Z, key, True), (point, GET_X, key))]

    def go(point, *keys):
        return [(point, GET_Z, key) for key in keys]

    plan = []
    for layer in range(layers):
        qkv, (prj,), sh = (store.keys(layer, matrix) for matrix in (QKV, PRJ, SH))
        low, high = store.keys(layer, EX), store.keys(layer, EX + 1)
        at = 20 * layer
        if layer == 0:
            plan += go(0, *qkv, prj, *low) + pass_on(1, *qkv) + pass_on(2, prj) + go(2, high[0])
            plan += pass_on(5, low[0]) + pass_on(7, low[1]) + pass_on(8, low[2]) + go(8, *high[1:], *sh)
            plan += pass_on(9, high[0]) + pass_on(11, high[1]) + pass_on(12, high[2])
            plan += pass_on(13, sh[0]) + pass_on(14, sh[1])
        else:
            plan += go(at - 12, *qkv, prj, *sh) + pass_on(at - 5, *qkv, prj) + pass_on(at - 4, *sh)
            plan += go(at - 4, *low, *high[:2]) + pass_on(at + 2, *low[:2]) + pass_on(at + 5, low[2])
            plan += go(at + 8, high[2]) + pass_on(at + 8, *high[:2]) + pass_on(at + 11, high[2])
    return plan


def backward_plan(layer, last):
    sh, low, high, prj, qkv = ((layer, matrix) for matrix in (SH, EX, EX + 1, PRJ, QKV))
    plan = [(7, SUM_X, sh, 2), (8, SUM_X, sh, 2), (18, SUM_X, low, 2), (10, SUM_X, low, 1), (11, SUM_X, low, 1)]
    own, onward = [sh, low, high], [sh, low]
    if layer < last:
        above = [(layer + 1, PRJ), (layer + 1, QKV)]
        plan += [(0, SUM_X, key) for key in above] + [(1, SUM_Z, (layer + 1, EX + 1))]
        plan += [(6, SUM_X, key, 4) for key in above]
        onward += above
    if layer == 0:
        plan += [(12, SUM_X, high, 1), (14, SUM_X, high, 1), (15, SUM_X, high, 2), (16, SUM_X, prj, 4)]
        plan += [(17, SUM_X, qkv, 4)]
        own, onward = [*own, prj, qkv], [*onward, high, prj, qkv]
    return plan, own, onward


def on_device(
    ring, stream, cotangent, segments, expert_pick, slot_index, norm_gains,
    attention, projection, router, widening, narrowing, expansion, contraction,
):
    layers = attention.shape[0]
    segment = segments[0]
    length = segment.shape[0]
    all_experts = expansion.shape[1]
    width = stream.shape[1]
    quarter = stream.shape[0]
    wide = attention.shape[3]
    units = widening.shape[3]
    height = attention.shape[2]
    paired = ring == 8
    sequences = 2 if paired else 1
    experts = all_experts // sequences
    shared_units = units // sequences
    inverse = np.exp(np.arange(HEAD // 2, dtype=np.float32) * np.float32(-2.0 * math.log(10000.0) / HEAD))
    phases = np.arange(length, dtype=np.float32)[:, None] * inverse[None, :]
    cosine, sine = np.cos(phases), np.sin(phases)
    places = dict(
        cosine=jnp.asarray(np.concatenate([cosine] * 4, axis=1)),
        sine=jnp.asarray(np.concatenate([-sine, sine] * 2, axis=1)),
        seg_row=segment[None, :],
    )
    picks = [jnp.swapaxes(jnp.concatenate([expert_pick, slot_index], axis=2), 1, 2).reshape(4 * layers, length)]
    router_rows = jnp.swapaxes(router, 1, 2)

    columns = {QKV: 3 * wide, PRJ: wide, SH: 3 * shared_units} | {EX + e: 3 * units for e in range(experts)}
    parts = {matrix: [(0, height)] for matrix in columns}
    if paired:
        third = height // 3
        parts[QKV] = parts[EX] = [(at, third) for at in (0, third, 2 * third)]
        parts[SH] = [(0, height // 2), (height // 2, height - height // 2)]
        parts[EX + 1] = [(0, height // 2), (height // 2, third), (height // 2 + third, height - height // 2 - third)]
    store = Store(height, width, columns, parts, paired)
    if paired:
        store.source = pack_all(
            attention, projection, widening, narrowing, expansion, contraction, experts, shared_units
        )
    else:
        whole = jnp.concatenate([expansion[:, :, 0], expansion[:, :, 1], jnp.swapaxes(contraction, 2, 3)], axis=-1)
        shared = jnp.concatenate([widening[:, 0], widening[:, 1], jnp.swapaxes(narrowing, 1, 2)], axis=-1)
        for layer in range(layers):
            store.source[layer, QKV] = jnp.concatenate([*attention[layer]], axis=-1)
            store.source[layer, PRJ] = projection[layer].T
            store.source[layer, SH] = shared[layer]
            for e in range(experts):
                store.source[layer, EX + e] = whole[layer, e]
    if not paired:
        store.full = {
            key: lax.all_gather(source, "dp", axis=0, tiled=True)[None, None] for key, source in store.source.items()
        }

    vmem = pltpu.VMEM
    token_scatter = scatter_scratch(length, width)
    pair_scratch = dict(scatters=[token_scatter] * sequences, own_gather=gather_scratch())
    if paired:
        pair_scratch |= dict(
            other_gather=gather_scratch(),
            pair_send=pltpu.SemaphoreType.DMA((2,)),
            pair_recv=pltpu.SemaphoreType.DMA((2,)),
            pair_sum=vmem((quarter, width), BF16),
            pair_land=vmem((quarter, width), BF16),
        )
    attention_shapes = {NRM: (length, width), TURNED: (length, 4 * wide)}
    ffn_shapes = {
        MOE: (sequences, length, width),
        SHARED: (sequences, length, 2 * shared_units),
        ROUTED: (experts, sequences * CAP, width),
        ACT: (experts, sequences * CAP, 2 * units),
    }
    ffn_matrices = [SH, *(EX + e for e in range(experts))]
    rows_out = Out((quarter, width))
    gain_out = Out((1, width))
    last = layers - 1

    def kept_scratch(shapes):
        return {name: vmem(shape, BF16) for name, shape in shapes.items()}

    def kept_outs(shapes):
        return {name: Out(shape, BF16, True) for name, shape in shapes.items()}

    tables = dict(
        slot_rows=vmem((sequences * experts, length), jnp.int32),
        chosen_rows=vmem((sequences, 8, length), F32),
        columns=vmem((length, LANES), jnp.int32),
        router_rows=vmem((LANES, width), BF16),
    )
    news = dict(
        news=vmem((4 * layers, length), jnp.int32),
        news_send=pltpu.SemaphoreType.DMA((1,)),
        news_recv=pltpu.SemaphoreType.DMA((1,)),
    )
    result = call(
        store,
        forward,
        0,
        dict(x=stream, gains=[*norm_gains], routers=[*router_rows], picks=picks, **places),
        dict(
            mid=[rows_out] * layers,
            following=[rows_out] * layers,
            gate_rows=[Out((sequences, 8, length))] * layers,
            kept_out=[kept_outs(attention_shapes | ffn_shapes)] * layers,
            **(dict(picks_out=Out((4 * layers, length), jnp.int32)) if paired else {}),
        ),
        dict(
            chosen_cols=vmem((sequences, length, LANES), F32),
            **tables,
            **(news if paired else {}),
            kept=kept_scratch(attention_shapes | ffn_shapes),
            branch=vmem((sequences, length, width), F32),
            outs=vmem((CAP, width), BF16),
            gates=vmem((sequences, length, LANES), F32),
            gather=gather_scratch(),
            scatter=token_scatter,
            **pair_scratch,
        ),
        range(layers),
        [QKV, PRJ, *ffn_matrices],
        plan=forward_plan(store, layers) if paired else (),
    )
    if paired:
        picks = [*picks, result.picks_out]
    current = result.following[last]
    saved = [
        ([stream, *result.following][layer], result.mid[layer], result.kept_out[layer], result.gate_rows[layer])
        for layer in range(layers)
    ]
    next_id = 1

    upstream = cotangent
    parts_small = [None] * layers
    for layer in reversed(range(layers)):
        x_in, mid, kept, gate_rows = saved[layer]
        finish = paired and layer == 0
        plan, store.own_sums, store.straight_on = backward_plan(layer, last) if paired else ((), (), ())
        ins = dict(
            upstream=Far(upstream),
            x=Far(x_in),
            mid=Far(mid),
            gains=norm_gains[layer],
            router=router_rows[layer],
            picks=picks,
            gate_rows=gate_rows,
            kept_in={name: Far(array) for name, array in kept.items()},
            **places,
        )
        outs = dict(grad=rows_out, gain_att=gain_out, gain_ffn=gain_out, router_grad=Out((8, width)))
        work = dict(
            **tables,
            kept={
                MOE: vmem((sequences, length, width), BF16),
                SHARED: vmem((sequences, length, 2 * shared_units), BF16),
                ROUTED: vmem((sequences * CAP, width), BF16),
                ACT: vmem((sequences * CAP, 2 * units), BF16),
            },
            hidden_all=vmem((sequences, length, shared_units), BF16),
            hidden=vmem((sequences * CAP, units), BF16),
            slot_grad=vmem((sequences * CAP, width), BF16),
            moe_grad=vmem((sequences, length, width), F32),
            slot_sums=vmem((sequences, 8, length), F32),
            logit_grad=vmem((sequences, 8, length), BF16),
            up=vmem((sequences, length, width), BF16),
            rows=vmem((quarter, width), F32),
            outs=vmem((CAP, width), BF16),
            **pair_scratch,
        )
        if not paired:
            work |= dict(spare=vmem((2, length, width), BF16))
        if finish:
            rows = 8 * (1 + layers)
            ins |= dict(later=list(parts_small[last]))
            outs |= dict(small_sum=Out((rows, width)))
            work |= dict(
                stage=vmem((4, rows, width), F32),
                land=vmem((3, rows, width), F32),
                rows_z=vmem((4, rows, width), F32),
                small_send=pltpu.SemaphoreType.DMA((6,)),
                small_recv=pltpu.SemaphoreType.DMA((6,)),
            )
        result = call(
            store,
            last_backward if finish else layer_backward,
            next_id,
            ins,
            outs,
            work,
            [layer],
            [QKV, PRJ, *ffn_matrices],
            [QKV, PRJ, *ffn_matrices],
            plan=plan if paired else (),
        )
        upstream = result.grad
        parts_small[layer] = (result.gain_att, result.gain_ffn, result.router_grad)
        next_id += 1

    if paired:
        return unpack_all(
            current, upstream, result.small_sum, store.totals, layers, all_experts, experts, shared_units, units, wide
        )
    gains_grad, router_grad = lax.psum(
        (
            jnp.stack([jnp.concatenate(part[:2], axis=0) for part in parts_small]),
            jnp.stack([part[2][:all_experts] for part in parts_small]),
        ),
        ("dp", "tensor"),
    )
    totals = {
        key: lax.psum_scatter(part[0, 0], "dp", scatter_dimension=0, tiled=True).astype(F32)
        for key, part in store.made.items()
    }
    att = jnp.stack([totals[layer, QKV] for layer in range(layers)])
    prj = jnp.stack([totals[layer, PRJ] for layer in range(layers)])
    shared = jnp.stack([totals[layer, SH] for layer in range(layers)])
    whole = jnp.stack([jnp.stack([totals[layer, EX + e] for e in range(experts)]) for layer in range(layers)])
    return (
        current,
        upstream,
        gains_grad,
        jnp.stack([att[..., n * wide : (n + 1) * wide] for n in range(3)], axis=1),
        jnp.swapaxes(prj, 1, 2),
        jnp.swapaxes(router_grad, 1, 2),
        jnp.stack([shared[..., n * units : (n + 1) * units] for n in range(2)], axis=1),
        jnp.swapaxes(shared[..., 2 * units :], 1, 2),
        jnp.stack([whole[..., n * units : (n + 1) * units] for n in range(2)], axis=2),
        jnp.swapaxes(whole[..., 2 * units :], 2, 3),
    )


def solution(mesh):
    placed = (
        P(("dp", "tensor"), None),
        P(("dp", "tensor"), None),
        P("dp", None),
        P(None, "dp", None),
        P(None, "dp", None),
        P(),
        P(None, None, "dp", "tensor"),
        P(None, "tensor", "dp"),
        P(),
        P(None, None, "dp", "tensor"),
        P(None, "tensor", "dp"),
        P(None, None, None, "dp", "tensor"),
        P(None, None, "tensor", "dp"),
    )
    return jax.shard_map(
        functools.partial(on_device, mesh.shape["dp"]),
        mesh=mesh,
        in_specs=placed,
        out_specs=(
            P(("dp", "tensor"), None),
            P(("dp", "tensor"), None),
            P(),
            P(None, None, "dp", "tensor"),
            P(None, "tensor", "dp"),
            P(),
            P(None, None, "dp", "tensor"),
            P(None, "tensor", "dp"),
            P(None, None, None, "dp", "tensor"),
            P(None, None, "tensor", "dp"),
        ),
        check_vma=False,
    )
```

```python
import functools
import math
import types

import jax
import jax.numpy as jnp
import numpy as np
from jax import lax
from jax.experimental import pallas as pl
from jax.experimental.pallas import tpu as pltpu
from jax.sharding import PartitionSpec as P

HEAD = 64
CAP = 640
LANES = 128
BF16 = jnp.bfloat16
F32 = jnp.float32
QKV, PRJ, SH, EX = range(4)
NRM, TURNED, MOE, SHARED, ROUTED, ACT = range(6)
GET_Z, GET_X, SUM_X, SUM_Z = range(4)
VMEM_LIMIT = 63 * 1024 * 1024


def nn(left, right):
    return lax.dot_general(left, right, (((1,), (0,)), ((), ())), preferred_element_type=F32)


def nt(left, right):
    return lax.dot_general(left, right, (((1,), (1,)), ((), ())), preferred_element_type=F32)


def tn(left, right):
    return lax.dot_general(left, right, (((0,), (0,)), ((), ())), preferred_element_type=F32)


class Place:
    def __init__(self):
        self.dp = lax.axis_index("dp")
        self.me = lax.axis_index("tensor")
        core = lax.rem(self.me, 2)
        self.core_peer = self.me + 1 - 2 * core
        self.y_peer = lax.rem(self.me + 2, 4)
        self.far_peer = lax.rem(self.core_peer + 2, 4)
        self.z = lax.div(self.dp, 2)
        self.x = lax.rem(self.dp, 2)
        self.half = lax.rem(self.z, 2)

    def member(self, tensor):
        return (self.dp, tensor)

    def row(self, away, x):
        return lax.rem(self.z + away + 4, 4) * 2 + x

    def beyond(self, away):
        return (self.row(away, self.x), self.me)

    def beside(self):
        return (self.row(0, 1 - self.x), self.me)

    def partner(self):
        return ((self.z + 1 - 2 * self.half) * 2 + self.x, self.me)

    def greet(self, peers):
        barrier = pltpu.get_barrier_semaphore()
        for peer in peers:
            pl.semaphore_signal(barrier, inc=1, device_id=peer, device_id_type=pl.DeviceIdType.MESH)
        pl.semaphore_wait(barrier, len(peers))

    def greet_sequence(self):
        return [self.member(self.core_peer), self.member(self.y_peer)]

    def greet_all(self):
        return [self.beside(), self.beyond(1), self.beyond(2), self.beyond(3)]


def send(source, target, send_sem, recv_sem, device):
    copy = pltpu.make_async_remote_copy(
        src_ref=source,
        dst_ref=target,
        send_sem=send_sem,
        recv_sem=recv_sem,
        device_id=device,
        device_id_type=pl.DeviceIdType.MESH,
    )
    copy.start()
    return copy


class Local:
    def __init__(self, sems):
        self.sems, self.used, self.open = sems, 0, []

    def start(self, source, target, keep=False):
        copy = pltpu.make_async_copy(source, target, self.sems.at[self.used])
        self.used += 1
        copy.start()
        if keep:
            self.open.append(copy)
        return copy

    def close(self):
        for copy in self.open:
            copy.wait()


def quarter_rows(length, member):
    quarter = length // 4
    return pl.ds(pl.multiple_of(member * quarter, quarter), quarter)


class TokenGather:
    def __init__(self, place, buf, sems):
        self.place, self.buf = place, buf
        self.sems = (sems["send_sem"], sems["recv_sem"])

    def rows(self, member):
        return quarter_rows(self.buf.shape[0], member)

    def pass_on(self, owner, target, slot):
        block = self.buf.at[self.rows(owner)]
        return send(block, block, self.sems[0].at[slot], self.sems[1].at[slot], self.place.member(target))

    def start(self):
        place = self.place
        self.far = self.pass_on(place.me, place.y_peer, 1)
        self.near = self.pass_on(place.me, place.core_peer, 0)

    def arrivals(self):
        place = self.place
        yield place.me
        self.near.wait_recv()
        yield place.core_peer
        self.far.wait_recv()
        self.onward = self.pass_on(place.y_peer, place.core_peer, 2)
        yield place.y_peer
        self.onward.wait_recv()
        yield place.far_peer
        self.near.wait_send()
        self.far.wait_send()
        self.onward.wait_send()


class TokenScatter:
    def __init__(self, place, refs):
        self.place = place
        refs = types.SimpleNamespace(**refs)
        self.part, self.landing, self.summed, self.crossed = refs.part, refs.landing, refs.summed, refs.crossed
        self.sems = (refs.send_sem, refs.recv_sem)

    def push(self, source, target, slot, member):
        return send(source, target, self.sems[0].at[slot], self.sems[1].at[slot], self.place.member(member))

    def begin(self, block_of):
        place, part = self.place, self.part
        part[0] = block_of(place.far_peer).astype(BF16)
        self.first = self.push(part.at[0], self.landing.at[0], 0, place.core_peer)
        crossing = block_of(place.y_peer)
        self.first.wait_recv()
        self.summed[...] = (crossing + self.landing[0].astype(F32)).astype(BF16)
        self.across = self.push(self.summed, self.crossed, 1, place.y_peer)
        part[1] = block_of(place.core_peer).astype(BF16)
        self.second = self.push(part.at[1], self.landing.at[1], 2, place.core_peer)
        self.own = block_of(place.me)

    def total(self):
        self.second.wait_recv()
        own = self.own + self.landing[1].astype(F32)
        self.across.wait_recv()
        own = own + self.crossed[...].astype(F32)
        self.first.wait_send()
        self.second.wait_send()
        self.across.wait_send()
        return own


def scatter_scratch(length, width):
    quarter = length // 4
    return dict(
        part=pltpu.VMEM((2, quarter, width), BF16),
        landing=pltpu.VMEM((2, quarter, width), BF16),
        summed=pltpu.VMEM((quarter, width), BF16),
        crossed=pltpu.VMEM((quarter, width), BF16),
        send_sem=pltpu.SemaphoreType.DMA((3,)),
        recv_sem=pltpu.SemaphoreType.DMA((3,)),
    )


def gather_scratch():
    return dict(send_sem=pltpu.SemaphoreType.DMA((3,)), recv_sem=pltpu.SemaphoreType.DMA((3,)))


class Straight:
    def __init__(self, place, source, target, rows, sems):
        self.place, self.source, self.target, self.rows = place, source, target, rows
        self.send_sem, self.recv_sem, self.local_sem = sems

    def part_for(self, away):
        source = self.source
        if len(source.shape) == 3:
            source = source.at[lax.rem(self.place.z + away, 2)]
        return source.at[pl.ds(*self.rows)]

    def start(self):
        place, mine = self.place, self.target.at[self.place.z]
        self.own = pltpu.make_async_copy(self.part_for(0), mine, self.local_sem.at[0])
        self.own.start()
        self.copies = [
            send(self.part_for(away), mine, self.send_sem.at[away], self.recv_sem.at[away], place.beyond(away))
            for away in (2, 1, 3)
        ]

    def arrived(self):
        self.own.wait()
        for copy in self.copies:
            copy.wait_recv()

    def close(self):
        for copy in self.copies:
            copy.wait_send()


class Aside:
    def __init__(self, place, source, target, sems):
        self.place, self.source, self.target = place, source, target
        self.send_sem, self.recv_sem = sems

    def start(self):
        self.copy = send(
            self.source, self.target, self.send_sem.at[0], self.recv_sem.at[0], self.place.beside()
        )

    def arrived(self):
        self.copy.wait_recv()

    def close(self):
        self.copy.wait_send()


class AsideSum:
    def __init__(self, place, source, own, landing, out, onward, sems):
        self.place, self.source, self.own, self.landing = place, source, own, landing
        self.out, self.onward = out, onward
        self.send_sem, self.recv_sem, self.local_sem = sems
        self.left = [2, 1, 3, 0]

    def start(self):
        place = self.place
        self.copies = {}
        for away in self.left:
            at = lax.rem(place.z + away, 4)
            self.copies[away] = send(
                self.source.at[at, 1 - place.x],
                self.landing.at[at],
                self.send_sem.at[away],
                self.recv_sem.at[away],
                place.beside(),
            )
        self.load = None
        if self.own is not None:
            self.load = pltpu.make_async_copy(self.source.at[:, place.x], self.own, self.local_sem.at[0])
            self.load.start()

    def take(self, count):
        for away in self.left[:count]:
            at = lax.rem(self.place.z + away, 4)
            self.copies[away].wait_recv()
            if self.load is not None:
                self.load.wait()
                self.load = None
            own = self.source[at, self.place.x] if self.own is None else self.own[at]
            self.landing[at] = (own.astype(F32) + self.landing[at].astype(F32)).astype(BF16)
            if self.onward is not None:
                self.onward.push(away)
        self.left = self.left[count:]

    def arrived(self):
        self.take(len(self.left))
        if self.out is not None:
            self.store = pltpu.make_async_copy(self.landing, self.out, self.local_sem.at[1])
            self.store.start()

    def close(self):
        for copy in self.copies.values():
            copy.wait_send()
        if self.out is not None:
            self.store.wait()


class StraightSum:
    def __init__(self, place, source, landing, totals, sems):
        self.place, self.source, self.landing, self.totals = place, source, landing, totals
        self.send_sem, self.recv_sem, self.local_sem = sems
        self.copies = []

    def push(self, away):
        block = self.source.at[lax.rem(self.place.z + away, 4)]
        if away == 0:
            self.own = pltpu.make_async_copy(block, self.landing.at[0], self.local_sem.at[0])
            self.own.start()
            return
        sems = self.send_sem.at[away], self.recv_sem.at[away]
        self.copies.append(send(block, self.landing.at[away], *sems, self.place.beyond(away)))

    def start(self):
        for away in (2, 1, 3, 0):
            self.push(away)

    def arrived(self):
        for copy in self.copies:
            copy.wait_recv()
        self.own.wait()
        blocks = [self.landing[away].astype(F32) for away in range(4)]
        if len(self.totals) == 1:
            self.totals[0][...] = ((blocks[0] + blocks[2]) + (blocks[1] + blocks[3])).astype(BF16)
        else:
            self.totals[0][...] = (blocks[0] + blocks[2]).astype(BF16)
            self.totals[1][...] = (blocks[1] + blocks[3]).astype(BF16)

    def close(self):
        for copy in self.copies:
            copy.wait_send()


def normalise(values, gain):
    factor = lax.rsqrt(jnp.mean(values * values, axis=-1, keepdims=True) + 1e-06)
    return values * factor * gain


def normalise_back(values, gain, upstream):
    factor = lax.rsqrt(jnp.mean(values * values, axis=-1, keepdims=True) + 1e-06)
    scaled = upstream * gain
    inward = factor * scaled - values * factor * factor * factor * jnp.mean(
        scaled * values, axis=-1, keepdims=True
    )
    return inward, jnp.sum(upstream * values * factor, axis=0, keepdims=True)


def swap_halves(values):
    width = values.shape[1]
    lane = lax.broadcasted_iota(jnp.int32, values.shape, 1)
    return jnp.where(
        lax.rem(lane, HEAD) < HEAD // 2,
        pltpu.roll(values, width - HEAD // 2, 1),
        pltpu.roll(values, HEAD // 2, 1),
    )


def turn(values, cosine, sine):
    times = values.shape[1] // cosine.shape[1]
    return values * jnp.concatenate([cosine] * times, axis=1) + swap_halves(
        values
    ) * jnp.concatenate([sine] * times, axis=1)


def allowed_keys(seg_row, seg_col, offset):
    shape = (seg_col.shape[0], seg_row.shape[1])
    row_index = offset + lax.broadcasted_iota(jnp.int32, shape, 0)
    column_index = lax.broadcasted_iota(jnp.int32, shape, 1)
    return (column_index <= row_index) & (seg_row == seg_col)


def softmax_rows(query, keys, allowed):
    masked = jnp.where(allowed, nt(query, keys), -1e30)
    exponent = jnp.exp(masked - jnp.max(masked, axis=-1, keepdims=True))
    return exponent * (1.0 / jnp.sum(exponent, axis=-1, keepdims=True))


def sigmoid(values):
    return 1.0 / (1.0 + jnp.exp(-values))


def make_tables(k, forward):
    sequences = len(k.picks)
    experts, length = k.slot_rows.shape[0] // sequences, k.slot_rows.shape[1]
    count = sequences * experts
    total = k.router.shape[0]
    if k.exchange and k.layer == 0:
        k.picks_sent.wait()
        k.picks_out[...] = k.picks[1][...]
    first = experts * k.place.half if sequences > 1 else 0
    for s, picks in enumerate(k.picks):
        pick_a, pick_b, slot_a, slot_b = (picks[4 * k.layer + n : 4 * k.layer + n + 1, :] for n in range(4))
        rows = []
        for e in range(total):
            expert = lax.rem(e + first, total)
            by_a, by_b = pick_a == expert, pick_b == expert
            rows.append(jnp.where(by_a | by_b, 1.0, 0.0))
            if e < experts:
                k.slot_rows[s * experts + e : s * experts + e + 1, :] = jnp.where(
                    by_a, slot_a, jnp.where(by_b, slot_b, -1)
                )
        chosen = jnp.concatenate(rows + [jnp.zeros((8 - total, length), F32)], axis=0)
        k.chosen_rows[s] = chosen
        if forward:
            k.chosen_cols[s] = jnp.transpose(
                jnp.concatenate([chosen, jnp.zeros((LANES - 8, length), F32)], axis=0)
            )
    rows = [
        k.slot_rows[...].astype(F32),
        jnp.zeros((8 - count, length), F32),
        k.seg_row[...].astype(F32),
        jnp.zeros((LANES - 9, length), F32),
    ]
    k.columns[...] = jnp.transpose(jnp.concatenate(rows, axis=0)).astype(jnp.int32)
    router = k.router[...].astype(F32)
    if sequences > 1:
        turned = jnp.concatenate([router[experts:], router[:experts]], axis=0)
        router = jnp.where(k.place.half == 1, turned, router)
    k.router_rows[...] = jnp.zeros_like(k.router_rows)
    k.router_rows[0:8, :] = jnp.concatenate(
        [router, jnp.zeros((8 - total, router.shape[1]), F32)], axis=0
    ).astype(BF16)


def attention_forward(k):
    length = k.kept[TURNED].shape[0]
    wide = k.kept[TURNED].shape[1] // 4
    heads = wide // HEAD
    place = k.place
    normed, turned = k.kept[NRM], k.kept[TURNED]
    k.early(QKV, PRJ)
    gather = TokenGather(place, normed, k.gather)
    normed[gather.rows(place.me), :] = normalise(k.x_in[...], k.gains_now[0:1, :]).astype(BF16)
    gather.start()
    make_tables(k, True)
    k.at(1)
    k.weight(QKV)
    for owner in gather.arrivals():
        rows = gather.rows(owner)
        projected = nn(normed[rows, :], k.matrix(QKV, 0, 3 * wide))
        turned[rows, : 2 * wide] = turn(projected[:, : 2 * wide], k.cosine[rows, :], k.sine[rows, :]).astype(BF16)
        turned[rows, 2 * wide : 3 * wide] = projected[:, 2 * wide :].astype(BF16)
    k.keep(NRM)
    k.at(2)
    block = 128
    for offset in range(0, length, block):
        extent = offset + block
        allowed = allowed_keys(k.seg_row[:, :extent], k.columns[offset:extent, 8:9], offset)
        for head in range(heads):
            first = head * HEAD
            query = turned[offset:extent, first : first + HEAD] * BF16(HEAD**-0.5)
            keys = turned[:extent, wide + first : wide + first + HEAD]
            values = turned[:extent, 2 * wide + first : 2 * wide + first + HEAD]
            probability = softmax_rows(query, keys, allowed).astype(BF16)
            turned[offset:extent, 3 * wide + first : 3 * wide + first + HEAD] = nn(probability, values).astype(BF16)
        if extent % 256 == 0:
            k.at(2 + extent // 256)
    k.keep(TURNED)
    scatter = TokenScatter(place, k.scatter)
    k.weight(PRJ)
    scatter.begin(lambda owner: nt(turned[quarter_rows(length, owner), 3 * wide :], k.matrix(PRJ, 0, wide)))
    k.at(7)
    k.mid_now[...] = k.x_in[...] + scatter.total()


def attention_backward(k):
    sequences, length, width = k.up.shape
    wide = width // 4
    heads = wide // HEAD
    place = k.place
    up, normed = k.up.at[0], k.kept[MOE].at[0]
    turned, grads = (k.kept[MOE].at[1], k.up.at[1]) if sequences > 1 else (k.spare.at[0], k.spare.at[1])
    sums = k.moe_grad.at[0]
    load_turned = k.local.start(k.kept_in[TURNED], turned)
    load_normed = k.local.start(k.kept_in[NRM], normed)
    gather = TokenGather(place, up, k.own_gather)
    up[gather.rows(place.me), :] = k.grad[...].astype(BF16)
    load_rows = k.local.start(k.x, k.rows)
    gather.start()
    k.at(10)
    k.weight(QKV)
    k.weight(PRJ)
    sums[...] = jnp.zeros((length, width), F32)
    for owner in gather.arrivals():
        rows = gather.rows(owner)
        grads[rows, 3 * wide :] = nn(up[rows, :], k.matrix(PRJ, 0, wide)).astype(BF16)
    load_turned.wait()
    block = 128
    for offset in range(0, length, block):
        if offset % 256 == 0:
            k.at(11 + offset // 256)
        extent = offset + block
        allowed = allowed_keys(k.seg_row[:, :extent], k.columns[offset:extent, 8:9], offset)
        for head in range(heads):
            own, key, value, out = (slice(n * wide + head * HEAD, n * wide + (head + 1) * HEAD) for n in range(4))
            query = turned[offset:extent, own] * BF16(HEAD**-0.5)
            keys = turned[:extent, key]
            outer = grads[offset:extent, out]
            probability = softmax_rows(query, keys, allowed)
            inner = nt(outer, turned[:extent, value])
            score = probability * (inner - jnp.sum(probability * inner, axis=-1, keepdims=True))
            score = score.astype(BF16)
            sums[offset:extent, own] = nn(score, keys) * HEAD**-0.5
            sums[:extent, key] += tn(score, query)
            sums[:extent, value] += tn(probability.astype(BF16), outer)
    load_normed.wait()
    k.put_product(PRJ, 0, (up, turned, slice(3 * wide, 4 * wide)))
    k.made(PRJ)
    for offset in range(0, length, block):
        rows = slice(offset, offset + block)
        both = turn(sums[rows, : 2 * wide], k.cosine[rows, :], -k.sine[rows, :])
        grads[rows, : 2 * wide] = both.astype(BF16)
        grads[rows, 2 * wide : 3 * wide] = sums[rows, 2 * wide : 3 * wide].astype(BF16)
    scatter = TokenScatter(place, k.scatters[0])
    scatter.begin(lambda owner: nt(grads[quarter_rows(length, owner), : 3 * wide], k.matrix(QKV, 0, 3 * wide)))
    k.at(15)
    k.put_product(QKV, 0, (normed, grads, slice(0, 3 * wide)))
    k.made(QKV)
    k.at(16)
    load_rows.wait()
    inward, k.gain_att[...] = normalise_back(k.rows[...], k.gains[0:1, :], scatter.total())
    k.grad[...] += inward


def pick_softmax(logits, chosen, axis):
    highest = jnp.max(jnp.where(chosen > 0, logits, -1e30), axis=axis, keepdims=True)
    exponent = chosen * jnp.exp(jnp.where(chosen > 0, logits - highest, 0.0))
    return exponent / jnp.sum(exponent, axis=axis, keepdims=True)


def slot_halves():
    return [(0, CAP // 2), (CAP // 2, CAP)]


def slots_by_token(slot_row, first, last):
    shape = (last - first, slot_row.shape[1])
    return lax.broadcasted_iota(jnp.int32, shape, 0) == slot_row - first


def tokens_by_slot(slot_column):
    shape = (slot_column.shape[0], CAP)
    return (lax.broadcasted_iota(jnp.int32, shape, 1) == slot_column).astype(F32).astype(BF16)


def hidden_of(inner):
    units = inner.shape[1] // 2
    gate = inner[:, :units]
    return (gate * sigmoid(gate) * inner[:, units:]).astype(BF16)


def swiglu_back(down, inner):
    units = inner.shape[1] // 2
    gate, raised = inner[:, :units], inner[:, units:]
    squashed = sigmoid(gate)
    gate_grad = down * raised * squashed * (1.0 + gate * (1.0 - squashed))
    up_grad = down * gate * squashed
    return jnp.concatenate([gate_grad.astype(BF16), up_grad.astype(BF16)], axis=1)


def expert_order(sequences, experts):
    if sequences == 1:
        return [(0, e) for e in range(experts)]
    return [(0, 0), (1, 0), (1, 1), (0, 1)]


def both_arrivals(k, buf, on_rows, between, point):
    place = k.place
    sequences = buf.shape[0]
    own = TokenGather(place, buf.at[0], k.own_gather)
    quarter = own.rows(place.me)
    if sequences > 1:
        crossing = send(
            buf.at[0, quarter], buf.at[1, quarter], k.pair_send.at[0], k.pair_recv.at[0], place.partner()
        )
    own.start()
    k.at(point)
    for count, owner in enumerate(own.arrivals()):
        on_rows(0, own.rows(owner))
        if count == 1:
            k.at(point + 1)
    k.at(point + 2)
    if sequences > 1:
        crossing.wait_recv()
        other = TokenGather(place, buf.at[1], k.other_gather)
        other.start()
        between()
        k.at(point + 3)
        for owner in other.arrivals():
            on_rows(1, other.rows(owner))
        crossing.wait_send()
    else:
        between()
    k.at(point + 4)


def give_back(k, total):
    k.pair_sum[...] = total.astype(BF16)
    return send(k.pair_sum, k.pair_land, k.pair_send.at[1], k.pair_recv.at[1], k.place.partner())


def ffn_forward(k):
    sequences, length = k.kept[MOE].shape[:2]
    experts = k.kept[ROUTED].shape[0]
    place = k.place
    moe, branch = k.kept[MOE], k.branch
    k.early(SH, *(EX + e for e in range(experts)))
    moe[0, quarter_rows(length, place.me), :] = normalise(k.mid_now[...], k.gains_now[1:2, :]).astype(BF16)
    units = k.w[SH].shape[-1] // 3
    wide = k.w[EX].shape[-1] // 3

    def shared(s, rows):
        k.weight(SH)
        inner = nn(moe[s, rows, :], k.matrix(SH, 0, 2 * units))
        k.kept[SHARED][s, rows, :] = inner.astype(BF16)
        return nt(hidden_of(inner), k.matrix(SH, 2 * units, 3 * units))

    def on_rows(s, rows):
        if not k.shared_last:
            branch[s, rows, :] = shared(s, rows)
        logits = nt(moe[s, rows, :], k.router_rows[...])
        k.gates[s, rows, :] = pick_softmax(logits, k.chosen_cols[s, rows, :], 1)

    scatters = [TokenScatter(place, refs) for refs in k.scatters]

    def dispatch(s, e):
        index = s * experts + e
        for first, last in slot_halves():
            held = slots_by_token(k.slot_rows[index : index + 1, :], first, last).astype(F32).astype(BF16)
            k.kept[ROUTED][e, s * CAP + first : s * CAP + last, :] = nn(held, moe[s]).astype(BF16)

    def expert(s, e):
        k.weight(EX + e)
        index = s * experts + e
        for first, last in slot_halves():
            slots = slice(s * CAP + first, s * CAP + last)
            inner = nn(k.kept[ROUTED][e, slots, :], k.matrix(EX + e, 0, 2 * wide))
            k.kept[ACT][e, slots, :] = inner.astype(BF16)
            k.outs[first:last, :] = nt(hidden_of(inner), k.matrix(EX + e, 2 * wide, 3 * wide)).astype(BF16)
        if e < experts - 1 or k.shared_last:
            for first in range(0, length, length // 2):
                rows = slice(first, first + length // 2)
                combine = tokens_by_slot(k.columns[rows, index : index + 1])
                value = k.gates[s, rows, e : e + 1] * nn(combine, k.outs[...])
                branch[s, rows, :] = value if k.shared_last and e == 0 else branch[s, rows, :] + value
            return

        def block_of(owner):
            rows = quarter_rows(length, owner)
            combine = tokens_by_slot(k.columns[rows, index : index + 1])
            return branch[s, rows, :] + k.gates[s, rows, e : e + 1] * nn(combine, k.outs[...])

        if s == 0:
            k.settle()
        scatters[s].begin(block_of)

    def shared_block(s, owner):
        rows = quarter_rows(length, owner)
        return branch[s, rows, :] + shared(s, rows)

    order = expert_order(sequences, experts)

    def between():
        for e in range(experts):
            dispatch(0, e)
        k.gates_out[0] = pick_softmax(nt(k.router_rows[0:8, :], moe[0]), k.chosen_rows[0], 0)
        expert(*order[0])

    both_arrivals(k, moe, on_rows, between, 8)
    k.keep(MOE)
    for step, (s, e) in enumerate(order[1:]):
        if s > 0:
            dispatch(s, e)
        expert(s, e)
        k.at(13 + step)
    if k.shared_last:
        for s in reversed(range(sequences)):
            if s == 0:
                k.settle()
            scatters[s].begin(functools.partial(shared_block, s))
    k.keep(SHARED)
    for s in range(1, sequences):
        k.gates_out[s] = pick_softmax(nt(k.router_rows[0:8, :], moe[s]), k.chosen_rows[s], 0)
    k.keep(ROUTED)
    k.keep(ACT)
    if sequences > 1:
        returned = give_back(k, scatters[1].total())
        k.at(16)
    following = k.mid_now[...] + scatters[0].total()
    if sequences > 1:
        returned.wait_recv()
        following = following + k.pair_land[...].astype(F32)
        returned.wait_send()
    k.following_now[...] = following
    k.settle()


def ffn_backward(k):
    sequences, length = k.kept[MOE].shape[:2]
    experts = k.kept_in[ROUTED].shape[0]
    place = k.place
    moe, up, moe_grad = k.kept[MOE], k.up, k.moe_grad
    routed, act, shared = k.kept[ROUTED], k.kept[ACT], k.kept[SHARED]
    load_shared = k.local.start(k.kept_in[SHARED], shared)
    load_upstream = k.local.start(k.upstream, k.grad)
    load_rows = k.local.start(k.mid, k.rows)
    k.early(SH, *(EX + e for e in range(experts)))

    def load_expert(e):
        return [k.local.start(k.kept_in[name].at[e], k.kept[name]) for name in (ACT, ROUTED)]

    loads = {0: load_expert(0)}
    load_moe = k.local.start(k.kept_in[MOE], moe)
    k.early(QKV, PRJ)
    make_tables(k, False)
    load_upstream.wait()
    up[0, quarter_rows(length, place.me), :] = k.grad[...].astype(BF16)
    units = k.w[SH].shape[-1] // 3
    wide = k.w[EX].shape[-1] // 3
    fresh = {SH}

    def on_rows(s, rows):
        k.weight(SH)
        if SH in fresh:
            fresh.remove(SH)
            load_shared.wait()
        inner = shared[s, rows, :].astype(F32)
        k.hidden_all[s, rows, :] = hidden_of(inner)
        down = nn(up[s, rows, :], k.matrix(SH, 2 * units, 3 * units))
        inner_grad = swiglu_back(down, inner)
        shared[s, rows, :] = inner_grad
        moe_grad[s, rows, :] = nt(inner_grad, k.matrix(SH, 0, 2 * units))

    scatters = [TokenScatter(place, refs) for refs in k.scatters]
    for s in range(sequences):
        k.slot_sums[s] = jnp.zeros_like(k.slot_sums[s])
    done = [0] * experts

    def expert(s, e):
        k.weight(EX + e)
        index = s * experts + e
        holding = k.slot_rows[index : index + 1, :]
        gate_row = k.gate_rows[s, e : e + 1, :]
        token_dots = jnp.zeros((1, length), F32)
        for first, last in slot_halves():
            slots = slice(s * CAP + first, s * CAP + last)
            held = slots_by_token(holding, first, last)
            gate_slot = jnp.sum(jnp.where(held, gate_row, 0.0), axis=1, keepdims=True)
            arrived = nn(held.astype(F32).astype(BF16), up[s]).astype(BF16)
            k.slot_grad[slots, :] = (arrived.astype(F32) * gate_slot).astype(BF16)
            down = nn(arrived, k.matrix(EX + e, 2 * wide, 3 * wide))
            for copy in loads.pop(e, ()):
                copy.wait()
            inner = act[slots, :].astype(F32)
            hidden = hidden_of(inner)
            k.hidden[slots, :] = hidden
            slot_dot = jnp.sum(hidden.astype(F32) * down, axis=1, keepdims=True)
            token_dots += jnp.sum(jnp.where(held, slot_dot, 0.0), axis=0, keepdims=True)
            inner_grad = swiglu_back(down * gate_slot, inner)
            act[slots, :] = inner_grad
            k.outs[first:last, :] = nt(inner_grad, k.matrix(EX + e, 0, 2 * wide)).astype(BF16)
        k.slot_sums[s, e : e + 1, :] = token_dots
        if e < experts - 1:
            for first in range(0, length, length // 2):
                rows = slice(first, first + length // 2)
                combine = tokens_by_slot(k.columns[rows, index : index + 1])
                moe_grad[s, rows, :] += nn(combine, k.outs[...])
        else:
            gates = k.gate_rows[s]
            product = jnp.where(k.chosen_rows[s] > 0, gates, 1.0)
            for rows in (4, 2, 1):
                product = product[:rows, :] * product[rows:, :]
            sums = k.slot_sums[s]
            logit_grad = k.chosen_rows[s] * product * (2.0 * sums - jnp.sum(sums, axis=0, keepdims=True))
            k.logit_grad[s] = logit_grad.astype(BF16)

            def block_of(owner):
                rows = quarter_rows(length, owner)
                combine = tokens_by_slot(k.columns[rows, index : index + 1])
                turned = tn(k.logit_grad[s, :, rows], k.router_rows[0:8, :])
                return moe_grad[s, rows, :] + nn(combine, k.outs[...]) + turned

            scatters[s].begin(block_of)
        done[e] += 1
        if done[e] == sequences:
            k.put_product(EX + e, 0, (routed, act, slice(None)))
            k.put_product(EX + e, 2 * wide, (k.slot_grad, k.hidden, slice(None)))
            k.made(EX + e)
            if e + 1 < experts:
                loads[e + 1] = load_expert(e + 1)

    order = expert_order(sequences, experts)
    both_arrivals(k, up, on_rows, lambda: expert(*order[0]), 1)
    load_moe.wait()
    every = range(sequences)
    k.put_product(SH, 0, *((moe.at[s], shared.at[s], slice(None)) for s in every))
    k.put_product(SH, 2 * units, *((up.at[s], k.hidden_all.at[s], slice(None)) for s in every))
    k.made(SH)
    k.at(6)
    for step, (s, e) in enumerate(order[1:]):
        expert(s, e)
        k.at(7 + step)
    k.router_grad[...] = sum(nn(k.logit_grad[s], moe[s]) for s in range(sequences))
    if sequences > 1:
        returned = give_back(k, scatters[1].total())
    k.at(18)
    total = scatters[0].total()
    if sequences > 1:
        returned.wait_recv()
        total = total + k.pair_land[...].astype(F32)
        returned.wait_send()
    load_rows.wait()
    inward, k.gain_ffn[...] = normalise_back(k.rows[...], k.gains[1:2, :], total)
    k.grad[...] += inward


def forward(k):
    for layer in range(len(k.gains)):
        k.layer, k.base = layer, 20 * layer
        k.shared_last = k.sharing and layer == 0
        k.gains_now, k.router = k.gains[layer], k.routers[layer]
        k.x_in = k.following[layer - 1] if layer else k.x
        k.mid_now, k.following_now, k.gates_out = k.mid[layer], k.following[layer], k.gate_rows[layer]
        attention_forward(k)
        ffn_forward(k)


def layer_backward(k):
    ffn_backward(k)
    attention_backward(k)


def last_backward(k):
    layer_backward(k)
    place, stage = k.place, k.stage
    half = k.slot_rows.shape[0] // 2
    stage[0] = jnp.zeros_like(stage[0])
    for at, row in enumerate((k.gain_att, k.gain_ffn, *k.later[:2])):
        stage[0, at : at + 1, :] = row[...]
    for at, part in enumerate((k.router_grad, k.later[2])):
        first, second = part[:half, :], part[half : 2 * half, :]
        upper = place.half == 1
        stage[0, 8 * (at + 1) : 8 * (at + 1) + half, :] = jnp.where(upper, second, first)
        stage[0, 8 * (at + 1) + half : 8 * (at + 1) + 2 * half, :] = jnp.where(upper, first, second)
    partners = (place.member(place.core_peer), place.member(place.y_peer), place.beside())
    for step, partner in enumerate(partners):
        copy = send(stage.at[step], k.land.at[step], k.small_send.at[step], k.small_recv.at[step], partner)
        copy.wait_recv()
        stage[step + 1] = stage[step] + k.land[step]
        copy.wait_send()
    k.at(17)
    last = len(partners)
    copies = []
    for away in (1, 2, 3):
        copies.append(
            send(
                stage.at[last],
                k.rows_z.at[place.z],
                k.small_send.at[last + away - 1],
                k.small_recv.at[last + away - 1],
                place.beyond(away),
            )
        )
    k.rows_z[place.z] = stage[last]
    for copy in copies:
        copy.wait_recv()
    k.small_sum[...] = (k.rows_z[0] + k.rows_z[1]) + (k.rows_z[2] + k.rows_z[3])
    for copy in copies:
        copy.wait_send()


class Far:
    def __init__(self, array):
        self.array = array


class Out:
    def __init__(self, shape, kind=F32, far=False):
        self.shape, self.kind, self.far = shape, kind, far


class Store:
    def __init__(self, height, width, columns, parts, paired):
        self.height, self.width, self.columns, self.parts, self.paired = height, width, columns, parts, paired
        self.source, self.full = {}, {}
        self.z, self.x = {}, {}
        self.made, self.sums, self.totals = {}, {}, {}
        self.own_sums, self.straight_on = set(), []

    def keys(self, layer, matrix):
        return [(layer, matrix, part) for part in range(len(self.parts[matrix]))]

    def shape_of(self, matrix):
        if self.paired:
            return (4, 2, self.height, self.columns[matrix])
        return (1, 1, self.width, self.columns[matrix])


def is_leaf(value):
    return not isinstance(value, (dict, list))


def call(store, body, collective_id, ins, outs, scratch, layers, weights=(), made=(), plan=()):
    ins, outs, scratch = dict(ins), dict(outs), dict(scratch)
    layer = layers[0]
    dma, vmem = pltpu.SemaphoreType.DMA, pltpu.VMEM
    width = store.width
    starts = [(kind, key) for _, kind, key, *taken in plan if not taken]
    starts += [(SUM_X, (layer, matrix)) for matrix in made if (layer, matrix) in store.own_sums]
    starts += [(SUM_Z, key) for key in store.straight_on]
    keys = [[key for own, key in starts if own == kind] for kind in range(4)]
    keys_in = [key for own in layers for matrix in weights for key in store.keys(own, matrix)]
    ins["src"] = {key: Far(store.source[key[:2]]) for key in keys[GET_Z]}
    ins["full_in"] = {(own, m): Far(store.full[own, m]) for own in layers for m in weights if not store.paired}
    ins["z_in"], ins["x_in"] = {}, {}
    if store.paired:
        wanted = set(keys_in) | set(keys[GET_X])
        ins["z_in"] = {key: Far(store.z[key]) for key in sorted(wanted - set(keys[GET_Z]))}
        ins["x_in"] = {key: Far(store.x[key]) for key in sorted(set(keys_in) - set(keys[GET_X]))}
    ins["made_in"] = {key: Far(store.made[key]) for key in keys[SUM_X] if key in store.made}
    ins["sums_in"] = {key: Far(store.sums[key]) for key in keys[SUM_Z] if key not in keys[SUM_X]}

    def part_shape(key):
        return (4, store.parts[key[1]][key[2]][1], store.columns[key[1]])

    def block_shape(key):
        return (4, store.height, store.columns[key[1]])

    outs["z_out"] = {key: Out(part_shape(key), BF16, True) for key in keys[GET_Z]}
    outs["x_out"] = {key: Out(part_shape(key), BF16, True) for key in keys[GET_X]}
    outs["sums_out"] = {key: Out(block_shape(key), BF16, True) for key in keys[SUM_X] if key not in keys[SUM_Z]}
    outs["totals"] = {key: [Out(block_shape(key)[1:], BF16)] * (1 if key[1] in (QKV, PRJ) else 2) for key in keys[SUM_Z]}
    outs["made_out"] = {
        m: Out(store.shape_of(m), BF16, True) for m in made if (layer, m) not in store.own_sums
    }
    scratch["w"] = {m: vmem(store.shape_of(m), BF16) for m in weights}
    scratch["sems"] = {
        GET_Z: {key: [dma((4,)), dma((4,)), dma((1,))] for key in keys[GET_Z]},
        GET_X: {key: [dma((1,)), dma((1,))] for key in keys[GET_X]},
        SUM_X: {key: [dma((4,)), dma((4,)), dma((2,))] for key in keys[SUM_X]},
        SUM_Z: {key: [dma((4,)), dma((4,)), dma((1,))] for key in keys[SUM_Z]},
    }
    scratch["blocks"] = {key: vmem(block_shape(key), BF16) for key in keys[SUM_X]}
    scratch["own"] = {key: vmem(block_shape(key), BF16) for key in keys[SUM_X] if key in store.made}
    scratch["lands"] = {key: vmem(block_shape(key), BF16) for key in keys[SUM_Z]}
    scratch["lsem"] = dma((2 * len(keys_in) + 20,))
    trees = [jax.tree.flatten(tree, is_leaf=is_leaf) for tree in (ins, outs, scratch)]
    (ins_flat, _), (outs_flat, outs_tree), (scratch_flat, _) = trees
    around = bool(starts)

    def kernel(*refs):
        k = types.SimpleNamespace()
        at = 0
        for flat, tree in trees:
            for name, value in jax.tree.unflatten(tree, refs[at : at + len(flat)]).items():
                setattr(k, name, value)
            at += len(flat)
        place = k.place = Place()
        k.local = Local(k.lsem)
        k.layer, k.base, k.sharing = layer, 0, store.paired
        k.stores = []
        peers = place.greet_sequence()
        if around:
            peers += place.greet_all()
        elif store.paired:
            peers += [place.partner()]
        place.greet(peers)
        k.exchange = hasattr(k, "news")
        if k.exchange:
            k.picks_sent = send(k.picks[0], k.news, k.news_send.at[0], k.news_recv.at[0], place.partner())
            k.picks = [k.picks[0], k.news]

        def job(kind, key):
            sems = k.sems[kind][key]
            if kind == GET_Z:
                return Straight(place, k.src[key], k.z_out[key], store.parts[key[1]][key[2]], sems)
            if kind == GET_X:
                source = k.z_out[key] if key in k.z_out else k.z_in[key]
                return Aside(place, source, k.x_out[key], sems)
            if kind == SUM_X:
                source = k.made_in[key] if key in k.made_in else k.w[key[1]]
                onward = None
                if key in k.lands:
                    onward = running[SUM_Z, key] = job(SUM_Z, key)
                return AsideSum(place, source, k.own.get(key), k.blocks[key], k.sums_out.get(key), onward, sems)
            source = k.blocks[key] if key in k.blocks else k.sums_in[key]
            return StraightSum(place, source, k.lands[key], k.totals[key], sems)

        running, ended = {}, set()

        def start(kind, key):
            transfer = running[kind, key] = job(kind, key)
            transfer.start()

        def end(kind, key):
            if (kind, key) not in ended:
                ended.add((kind, key))
                running[kind, key].arrived()

        def at_point(point):
            for own, kind, key, *taken in plan:
                if own != point + k.base:
                    continue
                if kind == SUM_X and taken:
                    running[kind, key].take(*taken)
                else:
                    (end if taken else start)(kind, key)

        loads, loaded = {}, set()

        def parts_of(matrix):
            return [(key, *store.parts[matrix][key[2]]) for key in store.keys(k.layer, matrix)]

        def load_part(key, first, rows):
            w = k.w[key[1]]
            span = pl.ds(first, rows)
            for got, landed, kind, x in (
                (k.z_in, k.z_out, GET_Z, place.x),
                (k.x_in, k.x_out, GET_X, 1 - place.x),
            ):
                if key in landed:
                    end(kind, key)
                source = landed[key] if key in landed else got[key]
                loads.setdefault(key, []).append(k.local.start(source, w.at[:, x, span]))

        def early(*matrices):
            for matrix in matrices:
                if not store.paired:
                    loads[k.layer, matrix] = [k.local.start(k.full_in[k.layer, matrix], k.w[matrix])]
                    continue
                for key, first, rows in parts_of(matrix):
                    if key in k.z_in and key in k.x_in:
                        load_part(key, first, rows)

        def weight(matrix):
            if (k.layer, matrix) in loaded:
                return
            loaded.add((k.layer, matrix))
            if not store.paired:
                for copy in loads[k.layer, matrix]:
                    copy.wait()
                return
            for key, first, rows in parts_of(matrix):
                if key not in loads:
                    load_part(key, first, rows)
            for key, *_ in parts_of(matrix):
                for copy in loads[key]:
                    copy.wait()

        def matrix_of(matrix, first, last):
            value = k.w[matrix][:, :, :, first:last]
            return value.reshape(width, last - first)

        def put_product(matrix, first, *pairs):
            ref, half = k.w[matrix], width // 2
            blocks = ref.shape[0] // 2
            for part in range(2):
                cut = slice(part * half, (part + 1) * half)
                value = sum(tn(left[:, cut], right[:, taken]) for left, right, taken in pairs).astype(BF16)
                count, columns = value.shape[1], slice(first, first + value.shape[1])
                if blocks:
                    shape = (blocks, *ref.shape[1:3], count)
                    ref[part * blocks : (part + 1) * blocks, :, :, columns] = value.reshape(shape)
                else:
                    ref[0, 0, part * half : (part + 1) * half, columns] = value

        def finished(matrix):
            if (layer, matrix) in k.blocks:
                start(SUM_X, (layer, matrix))
            else:
                k.local.start(k.w[matrix], k.made_out[matrix], True)

        k.at, k.early, k.weight, k.matrix, k.made = at_point, early, weight, matrix_of, finished
        k.put_product = put_product

        def keep(name):
            k.stores.append(k.local.start(k.kept[name], k.kept_out[k.layer][name]))

        def settle():
            while k.stores:
                k.stores.pop().wait()

        k.keep, k.settle = keep, settle
        at_point(0)
        body(k)
        for kind, key in sorted(running):
            end(kind, key)
        for transfer in running.values():
            transfer.close()
        k.local.close()

    hbm, near = pl.BlockSpec(memory_space=pl.ANY), pl.BlockSpec(memory_space=pltpu.VMEM)
    results = pl.pallas_call(
        kernel,
        out_shape=[jax.ShapeDtypeStruct(out.shape, out.kind) for out in outs_flat],
        in_specs=[hbm if isinstance(value, Far) else near for value in ins_flat],
        out_specs=[hbm if out.far else near for out in outs_flat],
        scratch_shapes=scratch_flat,
        compiler_params=pltpu.CompilerParams(
            collective_id=collective_id, has_side_effects=True, vmem_limit_bytes=VMEM_LIMIT
        ),
    )(*[value.array if isinstance(value, Far) else value for value in ins_flat])
    result = types.SimpleNamespace(**jax.tree.unflatten(outs_tree, results))
    store.z |= result.z_out
    store.x |= result.x_out
    store.sums |= result.sums_out
    store.totals |= result.totals
    store.made |= {(layer, m): value for m, value in result.made_out.items()}
    return result


def plain(body, outs, *arrays):
    near = pl.BlockSpec(memory_space=pltpu.VMEM)
    return pl.pallas_call(
        body,
        out_shape=[jax.ShapeDtypeStruct(out.shape, out.kind) for out in outs],
        in_specs=[near] * len(arrays),
        out_specs=[near] * len(outs),
        compiler_params=pltpu.CompilerParams(vmem_limit_bytes=VMEM_LIMIT),
    )(*arrays)


def turned_over(value):
    return jnp.transpose(value.astype(F32))


def pack_all(attention, projection, widening, narrowing, expansion, contraction, experts, shared_units):
    layers, _, height, wide = attention.shape
    units = widening.shape[3]
    keys, outs = [], []
    for layer in range(layers):
        shapes = {QKV: (height, 3 * wide), PRJ: (height, wide), SH: (2, height, 3 * shared_units)}
        shapes |= {EX + e: (2, height, 3 * units) for e in range(experts)}
        keys += [(layer, matrix) for matrix in shapes]
        outs += [Out(shape, BF16) for shape in shapes.values()]

    def body(att, prj, wid, nar, exp, con, *results):
        results = dict(zip(keys, results, strict=True))
        for layer in range(layers):
            for n in range(3):
                results[layer, QKV][:, n * wide : (n + 1) * wide] = att[layer, n]
            results[layer, PRJ][...] = turned_over(prj[layer]).astype(BF16)
            for half in range(2):
                cut = slice(half * shared_units, (half + 1) * shared_units)
                shared = results[layer, SH]
                shared[half, :, : 2 * shared_units] = jnp.concatenate([wid[layer, n, :, cut] for n in range(2)], axis=1)
                shared[half, :, 2 * shared_units :] = nar[layer, :, cut]
                for e in range(experts):
                    whole, given = results[layer, EX + e], half * experts + e
                    for n in range(2):
                        whole[half, :, n * units : (n + 1) * units] = exp[layer, given, n]
                    whole[half, :, 2 * units :] = con[layer, given]

    narrowing, contraction = jnp.swapaxes(narrowing, 1, 2), jnp.swapaxes(contraction, 2, 3)
    results = plain(body, outs, attention, projection, widening, narrowing, expansion, contraction)
    return dict(zip(keys, results, strict=True))


def unpack_all(current, upstream, small, totals, layers, all_experts, experts, shared_units, units, wide):
    width = current.shape[1]
    height = totals[0, QKV][0].shape[0]
    keys = sorted(totals)
    counts = [len(totals[key]) for key in keys]
    outs = [
        Out(current.shape),
        Out(upstream.shape),
        Out((layers, 2, width)),
        Out((layers, 3, height, wide)),
        Out((layers, wide, height)),
        Out((layers, all_experts, width)),
        Out((layers, 2, height, units)),
        Out((layers, height, units)),
        Out((layers, all_experts, 2, height, units)),
        Out((layers, all_experts, height, units)),
    ]

    def body(*refs):
        now, up, sums = refs[:3]
        parts, at = {}, 3
        for key, count in zip(keys, counts, strict=True):
            parts[key] = refs[at : at + count]
            at += count
        now_out, up_out, gains, att, prj, router, wid, nar, exp, con = refs[at:]
        upper = Place().half == 1
        now_out[...] = now[...]
        up_out[...] = up[...]

        def halves(key):
            mine, theirs = (part[...].astype(F32) for part in parts[key])
            return jnp.where(upper, theirs, mine), jnp.where(upper, mine, theirs)

        for layer in range(layers):
            gains[layer] = sums[2 * layer : 2 * layer + 2, :]
            router[layer] = sums[8 * layer + 8 : 8 * layer + 8 + all_experts, :]
            whole = parts[layer, QKV][0]
            for n in range(3):
                att[layer, n] = whole[:, n * wide : (n + 1) * wide].astype(F32)
            prj[layer] = turned_over(parts[layer, PRJ][0][...])
            for half, value in enumerate(halves((layer, SH))):
                cut = slice(half * shared_units, (half + 1) * shared_units)
                for n in range(2):
                    wid[layer, n, :, cut] = value[:, n * shared_units : (n + 1) * shared_units]
                nar[layer, :, cut] = value[:, 2 * shared_units :]
            for e in range(experts):
                for half, value in enumerate(halves((layer, EX + e))):
                    for n in range(2):
                        exp[layer, half * experts + e, n] = value[:, n * units : (n + 1) * units]
                    con[layer, half * experts + e] = value[:, 2 * units :]

    arrays = [current, upstream, small, *(part for key in keys for part in totals[key])]
    now, up, gains, att, prj, router, wid, nar, exp, con = plain(body, outs, *arrays)
    return now, up, gains, att, prj, jnp.swapaxes(router, 1, 2), wid, jnp.swapaxes(nar, 1, 2), exp, jnp.swapaxes(con, 2, 3)


def forward_plan(store, layers):
    def pass_on(point, *keys):
        return [step for key in keys for step in ((point, GET_Z, key, True), (point, GET_X, key))]

    def go(point, *keys):
        return [(point, GET_Z, key) for key in keys]

    plan = []
    for layer in range(layers):
        qkv, (prj,), sh = (store.keys(layer, matrix) for matrix in (QKV, PRJ, SH))
        low, high = store.keys(layer, EX), store.keys(layer, EX + 1)
        at = 20 * layer
        if layer == 0:
            plan += go(0, *qkv, prj, *low) + pass_on(1, *qkv) + pass_on(2, prj) + go(2, high[0])
            plan += pass_on(5, low[0]) + pass_on(7, low[1]) + pass_on(8, low[2]) + go(8, *high[1:], *sh)
            plan += pass_on(9, high[0]) + pass_on(11, high[1]) + pass_on(12, high[2])
            plan += pass_on(13, sh[0]) + pass_on(14, sh[1])
        else:
            plan += go(at - 12, *qkv, prj, *sh) + pass_on(at - 5, *qkv, prj) + pass_on(at - 4, *sh)
            plan += go(at - 4, *low, *high[:2]) + pass_on(at + 2, *low[:2]) + pass_on(at + 5, low[2])
            plan += go(at + 8, high[2]) + pass_on(at + 8, *high[:2]) + pass_on(at + 11, high[2])
    return plan


def backward_plan(layer, last):
    sh, low, high, prj, qkv = ((layer, matrix) for matrix in (SH, EX, EX + 1, PRJ, QKV))
    plan = [(7, SUM_X, sh, 2), (8, SUM_X, sh, 2), (18, SUM_X, low, 2), (10, SUM_X, low, 1), (11, SUM_X, low, 1)]
    own, onward = [sh, low, high], [sh, low]
    if layer < last:
        above = [(layer + 1, PRJ), (layer + 1, QKV)]
        plan += [(0, SUM_X, key) for key in above] + [(1, SUM_Z, (layer + 1, EX + 1))]
        plan += [(6, SUM_X, key, 4) for key in above]
        onward += above
    if layer == 0:
        plan += [(12, SUM_X, high, 1), (14, SUM_X, high, 1), (15, SUM_X, high, 2), (16, SUM_X, prj, 4)]
        plan += [(17, SUM_X, qkv, 4)]
        own, onward = [*own, prj, qkv], [*onward, high, prj, qkv]
    return plan, own, onward


def on_device(
    ring, stream, cotangent, segments, expert_pick, slot_index, norm_gains,
    attention, projection, router, widening, narrowing, expansion, contraction,
):
    layers = attention.shape[0]
    segment = segments[0]
    length = segment.shape[0]
    all_experts = expansion.shape[1]
    width = stream.shape[1]
    quarter = stream.shape[0]
    wide = attention.shape[3]
    units = widening.shape[3]
    height = attention.shape[2]
    paired = ring == 8
    sequences = 2 if paired else 1
    experts = all_experts // sequences
    shared_units = units // sequences
    inverse = np.exp(np.arange(HEAD // 2, dtype=np.float32) * np.float32(-2.0 * math.log(10000.0) / HEAD))
    phases = np.arange(length, dtype=np.float32)[:, None] * inverse[None, :]
    cosine, sine = np.cos(phases), np.sin(phases)
    places = dict(
        cosine=jnp.asarray(np.concatenate([cosine] * 4, axis=1)),
        sine=jnp.asarray(np.concatenate([-sine, sine] * 2, axis=1)),
        seg_row=segment[None, :],
    )
    picks = [jnp.swapaxes(jnp.concatenate([expert_pick, slot_index], axis=2), 1, 2).reshape(4 * layers, length)]
    router_rows = jnp.swapaxes(router, 1, 2)

    columns = {QKV: 3 * wide, PRJ: wide, SH: 3 * shared_units} | {EX + e: 3 * units for e in range(experts)}
    parts = {matrix: [(0, height)] for matrix in columns}
    if paired:
        third = height // 3
        parts[QKV] = parts[EX] = [(at, third) for at in (0, third, 2 * third)]
        parts[SH] = [(0, height // 2), (height // 2, height - height // 2)]
        parts[EX + 1] = [(0, height // 2), (height // 2, third), (height // 2 + third, height - height // 2 - third)]
    store = Store(height, width, columns, parts, paired)
    if paired:
        store.source = pack_all(
            attention, projection, widening, narrowing, expansion, contraction, experts, shared_units
        )
    else:
        whole = jnp.concatenate([expansion[:, :, 0], expansion[:, :, 1], jnp.swapaxes(contraction, 2, 3)], axis=-1)
        shared = jnp.concatenate([widening[:, 0], widening[:, 1], jnp.swapaxes(narrowing, 1, 2)], axis=-1)
        for layer in range(layers):
            store.source[layer, QKV] = jnp.concatenate([*attention[layer]], axis=-1)
            store.source[layer, PRJ] = projection[layer].T
            store.source[layer, SH] = shared[layer]
            for e in range(experts):
                store.source[layer, EX + e] = whole[layer, e]
    if not paired:
        store.full = {
            key: lax.all_gather(source, "dp", axis=0, tiled=True)[None, None] for key, source in store.source.items()
        }

    vmem = pltpu.VMEM
    token_scatter = scatter_scratch(length, width)
    pair_scratch = dict(scatters=[token_scatter] * sequences, own_gather=gather_scratch())
    if paired:
        pair_scratch |= dict(
            other_gather=gather_scratch(),
            pair_send=pltpu.SemaphoreType.DMA((2,)),
            pair_recv=pltpu.SemaphoreType.DMA((2,)),
            pair_sum=vmem((quarter, width), BF16),
            pair_land=vmem((quarter, width), BF16),
        )
    attention_shapes = {NRM: (length, width), TURNED: (length, 4 * wide)}
    ffn_shapes = {
        MOE: (sequences, length, width),
        SHARED: (sequences, length, 2 * shared_units),
        ROUTED: (experts, sequences * CAP, width),
        ACT: (experts, sequences * CAP, 2 * units),
    }
    ffn_matrices = [SH, *(EX + e for e in range(experts))]
    rows_out = Out((quarter, width))
    gain_out = Out((1, width))
    last = layers - 1

    def kept_scratch(shapes):
        return {name: vmem(shape, BF16) for name, shape in shapes.items()}

    def kept_outs(shapes):
        return {name: Out(shape, BF16, True) for name, shape in shapes.items()}

    tables = dict(
        slot_rows=vmem((sequences * experts, length), jnp.int32),
        chosen_rows=vmem((sequences, 8, length), F32),
        columns=vmem((length, LANES), jnp.int32),
        router_rows=vmem((LANES, width), BF16),
    )
    news = dict(
        news=vmem((4 * layers, length), jnp.int32),
        news_send=pltpu.SemaphoreType.DMA((1,)),
        news_recv=pltpu.SemaphoreType.DMA((1,)),
    )
    result = call(
        store,
        forward,
        0,
        dict(x=stream, gains=[*norm_gains], routers=[*router_rows], picks=picks, **places),
        dict(
            mid=[rows_out] * layers,
            following=[rows_out] * layers,
            gate_rows=[Out((sequences, 8, length))] * layers,
            kept_out=[kept_outs(attention_shapes | ffn_shapes)] * layers,
            **(dict(picks_out=Out((4 * layers, length), jnp.int32)) if paired else {}),
        ),
        dict(
            chosen_cols=vmem((sequences, length, LANES), F32),
            **tables,
            **(news if paired else {}),
            kept=kept_scratch(attention_shapes | ffn_shapes),
            branch=vmem((sequences, length, width), F32),
            outs=vmem((CAP, width), BF16),
            gates=vmem((sequences, length, LANES), F32),
            gather=gather_scratch(),
            scatter=token_scatter,
            **pair_scratch,
        ),
        range(layers),
        [QKV, PRJ, *ffn_matrices],
        plan=forward_plan(store, layers) if paired else (),
    )
    if paired:
        picks = [*picks, result.picks_out]
    current = result.following[last]
    saved = [
        ([stream, *result.following][layer], result.mid[layer], result.kept_out[layer], result.gate_rows[layer])
        for layer in range(layers)
    ]
    next_id = 1

    upstream = cotangent
    parts_small = [None] * layers
    for layer in reversed(range(layers)):
        x_in, mid, kept, gate_rows = saved[layer]
        finish = paired and layer == 0
        plan, store.own_sums, store.straight_on = backward_plan(layer, last) if paired else ((), (), ())
        ins = dict(
            upstream=Far(upstream),
            x=Far(x_in),
            mid=Far(mid),
            gains=norm_gains[layer],
            router=router_rows[layer],
            picks=picks,
            gate_rows=gate_rows,
            kept_in={name: Far(array) for name, array in kept.items()},
            **places,
        )
        outs = dict(grad=rows_out, gain_att=gain_out, gain_ffn=gain_out, router_grad=Out((8, width)))
        work = dict(
            **tables,
            kept={
                MOE: vmem((sequences, length, width), BF16),
                SHARED: vmem((sequences, length, 2 * shared_units), BF16),
                ROUTED: vmem((sequences * CAP, width), BF16),
                ACT: vmem((sequences * CAP, 2 * units), BF16),
            },
            hidden_all=vmem((sequences, length, shared_units), BF16),
            hidden=vmem((sequences * CAP, units), BF16),
            slot_grad=vmem((sequences * CAP, width), BF16),
            moe_grad=vmem((sequences, length, width), F32),
            slot_sums=vmem((sequences, 8, length), F32),
            logit_grad=vmem((sequences, 8, length), BF16),
            up=vmem((sequences, length, width), BF16),
            rows=vmem((quarter, width), F32),
            outs=vmem((CAP, width), BF16),
            **pair_scratch,
        )
        if not paired:
            work |= dict(spare=vmem((2, length, width), BF16))
        if finish:
            rows = 8 * (1 + layers)
            ins |= dict(later=list(parts_small[last]))
            outs |= dict(small_sum=Out((rows, width)))
            work |= dict(
                stage=vmem((4, rows, width), F32),
                land=vmem((3, rows, width), F32),
                rows_z=vmem((4, rows, width), F32),
                small_send=pltpu.SemaphoreType.DMA((6,)),
                small_recv=pltpu.SemaphoreType.DMA((6,)),
            )
        result = call(
            store,
            last_backward if finish else layer_backward,
            next_id,
            ins,
            outs,
            work,
            [layer],
            [QKV, PRJ, *ffn_matrices],
            [QKV, PRJ, *ffn_matrices],
            plan=plan if paired else (),
        )
        upstream = result.grad
        parts_small[layer] = (result.gain_att, result.gain_ffn, result.router_grad)
        next_id += 1

    if paired:
        return unpack_all(
            current, upstream, result.small_sum, store.totals, layers, all_experts, experts, shared_units, units, wide
        )
    gains_grad, router_grad = lax.psum(
        (
            jnp.stack([jnp.concatenate(part[:2], axis=0) for part in parts_small]),
            jnp.stack([part[2][:all_experts] for part in parts_small]),
        ),
        ("dp", "tensor"),
    )
    totals = {
        key: lax.psum_scatter(part[0, 0], "dp", scatter_dimension=0, tiled=True).astype(F32)
        for key, part in store.made.items()
    }
    att = jnp.stack([totals[layer, QKV] for layer in range(layers)])
    prj = jnp.stack([totals[layer, PRJ] for layer in range(layers)])
    shared = jnp.stack([totals[layer, SH] for layer in range(layers)])
    whole = jnp.stack([jnp.stack([totals[layer, EX + e] for e in range(experts)]) for layer in range(layers)])
    return (
        current,
        upstream,
        gains_grad,
        jnp.stack([att[..., n * wide : (n + 1) * wide] for n in range(3)], axis=1),
        jnp.swapaxes(prj, 1, 2),
        jnp.swapaxes(router_grad, 1, 2),
        jnp.stack([shared[..., n * units : (n + 1) * units] for n in range(2)], axis=1),
        jnp.swapaxes(shared[..., 2 * units :], 1, 2),
        jnp.stack([whole[..., n * units : (n + 1) * units] for n in range(2)], axis=2),
        jnp.swapaxes(whole[..., 2 * units :], 2, 3),
    )


def solution(mesh):
    placed = (
        P(("dp", "tensor"), None),
        P(("dp", "tensor"), None),
        P("dp", None),
        P(None, "dp", None),
        P(None, "dp", None),
        P(),
        P(None, None, "dp", "tensor"),
        P(None, "tensor", "dp"),
        P(),
        P(None, None, "dp", "tensor"),
        P(None, "tensor", "dp"),
        P(None, None, None, "dp", "tensor"),
        P(None, None, "tensor", "dp"),
    )
    return jax.shard_map(
        functools.partial(on_device, mesh.shape["dp"]),
        mesh=mesh,
        in_specs=placed,
        out_specs=(
            P(("dp", "tensor"), None),
            P(("dp", "tensor"), None),
            P(),
            P(None, None, "dp", "tensor"),
            P(None, "tensor", "dp"),
            P(),
            P(None, None, "dp", "tensor"),
            P(None, "tensor", "dp"),
            P(None, None, None, "dp", "tensor"),
            P(None, None, "tensor", "dp"),
        ),
        check_vma=False,
    )
```
